32 devices in a mesh: dp: 16 (over z, y, core), query: 2 (over x).
Axes of the slice: x: 2, y: 2, z: 4, core: 2. Of those that a mesh axis runs over, the one named last changes fastest.
Arguments:
- tokens: bfloat16 [32, 512, 1280], P(('dp', 'query')), may hold values from -6 to 6
- cell_lengths: int32 [32, 4], P(('dp', 'query')), may hold values from 1 to 256, 512 in all within a row
- out_cotangent: bfloat16 [32, 512, 1280], P(('dp', 'query')), may hold values from -6 to 6
- ln_gains: float32 [2, 1280], replicated, may hold values from 0.5 to 1.5
- ln_biases: float32 [2, 1280], replicated, may hold values from -1.2 to 1.2
- proj_biases: float32 [4, 1280], replicated, may hold values from -1.2 to 1.2
- ff_biases: float32 [2, 5120], replicated, may hold values from -3 to 3
- w_qkv: bfloat16 [1280, 3840], P('query'), may hold values from -0.15625 to 0.15625
- w_out: bfloat16 [1280, 1280], P('query'), may hold values from -0.3125 to 0.3125
- w_up: bfloat16 [1280, 5120], P('query'), may hold values from -0.15625 to 0.15625
- w_down: bfloat16 [5120, 1280], P('query'), may hold values from -0.078125 to 0.078125
- dec_cell: bfloat16 [1280, 5120], P('query'), may hold values from -0.125 to 0.125
- dec_gene: bfloat16 [1280, 5120], P('query'), may hold values from -0.125 to 0.125
- dec_out: bfloat16 [5120], replicated, may hold values from -0.3125 to 0.3125
- gene_table: bfloat16 [1024, 1280], P('query'), may hold values from -6 to 6
- query_ids: int32 [128, 16], P('dp', 'query'), may hold values from 0 to 1023
- labels: int32 [128, 16], P('dp', 'query'), may hold values 0 or 1
Outputs:
- encoded: float32 [32, 512, 1280], P(('dp', 'query'))
- grad_tokens: float32 [32, 512, 1280], P(('dp', 'query'))
- grad_ln_gains: float32 [2, 1280], P(None, ('dp', 'query'))
- grad_ln_biases: float32 [2, 1280], P(None, ('dp', 'query'))
- grad_proj_biases: float32 [4, 1280], P(None, ('dp', 'query'))
- grad_ff_biases: float32 [2, 5120], P(None, ('dp', 'query'))
- grad_w_qkv: float32 [1280, 3840], P(('dp', 'query'))
- grad_w_out: float32 [1280, 1280], P(('dp', 'query'))
- grad_w_up: float32 [1280, 5120], P(('dp', 'query'))
- grad_w_down: float32 [5120, 1280], P(('dp', 'query'))
- grad_dec_cell: float32 [1280, 5120], P(('dp', 'query'))
- grad_dec_gene: float32 [1280, 5120], P(('dp', 'query'))
- grad_dec_out: float32 [5120], P(('dp', 'query'))
- grad_gene_table: float32 [1024, 1280], P(('dp', 'query'))
The draws below stay inside these ranges and needn't reach their ends.
Inputs may be any that keep to these rules, and one draw needn't show every extreme that they name: `cell_lengths`: the 4 cells of a row fill its 512 positions.
All inputs are finite; a program needn't handle non-finite values. No bound on the sum of `labels` on one device may be relied on, other than what follows from the above.
Results may differ from the reference program's by a relative error of at most 0.02.
Values may be sent and summed in bfloat16 or wider, within the bound.
No kernel may reach another device: no remote copies, remote signals or barrier semaphores. Data moves between devices by JAX's collectives and lax.ppermute only.
A program may use at most 576 MiB of HBM per device.

```python
import math
import jax
import jax.numpy as jnp
import numpy as np
from jax import lax

D = 1280
HEADS = 20
HEAD_DIM = 64
FF = 5120
ROW_LEN = 512
CELLS_ROW = 4
GENES = 1024
ROWS = 32
CELLS = 128
QUERIES = 16


def plant(drawn, key, smallest, top_value):
    dims = drawn.shape
    place = [jax.random.randint(jax.random.fold_in(key, axis), (), 0, dims[axis]) for axis in range(len(dims))]
    drawn = drawn.at[tuple(place)].set(smallest)
    longest = dims.index(max(dims))
    place[longest] = (place[longest] + 1) % dims[longest]
    return drawn.at[tuple(place)].set(top_value)


def block_scale(stream_key, dims, cuts, low, top_value):
    factor_of, own = 1.0, jax.random.fold_in(stream_key, 6)
    for position, blocks in cuts:
        draws = jnp.exp(jax.random.uniform(jax.random.fold_in(own, position), (blocks,), jnp.float32, low / len(cuts), top_value / len(cuts)))
        factor_of = factor_of * jnp.repeat(draws, dims[position] // blocks).reshape([-1 if axis == position else 1 for axis in range(len(dims))])
    return factor_of


def length_profile(amount, total, most, lean):
    portions = [(1 << 20) // math.isqrt(rank ** lean) + 1 for rank in range(2, amount + 1)]
    surplus, counts = total - most - (amount - 1), [1] * (amount - 1)
    while surplus > 0:
        candidates = [i for i in range(amount - 1) if counts[i] < most]
        whole, budget = sum([portions[i] for i in candidates]), surplus
        for i in candidates:
            extra = min(most - counts[i], max(1, budget * portions[i] // whole), surplus)
            counts[i] = counts[i] + extra
            surplus = surplus - extra
    return np.array([most] + counts)


def uneven_parts(own_key, number_of, total, reach, slope):
    if number_of == 2:
        one = jax.random.randint(own_key, (), max(1, total - reach), min(reach, total - 1) + 1)
        return jnp.stack([one, total - one])
    sizes = jnp.asarray(length_profile(number_of, total, reach, slope), jnp.int32)
    pairs = (number_of - 1) // 2
    giver, taker = sizes[1:1 + 2 * pairs:2], sizes[2:2 + 2 * pairs:2]
    slack = jnp.minimum(giver - 1, reach - taker)
    shifted = jax.random.randint(jax.random.fold_in(own_key, 1), (pairs,), 0, 1 << 20) % (slack + 1)
    sizes = sizes.at[1:1 + 2 * pairs:2].set(giver - shifted).at[2:2 + 2 * pairs:2].set(taker + shifted)
    return sizes[jax.random.permutation(jax.random.fold_in(own_key, 2), number_of)]


def noise(own_key, shape, scale, bound, pieces=(), kind=jnp.bfloat16):
    factor_of = block_scale(own_key, shape, pieces, -0.22, 0.18) if pieces else 1.0
    result = jax.random.normal(own_key, shape, jnp.float32) * scale * factor_of
    return jnp.minimum(jnp.maximum(result, -bound), bound).astype(kind)


def setup_inputs(seed: int = 0) -> dict:
    arg_keys = jax.random.split(jax.random.key(seed), 18)
    return {
        "tokens": noise(arg_keys[0], (ROWS, ROW_LEN, D), 1.0, 6.0, ((0, 32),)),
        "cell_lengths": jax.vmap(lambda own: uneven_parts(own, CELLS_ROW, ROW_LEN, ROW_LEN // 2, 2))(jax.random.split(arg_keys[1], ROWS)).reshape((ROWS, CELLS_ROW)).astype(jnp.int32),
        "out_cotangent": noise(arg_keys[2], (ROWS, ROW_LEN, D), 1.0, 6.0, ((0, 32),)),
        "ln_gains": jnp.clip(1.0 + 0.1 * jax.random.normal(arg_keys[3], (2, D), jnp.float32), 0.5, 1.5),
        "ln_biases": noise(arg_keys[4], (2, D), 0.2, 1.2, (), jnp.float32),
        "proj_biases": noise(arg_keys[5], (4, D), 0.2, 1.2, (), jnp.float32),
        "ff_biases": noise(arg_keys[6], (2, FF), 0.5, 3.0, (), jnp.float32),
        "w_qkv": noise(arg_keys[7], (D, 3 * D), D ** -0.5, 0.15625, ((0, 2),)),
        "w_out": noise(arg_keys[8], (D, D), (D // 4) ** -0.5, 0.3125, ((0, 2),)),
        "w_up": noise(arg_keys[9], (D, FF), D ** -0.5, 0.15625, ((0, 2),)),
        "w_down": noise(arg_keys[10], (FF, D), FF ** -0.5, 0.078125, ((0, 2),)),
        "dec_cell": noise(arg_keys[11], (D, FF), (2 * D) ** -0.5, 0.125, ((0, 2),)),
        "dec_gene": noise(arg_keys[12], (D, FF), (2 * D) ** -0.5, 0.125, ((0, 2),)),
        "dec_out": noise(arg_keys[13], (FF,), (FF // 16) ** -0.5, 0.3125),
        "gene_table": noise(arg_keys[14], (GENES, D), 1.0, 6.0, ((0, 2),)),
        "query_ids": plant(jax.random.randint(arg_keys[15], (CELLS, QUERIES), 0, GENES), jax.random.fold_in(arg_keys[15], 1), 0, GENES - 1).astype(jnp.int32),
        "labels": plant((jax.random.randint(arg_keys[16], (CELLS, QUERIES), 0, 2) < 1).astype(jnp.int32), jax.random.fold_in(arg_keys[16], 1), 0, 1),
    }


EPSILON = 1e-05
HIGHEST = lax.Precision.HIGHEST

@jax.custom_vjp
def low(v):
    return lax.optimization_barrier(v.astype(jnp.bfloat16)).astype(jnp.float32)

@jax.custom_vjp
def low_back(v):
    return v

def low_keep(v):
    return (low(v), None)

def low_pass(kept, grad):
    return (grad,)

def back_keep(v):
    return (v, None)

def back_low(kept, grad):
    return (low(grad),)
low.defvjp(low_keep, low_pass)
low_back.defvjp(back_keep, back_low)

def layer_norm(values_in, scale_row, offset_row):
    center = values_in - lax.optimization_barrier(jnp.mean(values_in, axis=-1, keepdims=True))
    spread = lax.optimization_barrier(jnp.mean(center * center, axis=-1, keepdims=True))
    return center * lax.rsqrt(spread + EPSILON) * scale_row + offset_row

def cell_layout(lengths):
    cell_ends = jnp.cumsum(lengths, axis=-1, dtype=jnp.int32).astype(jnp.int32)
    starts = (cell_ends - lengths).astype(jnp.int32)
    places = jnp.arange(ROW_LEN, dtype=jnp.int32)
    segment = lax.optimization_barrier(jnp.sum((places[None, :, None] >= cell_ends[:, None, :]).astype(jnp.int32), axis=-1, dtype=jnp.int32)).astype(jnp.int32)
    return (starts, segment)

def attend(qkv_row, segment_row):
    scale_factor = 1.0 / math.sqrt(HEAD_DIM)
    queries = qkv_row[:, :D].reshape(ROW_LEN, HEADS, HEAD_DIM)
    keys_in = qkv_row[:, D:2 * D].reshape(ROW_LEN, HEADS, HEAD_DIM)
    values_in = qkv_row[:, 2 * D:].reshape(ROW_LEN, HEADS, HEAD_DIM)
    scores = low_back(jnp.einsum('qhd,khd->hqk', queries, keys_in, precision=HIGHEST) * scale_factor)
    same_cell = segment_row[:, None] == segment_row[None, :]
    scores = jnp.where(same_cell[None], scores, -1e+30)
    highest_score = lax.optimization_barrier(jnp.max(scores, axis=-1, keepdims=True))
    weights = jnp.exp(scores - highest_score)
    attention = weights / lax.optimization_barrier(jnp.sum(weights, axis=-1, keepdims=True))
    mixed = jnp.einsum('hqk,khd->qhd', low(attention), values_in, precision=HIGHEST)
    return mixed.reshape(ROW_LEN, D)

def encode(block, segment_block, params):
    norm_gains, norm_shifts, proj_bias, ff_bias, qkv_weight, out_weight, up_weight, down_weight = params
    normed = low(layer_norm(block, norm_gains[0], norm_shifts[0]))
    zeroes = jnp.zeros_like(proj_bias[0])
    qkv = jnp.einsum('gld,de->gle', normed, qkv_weight, precision=HIGHEST) + jnp.concatenate([proj_bias[0], zeroes, proj_bias[1]])
    qkv = low(low_back(qkv))
    mixed = low(low_back(jax.vmap(attend)(qkv, segment_block)))
    branch = low_back(jnp.einsum('gld,de->gle', mixed, out_weight, precision=HIGHEST) + proj_bias[2])
    middle = block + branch
    second = low(layer_norm(middle, norm_gains[1], norm_shifts[1]))
    hidden = low_back(jnp.einsum('gld,df->glf', second, up_weight, precision=HIGHEST) + ff_bias[0])
    active = low(jax.nn.gelu(hidden, approximate=False))
    branch_two = low_back(jnp.einsum('glf,fd->gld', active, down_weight, precision=HIGHEST) + proj_bias[3])
    return middle + branch_two

def reference(tokens, cell_lengths, out_cotangent, ln_gains, ln_biases, proj_biases, ff_biases, w_qkv, w_out, w_up, w_down, dec_cell, dec_gene, dec_out, gene_table, query_ids, labels):
    starts, segment = cell_layout(cell_lengths)
    places = jnp.arange(ROW_LEN, dtype=jnp.int32)
    picker = (places[None, None, :] == starts[:, :, None]).astype(jnp.float32)
    label_float = labels.astype(jnp.float32)
    group = math.gcd(ROWS, max(1, 4096 // ROW_LEN))
    cell_block = math.gcd(CELLS, 16)
    block_count = CELLS // cell_block

    def forward(inputs, norm_gains, norm_shifts, proj_bias, ff_bias, qkv_weight, out_weight, up_weight, down_weight, cell_weight, gene_weight, logit_weight, table):
        params = (norm_gains, norm_shifts, proj_bias, ff_bias, qkv_weight, out_weight, up_weight, down_weight)

        def encode_step(member):
            return encode(member[0], member[1], params)
        encoded = lax.map(jax.checkpoint(encode_step), (inputs.reshape(ROWS // group, group, ROW_LEN, D), segment.reshape(ROWS // group, group, ROW_LEN)))
        encoded = encoded.reshape(ROWS, ROW_LEN, D)
        heads = jnp.einsum('rcl,rld->rcd', picker, encoded, precision=HIGHEST).reshape(CELLS, D)
        heads = low(low_back(heads))
        cell_part = low_back(jnp.dot(heads, cell_weight, precision=HIGHEST))
        gene_rows = low_back(jnp.take(table, query_ids, axis=0))

        def decode(member):
            cell_rows, gene_block, label_rows = member
            before = low_back(cell_rows[:, None, :] + jnp.einsum('cqd,df->cqf', gene_block, gene_weight, precision=HIGHEST) + ff_bias[1])
            gated_dec = jax.nn.gelu(before, approximate=False)
            logits = jnp.einsum('cqf,f->cq', gated_dec, logit_weight, precision=HIGHEST)
            return jnp.sum(jnp.logaddexp(logits, 0.0) - label_rows * logits)
        losses = lax.map(jax.checkpoint(decode), (cell_part.reshape(block_count, cell_block, FF), gene_rows.reshape(block_count, cell_block, QUERIES, D), label_float.reshape(block_count, cell_block, QUERIES)))
        return (encoded, jnp.sum(losses))
    (encoded, total_loss), pullback = jax.vjp(forward, tokens.astype(jnp.float32), ln_gains, ln_biases, proj_biases, ff_biases, w_qkv.astype(jnp.float32), w_out.astype(jnp.float32), w_up.astype(jnp.float32), w_down.astype(jnp.float32), dec_cell.astype(jnp.float32), dec_gene.astype(jnp.float32), dec_out.astype(jnp.float32), gene_table.astype(jnp.float32))
    grads = pullback((out_cotangent.astype(jnp.float32), jnp.ones((), jnp.float32)))
    return (encoded, grads[0], grads[1], grads[2], grads[3], grads[4], grads[5], grads[6], grads[7], grads[8], grads[9], grads[10], grads[11], grads[12])
```

```python
import math

import jax
import jax.numpy as jnp
from jax import lax
from jax.experimental import pallas as pl
from jax.experimental.pallas import tpu as pltpu
from jax.sharding import PartitionSpec as P

D = 1280
HEADS = 20
HEAD_DIM = 64
FF = 5120
ROW_LEN = 512
CELLS_ROW = 4
GENES = 1024
EPSILON = 1e-05
HIGHEST = lax.Precision.HIGHEST
F32 = jnp.float32
BF16 = jnp.bfloat16


def layer_norm(values_in, scale_row, offset_row):
    center = values_in - jnp.mean(values_in, axis=-1, keepdims=True)
    spread = jnp.mean(center * center, axis=-1, keepdims=True)
    return center * lax.rsqrt(spread + EPSILON) * scale_row + offset_row


def smooth_gate(values_in):
    return jax.nn.gelu(values_in, approximate=False)


def dot(left, right):
    return jnp.dot(left, right, preferred_element_type=F32)


def dot_rt(left, right):
    return lax.dot_general(left, right, (((1,), (1,)), ((), ())), preferred_element_type=F32)


def dot_lt(left, right):
    return lax.dot_general(left, right, (((0,), (0,)), ((), ())), preferred_element_type=F32)


def cell_layout(lengths):
    cell_ends = jnp.cumsum(lengths, axis=-1, dtype=jnp.int32)
    starts = cell_ends - lengths
    places = jnp.arange(ROW_LEN, dtype=jnp.int32)
    segment = jnp.sum(
        (places[None, :, None] >= cell_ends[:, None, :]).astype(jnp.int32), axis=-1, dtype=jnp.int32
    )
    return (starts, segment)


def split_heads(qkv_row):
    queries = qkv_row[:, :D].reshape(ROW_LEN, HEADS, HEAD_DIM)
    keys_in = qkv_row[:, D : 2 * D].reshape(ROW_LEN, HEADS, HEAD_DIM)
    values_in = qkv_row[:, 2 * D :].reshape(ROW_LEN, HEADS, HEAD_DIM)
    return (queries, keys_in, values_in)


def row_scores(queries, keys_in, segment_row):
    scores = jnp.einsum("qhd,khd->hqk", queries, keys_in, preferred_element_type=F32) * (
        1.0 / math.sqrt(HEAD_DIM)
    )
    same_cell = segment_row[:, None] == segment_row[None, :]
    return jnp.where(same_cell[None], scores, -1e30)


def attend(member):
    qkv_row, segment_row = member
    queries, keys_in, values_in = split_heads(qkv_row)
    scores = row_scores(queries, keys_in, segment_row)
    highest_score = jnp.max(scores, axis=-1, keepdims=True)
    weights = jnp.exp(scores - highest_score)
    weight_sum = jnp.sum(weights, axis=-1, keepdims=True)
    attention = (weights / weight_sum).astype(BF16)
    mixed = jnp.einsum("hqk,khd->qhd", attention, values_in, preferred_element_type=F32).astype(BF16)
    return (mixed.reshape(ROW_LEN, D), (highest_score + jnp.log(weight_sum))[:, :, 0])


def attend_back(member):
    qkv_row, segment_row, log_total, grad_mixed = member
    queries, keys_in, values_in = split_heads(qkv_row)
    scores = row_scores(queries, keys_in, segment_row)
    attention = jnp.exp(scores - log_total[:, :, None])
    grad_heads = grad_mixed.reshape(ROW_LEN, HEADS, HEAD_DIM)
    grad_probs = jnp.einsum("qhd,khd->hqk", grad_heads, values_in, preferred_element_type=F32)
    grad_scores = (
        attention * (grad_probs - jnp.sum(attention * grad_probs, axis=-1, keepdims=True))
    ).astype(BF16)
    scale_factor = 1.0 / math.sqrt(HEAD_DIM)
    grad_query = (
        jnp.einsum("hqk,khd->qhd", grad_scores, keys_in, preferred_element_type=F32) * scale_factor
    )
    grad_keys = (
        jnp.einsum("hqk,qhd->khd", grad_scores, queries, preferred_element_type=F32) * scale_factor
    )
    grad_values = jnp.einsum(
        "hqk,qhd->khd", attention.astype(BF16), grad_heads, preferred_element_type=F32
    )
    return jnp.concatenate(
        [
            grad_query.reshape(ROW_LEN, D),
            grad_keys.reshape(ROW_LEN, D),
            grad_values.reshape(ROW_LEN, D),
        ],
        axis=1,
    )


def assemble_kernel(pieces, width, count, place_ref, *refs):
    sources, full, sems = refs[:count], refs[count], refs[count + 1]
    step = pl.program_id(0)
    copies = []
    for i, (source, row, rows, column) in enumerate(pieces):
        start = pl.multiple_of(place_ref[i], 16)
        columns = pl.ds(pl.multiple_of(column + step * width, 128), width)
        copies.append(
            pltpu.make_async_copy(
                sources[source].at[pl.ds(row, rows), columns],
                full.at[pl.ds(start, rows), :],
                sems.at[i],
            )
        )
    for copy in copies:
        copy.start()
    for copy in copies:
        copy.wait()


def assemble(sources, pieces, places, shape, width):
    count = len(sources)
    rows, columns = shape
    return pl.pallas_call(
        lambda *refs: assemble_kernel(pieces, width, count, *refs),
        grid=(columns // width,),
        out_shape=jax.ShapeDtypeStruct(shape, BF16),
        in_specs=[pl.BlockSpec(memory_space=pltpu.SMEM)]
        + [pl.BlockSpec(memory_space=pl.ANY)] * count,
        out_specs=pl.BlockSpec((rows, width), lambda j: (0, j)),
        scratch_shapes=[pltpu.SemaphoreType.DMA((len(pieces),))],
        compiler_params=pltpu.CompilerParams(vmem_limit_bytes=32 << 20),
        cost_estimate=pl.CostEstimate(flops=0, bytes_accessed=4 * rows * columns, transcendentals=0),
    )(jnp.stack(places).astype(jnp.int32), *sources)


def tie(value, *others):
    return lax.optimization_barrier((value, *others))[0]


class Grid:
    def __init__(self, mesh):
        dp, query = mesh.shape["dp"], mesh.shape["query"]
        core = 2 if dp % 2 == 0 else 1
        rest = dp // core
        outer = 4 if rest % 4 == 0 else rest
        inner = rest // outer
        self.dp, self.query = dp, query
        self.size = {"z": outer, "y": inner, "c": core, "x": query}
        self.stride = {"z": inner * core, "y": core, "c": 1}
        self.order = ["z", "y", "c", "x"]

    def place(self, axis):
        if axis == "x":
            return lax.axis_index("query")
        return (lax.axis_index("dp") // self.stride[axis]) % self.size[axis]

    def partner(self, axis, at, step):
        size = self.size[axis]
        return at ^ step if size & (size - 1) == 0 else (at + step) % size

    def sender(self, axis, at, step):
        size = self.size[axis]
        return at ^ step if size & (size - 1) == 0 else (at + size - step) % size

    def hop(self, value, axis, step=1):
        if axis == "x":
            pairs = [(i, self.partner("x", i, step)) for i in range(self.query)]
            return lax.ppermute(value, "query", pairs)
        stride, size = self.stride[axis], self.size[axis]
        pairs = []
        for i in range(self.dp):
            at = (i // stride) % size
            pairs.append((i, i + (self.partner(axis, at, step) - at) * stride))
        return lax.ppermute(value, "dp", pairs)

    def share(self, value, axis=0):
        if self.query == 1:
            return value
        if self.query != 2:
            return lax.all_gather(value, "query", axis=axis, tiled=True)
        other = self.hop(value, "x")
        first = lax.axis_index("query") == 0
        return jnp.concatenate(
            [jnp.where(first, value, other), jnp.where(first, other, value)], axis=axis
        )

    def total(self, value):
        if self.query == 1:
            return value
        if self.query != 2:
            return lax.psum(value, "query")
        return value + self.hop(value, "x")

    def scatter_step(self, value, axis, dim, kind):
        size = self.size[axis]
        me = self.place(axis)

        def part(index):
            return lax.dynamic_index_in_dim(value, index, axis=dim, keepdims=False)

        if size == 1:
            return part(0)
        sent = [
            self.hop(part(self.partner(axis, me, step)), axis, step) for step in range(1, size)
        ]
        total = part(me).astype(F32)
        for received in sent:
            total = total + received.astype(F32)
        return total.astype(kind)

    def scatter(self, value, order, kind=BF16):
        dims = [axis for axis in self.order if axis in order]
        for axis in order:
            dim = dims.index(axis)
            value = self.scatter_step(value, axis, dim, kind)
            dims.pop(dim)
        return value

    def scatter_z(self, value):
        stride, size = self.stride["z"], self.size["z"]
        groups = [[k * stride + i for k in range(size)] for i in range(stride)]
        return lax.psum_scatter(
            value, "dp", scatter_dimension=0, axis_index_groups=groups, tiled=True
        )

    def blocks(self, value):
        shape = [self.size[axis] for axis in self.order]
        rows = value.shape[0] // math.prod(shape)
        return value.reshape(*shape, rows, *value.shape[1:])

    def own_columns(self, value):
        width = value.shape[1] // (self.dp * self.query)
        shaped = value.reshape(value.shape[0], self.dp, self.query, width)
        mine = lax.dynamic_index_in_dim(shaped, self.place("x"), axis=2, keepdims=False)
        return mine.reshape(value.shape[0], self.dp * width)

    def gather_rows(self, shards):
        size = self.size
        if self.query != 2 or size["y"] != 2 or size["c"] != 2 or size["z"] % 2:
            return [lax.all_gather(shard, "query", axis=0, tiled=True) for shard in shards]
        zb, y, c, x = self.place("z") % 2, self.place("y"), self.place("c"), self.place("x")
        unit = min(shard.shape[0] for shard in shards) // 8

        def at(zb_, y_, c_):
            return (zb_ * 2 + y_) * 2 + c_

        mine = at(zb, y, c)
        columns = []
        for shard in shards:
            fold = shard.shape[0] // (8 * unit)
            for k in range(fold):
                columns.append(
                    lax.dynamic_slice_in_dim(shard, (mine * fold + k) * unit, unit, 0)
                )
        sent = jnp.concatenate(columns, axis=1) if len(columns) > 1 else columns[0]
        first = self.hop(sent, "x")
        by_y = self.hop(first, "y")
        by_z = self.hop(first, "z")
        cut = unit // 2 // 16 * 16
        corner_y = self.hop(by_z[:cut], "y")
        corner_z = self.hop(by_y[cut:], "z")
        near = jnp.concatenate([first, by_y, by_z, corner_y, corner_z], axis=0)
        far = self.hop(near, "c")
        wholes = []
        column = 0
        for shard in shards:
            rows, width = shard.shape
            fold = rows // (8 * unit)
            pieces, places = [(0, 0, rows, 0)], [x * rows]
            for source, c_ in ((1, c), (2, 1 - c)):
                for part, (zb_, y_) in enumerate(((zb, y), (zb, 1 - y), (1 - zb, y), (1 - zb, 1 - y))):
                    for k in range(fold):
                        pieces.append((source, part * unit, unit, column + k * width))
                        places.append((1 - x) * rows + (at(zb_, y_, c_) * fold + k) * unit)
            block = 640 if rows <= 640 else 256
            wholes.append(assemble([shard, near, far], pieces, places, (2 * rows, width), block))
            column += fold * width
        return wholes


def make_shards(grid):
    def weight_term(left, right):
        half = right.shape[1] // 2
        sums = []
        for part, order in ((right[:, :half], "cxy"), (right[:, half:], "cyx")):
            terms = grid.blocks(dot_lt(left, part).astype(BF16))
            dims = ["z", "y", "c", "x"]
            for axis in order:
                dim = dims.index(axis)
                terms = grid.scatter_step(terms, axis, dim, BF16)
                dims.pop(dim)
            sums.append(terms)
        whole = jnp.concatenate(sums, axis=-1)
        return grid.scatter_z(whole).reshape(whole.shape[1:]).astype(F32)

    def shards(
        tokens,
        cell_lengths,
        out_cotangent,
        ln_gains,
        ln_biases,
        proj_biases,
        ff_biases,
        w_qkv,
        w_out,
        w_up,
        w_down,
        dec_cell,
        dec_gene,
        dec_out,
        gene_table,
        query_ids,
        labels,
    ):
        row_count = tokens.shape[0]
        token_count = row_count * ROW_LEN
        dp_count, query_count = grid.dp, grid.query
        place = lax.axis_index("query")
        starts, segment = cell_layout(cell_lengths)
        local_cells = row_count * CELLS_ROW
        pair_cells, local_queries = query_ids.shape
        pairs = pair_cells * local_queries
        half_width = D // query_count

        full_qkv, full_out = grid.gather_rows([w_qkv, w_out])
        full_up, full_down = grid.gather_rows([w_up, w_down])

        ids = grid.share(query_ids.reshape(1, pairs)).reshape(query_count * pairs)
        table_rows = gene_table.shape[0]
        local_ids = ids - place * table_rows
        held = (local_ids[:, None] == jnp.arange(table_rows, dtype=jnp.int32)[None, :]).astype(BF16)
        gene_rows = grid.total(dot(held, gene_table).astype(BF16))
        gene_half = lax.dynamic_slice_in_dim(gene_rows, place * half_width, half_width, 1)
        gene_partial = dot(gene_half, dec_gene).reshape(query_count, pairs, FF)
        gene_part = grid.scatter_step(gene_partial.astype(BF16), "x", 0, F32) + ff_biases[1]

        flat_tokens = tokens.astype(F32).reshape(token_count, D)
        normed, first_pull = jax.vjp(layer_norm, flat_tokens, ln_gains[0], ln_biases[0])
        normed_low = normed.astype(BF16)
        zeroes = jnp.zeros((D,), F32)
        qkv_bias = jnp.concatenate([proj_biases[0], zeroes, proj_biases[1]])
        qkv_low = (dot(normed_low, full_qkv) + qkv_bias).astype(BF16)
        qkv_rows = qkv_low.reshape(row_count, ROW_LEN, 3 * D)
        mixed_rows, log_totals = lax.map(attend, (qkv_rows, segment))
        mixed_low = mixed_rows.reshape(token_count, D)
        middle = flat_tokens + dot(mixed_low, full_out) + proj_biases[2]
        second, second_pull = jax.vjp(layer_norm, middle, ln_gains[1], ln_biases[1])
        second_low = second.astype(BF16)
        hidden = dot(second_low, full_up) + ff_biases[0]
        active, active_pull = jax.vjp(smooth_gate, hidden)
        active_low = active.astype(BF16)
        encoded = middle + dot(active_low, full_down) + proj_biases[3]
        encoded_rows = encoded.reshape(row_count, ROW_LEN, D)
        heads_low = (
            jnp.take_along_axis(encoded_rows, starts[:, :, None], axis=1)
            .reshape(local_cells, D)
            .astype(BF16)
        )
        cell_heads = grid.share(heads_low)
        heads_half = lax.dynamic_slice_in_dim(cell_heads, place * half_width, half_width, 1)
        cell_part = grid.total(dot(heads_half, dec_cell))
        before = cell_part[:, None, :] + gene_part.reshape(pair_cells, local_queries, FF)
        gated_dec, gated_pull = jax.vjp(smooth_gate, before)
        logit_weight = dec_out.astype(F32)
        logits = jnp.sum(gated_dec * logit_weight, axis=-1)
        logit_slope = jax.nn.sigmoid(logits) - labels.astype(F32)
        (grad_before,) = gated_pull(logit_slope[:, :, None] * logit_weight)
        before_low = grad_before.astype(BF16)
        before_sums = jnp.sum(before_low, axis=1, dtype=F32)
        grad_dec_bias = jnp.sum(before_sums, axis=0)
        grad_logit = jnp.sum(gated_dec * logit_slope[:, :, None], axis=(0, 1))
        cell_total = grid.total(before_sums).astype(BF16)
        heads_part = dot_rt(cell_total, dec_cell).astype(BF16)
        heads_all = grid.share(heads_part, axis=1)
        heads_back = lax.dynamic_slice_in_dim(
            heads_all, place * local_cells, local_cells, 0
        ).astype(F32)

        places = jnp.arange(ROW_LEN, dtype=jnp.int32)
        picker = (places[None, :, None] == starts[:, None, :]).astype(F32)
        grad_encoded = out_cotangent.astype(F32) + jnp.sum(
            picker[:, :, :, None] * heads_back.reshape(row_count, 1, CELLS_ROW, D), axis=2
        )
        grad_flat = grad_encoded.reshape(token_count, D)

        branch_low = grad_flat.astype(BF16)
        grad_down = weight_term(active_low, branch_low)
        grad_out_bias = jnp.sum(branch_low, axis=0, dtype=F32)
        grad_active = dot_rt(branch_low, full_down)
        (grad_hidden,) = active_pull(grad_active)
        hidden_low = grad_hidden.astype(BF16)
        grad_up = weight_term(second_low, hidden_low)
        grad_up_bias = jnp.sum(hidden_low, axis=0, dtype=F32)
        grad_second = dot_rt(hidden_low, full_up)
        middle_part, grad_gain_two, grad_shift_two = second_pull(grad_second)
        grad_middle = grad_flat + middle_part

        before_all = grid.share(before_low.reshape(1, pairs, FF)).reshape(query_count * pairs, FF)
        gene_terms = dot_lt(grid.own_columns(gene_rows), before_all).astype(BF16)
        shape = [grid.size[axis] for axis in "zyc"]
        grad_gene = grid.scatter(gene_terms.reshape(*shape, -1, FF), "cyz").astype(F32)
        genes_part = dot_rt(before_all, dec_gene).astype(BF16)
        genes_back = grid.share(genes_part, axis=1)
        choose = (ids[:, None] == jnp.arange(GENES, dtype=jnp.int32)[None, :]).astype(BF16)
        table_terms = dot_lt(grid.own_columns(choose), genes_back).astype(BF16)
        grad_table = grid.scatter(table_terms.reshape(*shape, -1, D), "cyz").astype(F32)
        all_heads = lax.all_gather(cell_heads, "dp", axis=0, tiled=True)
        all_cells = lax.all_gather(cell_total, "dp", axis=0, tiled=True)
        owned = D // (dp_count * query_count)
        mine = lax.axis_index("dp") * query_count + place
        grad_cell = dot_lt(
            lax.dynamic_slice_in_dim(all_heads, mine * owned, owned, 1), all_cells
        )

        attn_low = grad_middle.astype(BF16)
        grad_attn_bias = jnp.sum(attn_low, axis=0, dtype=F32)
        grad_out = weight_term(mixed_low, attn_low)
        mixed_back = dot_rt(attn_low, full_out).astype(BF16)
        qkv_back = lax.map(
            attend_back, (qkv_rows, segment, log_totals, mixed_back.reshape(row_count, ROW_LEN, D))
        )
        qkv_back_low = qkv_back.reshape(token_count, 3 * D).astype(BF16)
        grad_qkv = weight_term(normed_low, qkv_back_low)
        bias_sums = jnp.sum(qkv_back_low, axis=0, dtype=F32)
        grad_normed = dot_rt(qkv_back_low, full_qkv)
        token_part, grad_gain_one, grad_shift_one = first_pull(grad_normed)
        grad_tokens = (grad_middle + token_part).reshape(row_count, ROW_LEN, D)

        owners = dp_count * query_count

        def owned_cols(values):
            return values.reshape(-1, owners, values.shape[-1] // owners).transpose(1, 0, 2).reshape(owners, -1)

        small = [
            jnp.stack([grad_gain_one, grad_gain_two]),
            jnp.stack([grad_shift_one, grad_shift_two]),
            jnp.stack([bias_sums[:D], bias_sums[2 * D :], grad_attn_bias, grad_out_bias]),
            jnp.stack([grad_up_bias, grad_dec_bias]),
            grad_logit[None, :],
        ]
        flat = [owned_cols(v) for v in small]
        joined = jnp.concatenate(flat, axis=1)
        summed = grid.scatter(grid.blocks(joined), "cxyz", F32).reshape(-1)
        outs = []
        start = 0
        for value, piece in zip(small, flat):
            size = piece.shape[1]
            outs.append(summed[start : start + size].reshape(value.shape[0], -1))
            start += size

        return (
            encoded_rows,
            grad_tokens,
            outs[0],
            outs[1],
            outs[2],
            outs[3],
            grad_qkv,
            grad_out,
            grad_up,
            grad_down,
            grad_cell,
            grad_gene,
            outs[4][0],
            grad_table,
        )

    return shards


def solution(mesh):
    placed = (
        P(("dp", "query"), None, None),
        P(("dp", "query"), None),
        P(("dp", "query"), None, None),
        P(),
        P(),
        P(),
        P(),
        P("query", None),
        P("query", None),
        P("query", None),
        P("query", None),
        P("query", None),
        P("query", None),
        P(),
        P("query", None),
        P("dp", "query"),
        P("dp", "query"),
    )
    rows = P(("dp", "query"), None)
    return jax.shard_map(
        make_shards(Grid(mesh)),
        mesh=mesh,
        in_specs=placed,
        out_specs=(
            P(("dp", "query"), None, None),
            P(("dp", "query"), None, None),
            P(None, ("dp", "query")),
            P(None, ("dp", "query")),
            P(None, ("dp", "query")),
            P(None, ("dp", "query")),
            rows,
            rows,
            rows,
            rows,
            rows,
            rows,
            P(("dp", "query")),
            rows,
        ),
        check_vma=False,
    )
```

```python
import math

import jax
import jax.numpy as jnp
from jax import lax
from jax.experimental import pallas as pl
from jax.experimental.pallas import tpu as pltpu
from jax.sharding import PartitionSpec as P

D = 1280
HEADS = 20
HEAD_DIM = 64
FF = 5120
ROW_LEN = 512
CELLS_ROW = 4
GENES = 1024
EPSILON = 1e-05
HIGHEST = lax.Precision.HIGHEST
F32 = jnp.float32
BF16 = jnp.bfloat16
VMEM_ASKED = 56 << 20


def layer_norm(values_in, scale_row, offset_row):
    center = values_in - jnp.mean(values_in, axis=-1, keepdims=True)
    spread = jnp.mean(center * center, axis=-1, keepdims=True)
    return center * lax.rsqrt(spread + EPSILON) * scale_row + offset_row


def smooth_gate(values_in):
    return jax.nn.gelu(values_in, approximate=False)


def dot(left, right):
    return jnp.dot(left, right, preferred_element_type=F32)


def dot_rt(left, right):
    return lax.dot_general(left, right, (((1,), (1,)), ((), ())), preferred_element_type=F32)


def dot_lt(left, right):
    return lax.dot_general(left, right, (((0,), (0,)), ((), ())), preferred_element_type=F32)


def cell_layout(lengths):
    cell_ends = jnp.cumsum(lengths, axis=-1, dtype=jnp.int32)
    starts = cell_ends - lengths
    places = jnp.arange(ROW_LEN, dtype=jnp.int32)
    segment = jnp.sum(
        (places[None, :, None] >= cell_ends[:, None, :]).astype(jnp.int32), axis=-1, dtype=jnp.int32
    )
    return (starts, segment)


def cell_mask(segment_row, segment_column, mask):
    same = segment_column[...] == segment_row[...]
    mask[...] = jnp.where(same, 0.0, -1e30)


def attend_kernel(segment_row, segment_column, query, key, value, mixed, totals, mask):
    @pl.when(pl.program_id(1) == 0)
    def _():
        cell_mask(segment_row.at[0], segment_column.at[0], mask)

    ones = jnp.ones((8, ROW_LEN), BF16)
    value_t = value[0].T
    parts = []
    for head in range(2):
        columns = slice(head * HEAD_DIM, (head + 1) * HEAD_DIM)
        scaled = query[0, :, columns] * jnp.asarray(1.0 / math.sqrt(HEAD_DIM), BF16)
        scores = dot_rt(key[0, :, columns], scaled) + mask[...]
        top = jnp.max(scores, axis=0, keepdims=True)
        weights = jnp.exp(scores - top).astype(BF16)
        left = jnp.concatenate([value_t[columns], ones], axis=0)
        product = dot(left, weights)
        total = product[HEAD_DIM : HEAD_DIM + 1]
        parts.append(product[:HEAD_DIM] / total)
        totals[0, 0, head : head + 1] = top + jnp.log(total)
    mixed[0] = jnp.concatenate(parts, axis=0).T.astype(BF16)


def attend(qkv, segment, begin, pairs):
    rows = qkv.shape[0]
    every = HEADS // 2
    wide = 2 * HEAD_DIM

    def part(offset):
        return pl.BlockSpec((1, ROW_LEN, wide), lambda r, i: (r, 0, offset + i))

    return pl.pallas_call(
        attend_kernel,
        grid=(rows, pairs),
        in_specs=[
            pl.BlockSpec((1, 1, ROW_LEN), lambda r, i: (r, 0, 0)),
            pl.BlockSpec((1, ROW_LEN, 1), lambda r, i: (r, 0, 0)),
            part(begin),
            part(every + begin),
            part(2 * every + begin),
        ],
        out_specs=[
            pl.BlockSpec((1, ROW_LEN, wide), lambda r, i: (r, 0, i)),
            pl.BlockSpec((1, 1, 2, ROW_LEN), lambda r, i: (r, i, 0, 0)),
        ],
        out_shape=[
            jax.ShapeDtypeStruct((rows, ROW_LEN, pairs * wide), BF16),
            jax.ShapeDtypeStruct((rows, pairs, 2, ROW_LEN), F32),
        ],
        scratch_shapes=[pltpu.VMEM((ROW_LEN, ROW_LEN), F32)],
        compiler_params=pltpu.CompilerParams(vmem_limit_bytes=VMEM_ASKED),
        cost_estimate=pl.CostEstimate(flops=1, bytes_accessed=1, transcendentals=0),
    )(segment[:, None, :], segment[:, :, None], qkv, qkv, qkv)


def attend_back_kernel(
    segment_row, segment_column, query, key, value, mixed, back, totals, d_query, d_key, d_value, mask
):
    @pl.when(pl.program_id(1) == 0)
    def _():
        cell_mask(segment_row.at[0], segment_column.at[0], mask)

    scale = jnp.asarray(1.0 / math.sqrt(HEAD_DIM), BF16)
    key_t = key[0].T
    product_t = (back[0].astype(F32) * mixed[0].astype(F32)).T
    queries, keys, values = [], [], []
    for head in range(2):
        columns = slice(head * HEAD_DIM, (head + 1) * HEAD_DIM)
        scaled = query[0, :, columns] * scale
        grad = back[0, :, columns]
        scores = dot_rt(key[0, :, columns], scaled) + mask[...]
        weights = jnp.exp(scores - totals[0, 0, head : head + 1])
        d_weights = dot_rt(value[0, :, columns], grad)
        shift = jnp.sum(product_t[columns], axis=0, keepdims=True)
        d_scores = (weights * (d_weights - shift)).astype(BF16)
        values.append(dot(weights.astype(BF16), grad))
        keys.append(dot(d_scores, scaled))
        queries.append(dot(key_t[columns], d_scores))
    d_query[0] = (jnp.concatenate(queries, axis=0).T * (1.0 / math.sqrt(HEAD_DIM))).astype(BF16)
    d_key[0] = jnp.concatenate(keys, axis=1).astype(BF16)
    d_value[0] = jnp.concatenate(values, axis=1).astype(BF16)


def attend_back(qkv, segment, mixed, back, totals):
    rows = qkv.shape[0]
    pairs = HEADS // 2
    wide = 2 * HEAD_DIM

    def part(offset):
        return pl.BlockSpec((1, ROW_LEN, wide), lambda r, i: (r, 0, offset + i))

    return pl.pallas_call(
        attend_back_kernel,
        grid=(rows, pairs),
        in_specs=[
            pl.BlockSpec((1, 1, ROW_LEN), lambda r, i: (r, 0, 0)),
            pl.BlockSpec((1, ROW_LEN, 1), lambda r, i: (r, 0, 0)),
            part(0),
            part(pairs),
            part(2 * pairs),
            part(0),
            part(0),
            pl.BlockSpec((1, 1, 2, ROW_LEN), lambda r, i: (r, i, 0, 0)),
        ],
        out_specs=[part(0)] * 3,
        out_shape=[jax.ShapeDtypeStruct((rows, ROW_LEN, D), BF16)] * 3,
        scratch_shapes=[pltpu.VMEM((ROW_LEN, ROW_LEN), F32)],
        compiler_params=pltpu.CompilerParams(vmem_limit_bytes=VMEM_ASKED),
        cost_estimate=pl.CostEstimate(flops=1, bytes_accessed=1, transcendentals=0),
    )(segment[:, None, :], segment[:, :, None], qkv, qkv, qkv, mixed, back, totals)


CHUNK = 640


def part_copies(sources, columns, place, buffer, sems, half_rows, act):
    shard, *parts = sources
    query, outer, inner, core = (place[i] for i in range(4))
    unit = parts[1].shape[0]
    act(
        pltpu.make_async_copy(
            shard.at[:, columns],
            buffer.at[pl.ds(pl.multiple_of(query * half_rows, 16), half_rows), :],
            sems.at[0],
        )
    )
    for side in range(2):
        c = core if side == 0 else 1 - core
        for part in range(4):
            zb, y = outer ^ (part // 2), inner ^ (part % 2)
            row = (1 - query) * half_rows + ((zb * 2 + y) * 2 + c) * unit
            source = parts[2 * side + part // 3]
            act(
                pltpu.make_async_copy(
                    source.at[pl.ds(part % 3 * unit, unit), columns],
                    buffer.at[pl.ds(pl.multiple_of(row, 16), unit), :],
                    sems.at[1 + side * 4 + part],
                )
            )


def chunk_place(step, place, half):
    steps = half // CHUNK
    own = step < steps
    return jnp.where(own, place[0] * steps + step, (1 - place[0]) * steps + step - steps)


def up_copies(sources, place, step, buffer, sems, act):
    half = FF // 2
    start = pl.multiple_of(chunk_place(step, place, half) * CHUNK, 128)
    columns = pl.ds(start, CHUNK)
    part_copies(sources, columns, place, buffer, sems, sources[0].shape[0], act)


def down_copies(sources, place, step, buffer, sems, act):
    shard, *parts = sources
    query, outer, inner, core = (place[i] for i in range(4))
    unit = parts[1].shape[0]
    fold = shard.shape[0] // (8 * unit)
    steps = shard.shape[0] // CHUNK
    own = step < steps
    local = jnp.where(own, step, step - steps)
    part = ((local // 2) ^ outer) * 2 + ((local % 2) ^ inner)

    @pl.when(own)
    def _():
        act(
            pltpu.make_async_copy(
                shard.at[pl.ds(pl.multiple_of(local * CHUNK, 16), CHUNK), :], buffer, sems.at[0]
            )
        )

    def remote(corner):
        for side in range(2):
            c = core if side == 0 else 1 - core
            row = 0 if corner else pl.multiple_of(part * unit, 16)
            for k in range(fold):
                act(
                    pltpu.make_async_copy(
                        parts[2 * side + corner].at[pl.ds(row, unit), pl.ds(k * D, D)],
                        buffer.at[pl.ds(pl.multiple_of((c * fold + k) * unit, 16), unit), :],
                        sems.at[1 + side * fold + k],
                    )
                )

    @pl.when(jnp.logical_and(jnp.logical_not(own), part < 3))
    def _():
        remote(0)

    @pl.when(jnp.logical_and(jnp.logical_not(own), part == 3))
    def _():
        remote(1)


def stream(copies, buffer, sems):
    step, steps = pl.program_id(0), pl.num_programs(0)
    slot = lax.rem(step, 2)

    @pl.when(step == 0)
    def _():
        copies(step, buffer.at[slot], sems.at[slot], lambda copy: copy.start())

    @pl.when(step + 1 < steps)
    def _():
        copies(step + 1, buffer.at[1 - slot], sems.at[1 - slot], lambda copy: copy.start())

    copies(step, buffer.at[slot], sems.at[slot], lambda copy: copy.wait())
    return buffer.at[slot]


def gate(values):
    inner = 0.5 * lax.erf(values * math.sqrt(0.5)) + 0.5
    bell = jnp.exp(values * values * -0.5) * (1.0 / math.sqrt(2.0 * math.pi))
    return values * inner, inner + values * bell


def up_kernel(place, second, bias, *refs):
    sources, (active, slope, buffer, sems) = refs[:5], refs[5:]
    weights = stream(lambda *at: up_copies(sources, place, *at), buffer, sems)
    value, rise = gate(dot(second[...], weights[...]) + bias[...])
    active[...] = value.astype(BF16)
    slope[...] = rise.astype(BF16)


def down_kernel(place, active, middle, *refs):
    sources, (out, buffer, sems) = refs[:5], refs[5:]
    weights = stream(lambda *at: down_copies(sources, place, *at), buffer, sems)

    @pl.when(pl.program_id(0) == 0)
    def _():
        out[...] = middle[...]

    out[...] += dot(active[...], weights[...])


def back_kernel(place, branch, slope, *refs):
    up, down = refs[:5], refs[5:10]
    d_hidden, sums, out, buffer, sems, buffer_two, sems_two = refs[10:]
    up_part = stream(lambda *at: up_copies(up, place, *at), buffer, sems)
    down_part = stream(lambda *at: down_copies(down, place, *at), buffer_two, sems_two)

    @pl.when(pl.program_id(0) == 0)
    def _():
        out[...] = jnp.zeros_like(out)

    d_active = dot_rt(branch[...], down_part[...])
    low = (d_active * slope[...].astype(F32)).astype(BF16)
    d_hidden[...] = low
    sums[...] = jnp.sum(low.astype(F32), axis=0, keepdims=True)
    out[...] += dot_rt(low, up_part[...])


def feed_call(kernel, count, inputs, outputs, slots, matmuls, place, *values):
    def at(j, place):
        return chunk_place(j, place, FF // 2)

    specs = {
        "hidden": pl.BlockSpec((count, CHUNK), lambda j, place: (0, at(j, place))),
        "row": pl.BlockSpec((1, CHUNK), lambda j, place: (0, at(j, place))),
        "whole": pl.BlockSpec((count, D), lambda j, place: (0, 0)),
        "any": pl.BlockSpec(memory_space=pl.ANY),
    }
    shapes = {
        "hidden": jax.ShapeDtypeStruct((count, FF), BF16),
        "row": jax.ShapeDtypeStruct((1, FF), F32),
        "whole": jax.ShapeDtypeStruct((count, D), F32),
    }
    scratch = []
    for slot in slots:
        scratch += [pltpu.VMEM((2, *slot), BF16), pltpu.SemaphoreType.DMA((2, 9))]
    return pl.pallas_call(
        kernel,
        grid_spec=pltpu.PrefetchScalarGridSpec(
            num_scalar_prefetch=1,
            grid=(FF // CHUNK,),
            in_specs=[specs[name] for name in inputs],
            out_specs=[specs[name] for name in outputs],
            scratch_shapes=scratch,
        ),
        out_shape=[shapes[name] for name in outputs],
        compiler_params=pltpu.CompilerParams(vmem_limit_bytes=VMEM_ASKED),
        cost_estimate=pl.CostEstimate(flops=1, bytes_accessed=1, transcendentals=0),
    )(place, *values)


UP_SLOT, DOWN_SLOT = (D, CHUNK), (CHUNK, D)


def feed_up(place, second, bias, up):
    names = ["whole", "row"] + ["any"] * 5
    return feed_call(
        up_kernel, second.shape[0], names, ["hidden", "hidden"], [UP_SLOT], 1, place, second, bias, *up
    )


def feed_down(place, active, middle, down):
    names = ["hidden", "whole"] + ["any"] * 5
    return feed_call(
        down_kernel, active.shape[0], names, ["whole"], [DOWN_SLOT], 1, place, active, middle, *down
    )[0]


def feed_back(place, branch, slope, up, down):
    names = ["whole", "hidden"] + ["any"] * 10
    return feed_call(
        back_kernel, branch.shape[0], names, ["hidden", "row", "whole"], [UP_SLOT, DOWN_SLOT], 2,
        place, branch, slope, *up, *down,
    )


def term_kernel(steps, place, *refs):
    count = len(steps)
    query, _, inner, core = (place[i] for i in range(4))
    lefts, rights, (own, sent, blocks), turned = (
        refs[:count],
        refs[count : 2 * count],
        refs[2 * count : 2 * count + 3],
        refs[2 * count + 3 :],
    )
    every = sum(steps)
    step = pl.program_id(0)
    half = jnp.where(step < every, 1 - core, core)

    @pl.when(step % every == 0)
    def _():
        outer = blocks.shape[0] // 8
        size = 2 * outer * blocks.shape[1]
        for left, into in zip(lefts, turned):
            blocks[...] = left[...].astype(F32).T.reshape(blocks.shape)
            for to in range(4):
                first, second = to // 2, to % 2
                x = query ^ jnp.where(half == 0, first, second)
                y = inner ^ jnp.where(half == 0, second, first)
                rows = [
                    blocks[((z * 2 + y) * 2 + c) * 2 + x] for z in range(outer) for c in range(2)
                ]
                into[pl.ds(to * size, size), :] = jnp.concatenate(rows, axis=0).astype(BF16)

    column = step % every
    begin = 0
    for left, right, size in zip(turned, rights, steps):
        for out, mine in ((own, True), (sent, False)):

            @pl.when(
                jnp.logical_and(
                    jnp.logical_and(column >= begin, column < begin + size), (step >= every) == mine
                )
            )
            def _():
                out[...] = dot(left[...], right[...]).astype(BF16).reshape(out.shape)

        begin += size


def weight_terms(place, *pairs):
    count, rows = pairs[0][0].shape
    steps = [right.shape[1] // 2 // CHUNK for _, right in pairs]
    every = sum(steps)
    shape = (2, 2, rows // 4, every * CHUNK)

    def right_spec(begin, size):
        def at(j, place):
            half = jnp.where(j < every, 1 - place[3], place[3])
            return (0, half * size + jnp.clip(j % every - begin, 0, size - 1))

        return pl.BlockSpec((count, CHUNK), at)

    block = (2, 2, rows // 4, CHUNK)
    left_spec = pl.BlockSpec((count, rows), lambda j, place: (0, 0))
    return pl.pallas_call(
        lambda *refs: term_kernel(steps, *refs),
        grid_spec=pltpu.PrefetchScalarGridSpec(
            num_scalar_prefetch=1,
            grid=(2 * every,),
            in_specs=[left_spec] * len(pairs)
            + [right_spec(sum(steps[:i]), size) for i, size in enumerate(steps)],
            out_specs=[
                pl.BlockSpec(block, lambda j, place: (0, 0, 0, jnp.maximum(j - every, 0))),
                pl.BlockSpec(block, lambda j, place: (0, 0, 0, jnp.minimum(j, every - 1))),
            ],
            scratch_shapes=[pltpu.VMEM((32, rows // 32, count), F32)]
            + [pltpu.VMEM((rows, count), BF16)] * len(pairs),
        ),
        out_shape=[jax.ShapeDtypeStruct(shape, BF16)] * 2,
        compiler_params=pltpu.CompilerParams(vmem_limit_bytes=VMEM_ASKED),
        cost_estimate=pl.CostEstimate(flops=1, bytes_accessed=1, transcendentals=0),
    )(place, *[left for left, _ in pairs], *[right for _, right in pairs])


def tall_kernel(place, left, right, own, sent, blocks, turned):
    query, _, inner, core = (place[i] for i in range(4))
    width = blocks.shape[1]
    blocks[...] = left[...].astype(F32).T.reshape(blocks.shape)
    for to in range(4):
        source = (to % 2) * 2 + to // 2
        turned[pl.ds(to * width, width), :] = blocks[source].astype(BF16)
    terms = dot(turned[...], right[...]).astype(BF16)
    size = terms.shape[1] // 2
    y_place = (pl.program_id(0) % 2) ^ inner
    for half in range(2):
        for x in range(2):
            x_place = x ^ query
            at = (y_place, x_place)
            value = terms[2 * x * width : 2 * (x + 1) * width, half * size : (half + 1) * size]

            @pl.when(core == half)
            def _():
                own[at[0], at[1], 0] = value

            @pl.when(core != half)
            def _():
                sent[at[0], at[1], 0] = value


def tall_terms(place, left, right, outer):
    count, rows = left.shape
    columns = right.shape[1]
    wide = rows // (2 * outer)
    shape = (2, 2, outer, wide // 2, columns // 2)
    out = pl.BlockSpec(
        (2, 2, 1, wide // 2, columns // 2), lambda j, place: (0, 0, j // 2, 0, 0)
    )
    own, sent = pl.pallas_call(
        tall_kernel,
        grid_spec=pltpu.PrefetchScalarGridSpec(
            num_scalar_prefetch=1,
            grid=(2 * outer,),
            in_specs=[
                pl.BlockSpec((count, wide), lambda j, place: (0, j)),
                pl.BlockSpec((count, columns), lambda j, place: (0, 0)),
            ],
            out_specs=[out, out],
            scratch_shapes=[
                pltpu.VMEM((4, wide // 4, count), F32),
                pltpu.VMEM((wide, count), BF16),
            ],
        ),
        out_shape=[jax.ShapeDtypeStruct(shape, BF16)] * 2,
        compiler_params=pltpu.CompilerParams(vmem_limit_bytes=VMEM_ASKED),
        cost_estimate=pl.CostEstimate(flops=1, bytes_accessed=1, transcendentals=0),
    )(place, left, right)
    flat = (2, 2, outer * wide // 2, columns // 2)
    return own.reshape(flat), sent.reshape(flat)


def assemble_kernel(pieces, width, count, place_ref, *refs):
    sources, full, sems = refs[:count], refs[count], refs[count + 1]
    step = pl.program_id(0)
    copies = []
    for i, (source, row, rows, column) in enumerate(pieces):
        start = pl.multiple_of(place_ref[i], 16)
        columns = pl.ds(pl.multiple_of(column + step * width, 128), width)
        copies.append(
            pltpu.make_async_copy(
                sources[source].at[pl.ds(row, rows), columns],
                full.at[pl.ds(start, rows), :],
                sems.at[i],
            )
        )
    for copy in copies:
        copy.start()
    for copy in copies:
        copy.wait()


def assemble(sources, pieces, places, shape, width):
    count = len(sources)
    rows, columns = shape
    return pl.pallas_call(
        lambda *refs: assemble_kernel(pieces, width, count, *refs),
        grid=(columns // width,),
        out_shape=jax.ShapeDtypeStruct(shape, BF16),
        in_specs=[pl.BlockSpec(memory_space=pltpu.SMEM)]
        + [pl.BlockSpec(memory_space=pl.ANY)] * count,
        out_specs=pl.BlockSpec((rows, width), lambda j: (0, j)),
        scratch_shapes=[pltpu.SemaphoreType.DMA((len(pieces),))],
        compiler_params=pltpu.CompilerParams(vmem_limit_bytes=32 << 20),
        cost_estimate=pl.CostEstimate(flops=1, bytes_accessed=1, transcendentals=0),
    )(jnp.stack(places).astype(jnp.int32), *sources)


def sync(*values):
    return lax.optimization_barrier(values)


def tie(value, *others):
    return lax.optimization_barrier((value, others))[0] if others else value


class Grid:
    def __init__(self, mesh):
        dp, query = mesh.shape["dp"], mesh.shape["query"]
        core = 2 if dp % 2 == 0 else 1
        rest = dp // core
        outer = 4 if rest % 4 == 0 else rest
        inner = rest // outer
        self.dp, self.query = dp, query
        self.size = {"z": outer, "y": inner, "c": core, "x": query}
        self.stride = {"z": inner * core, "y": core, "c": 1}
        self.order = ["z", "y", "c", "x"]

    def paired(self):
        size = self.size
        pairs = size["x"] == 2 and size["y"] == 2 and size["c"] == 2
        return pairs and size["z"] in (2, 4) and D % (self.dp * self.query * 8) == 0

    def place(self, axis):
        if axis == "x":
            return lax.axis_index("query")
        return (lax.axis_index("dp") // self.stride[axis]) % self.size[axis]

    def partner(self, axis, at, step):
        size = self.size[axis]
        return at ^ step if size & (size - 1) == 0 else (at + step) % size

    def sender(self, axis, at, step):
        size = self.size[axis]
        return at ^ step if size & (size - 1) == 0 else (at + size - step) % size

    def hop(self, value, axis, step=1):
        if axis == "x":
            pairs = [(i, self.partner("x", i, step)) for i in range(self.query)]
            return lax.ppermute(value, "query", pairs)
        stride, size = self.stride[axis], self.size[axis]
        pairs = []
        for i in range(self.dp):
            at = (i // stride) % size
            pairs.append((i, i + (self.partner(axis, at, step) - at) * stride))
        return lax.ppermute(value, "dp", pairs)

    def turn_hop(self, value, turn):
        pairs = []
        for i in range(self.dp):
            core = i % 2
            y = (i // self.stride["y"]) % 2
            for x in range(2):
                if core == turn:
                    to = i * 2 + 1 - x
                else:
                    to = (i + (1 - 2 * y) * self.stride["y"]) * 2 + x
                pairs.append((i * 2 + x, to))
        return lax.ppermute(value, ("dp", "query"), pairs)

    def share(self, value, axis=0, after=()):
        if self.query == 1:
            return value
        if self.query != 2:
            return lax.all_gather(value, "query", axis=axis, tiled=True)
        other = tie(self.hop(value, "x"), *after)
        first = lax.axis_index("query") == 0
        return jnp.concatenate(
            [jnp.where(first, value, other), jnp.where(first, other, value)], axis=axis
        )

    def joined(self, mine, other, axis=0):
        first = lax.axis_index("query") == 0
        return jnp.concatenate(
            [jnp.where(first, mine, other), jnp.where(first, other, mine)], axis=axis
        )

    def total(self, value):
        if self.query == 1:
            return value
        if self.query != 2:
            return lax.psum(value, "query")
        return value + self.hop(value, "x")

    def cut_step(self, value, axis, dim):
        me = self.place(axis)
        return (
            lax.dynamic_index_in_dim(value, me, axis=dim, keepdims=False),
            lax.dynamic_index_in_dim(value, 1 - me, axis=dim, keepdims=False),
        )

    def cut_columns(self, terms):
        half = terms.shape[1] // 2
        first = self.place("c") == 0
        left, right = terms[:, :half], terms[:, half:]
        return jnp.where(first, left, right), jnp.where(first, right, left)

    def join_columns(self, value):
        value = value.reshape(2, -1, value.shape[-1])
        mine, other = self.cut_step(value, "c", 0)
        got = self.hop(other, "c")
        first = self.place("c") == 0
        return jnp.concatenate(
            [jnp.where(first, mine, got), jnp.where(first, got, mine)], axis=1
        )

    def scatter_step(self, value, axis, dim, kind):
        size = self.size[axis]
        me = self.place(axis)

        def part(index):
            return lax.dynamic_index_in_dim(value, index, axis=dim, keepdims=False)

        if size == 1:
            return part(0)
        sent = [
            self.hop(part(self.partner(axis, me, step)), axis, step) for step in range(1, size)
        ]
        total = part(me).astype(F32)
        for received in sent:
            total = total + received.astype(F32)
        return total.astype(kind)

    def scatter(self, value, order, kind=BF16):
        dims = [axis for axis in self.order if axis in order]
        for axis in order:
            dim = dims.index(axis)
            value = self.scatter_step(value, axis, dim, kind)
            dims.pop(dim)
        return value

    def scatter_z(self, value):
        stride, size = self.stride["z"], self.size["z"]
        groups = [[k * stride + i for k in range(size)] for i in range(stride)]
        return lax.psum_scatter(
            value, "dp", scatter_dimension=0, axis_index_groups=groups, tiled=True
        )

    def blocks(self, value):
        shape = [self.size[axis] for axis in self.order]
        rows = value.shape[0] // math.prod(shape)
        return value.reshape(*shape, rows, *value.shape[1:])

    def own_columns(self, value):
        width = value.shape[1] // (self.dp * self.query)
        shaped = value.reshape(value.shape[0], self.dp, self.query, width)
        mine = lax.dynamic_index_in_dim(shaped, self.place("x"), axis=2, keepdims=False)
        return mine.reshape(value.shape[0], self.dp * width)

    def part_of(self, shards):
        zb, y, c = self.place("z") % 2, self.place("y"), self.place("c")
        unit = min(shard.shape[0] for shard in shards) // 8
        mine = (zb * 2 + y) * 2 + c
        columns = []
        for shard in shards:
            fold = shard.shape[0] // (8 * unit)
            for k in range(fold):
                columns.append(
                    lax.dynamic_slice_in_dim(shard, (mine * fold + k) * unit, unit, 0)
                )
        return jnp.concatenate(columns, axis=1) if len(columns) > 1 else columns[0]

    def sides_of(self, first, after=()):
        first = tie(first, *after)
        return [self.hop(first, "y"), self.hop(first, "z")]

    def corners_of(self, sides, after=()):
        by_y, by_z = tie(sides, *after)
        cut = by_y.shape[0] // 2 // 16 * 16
        sent = (by_z[:cut], by_y[cut:])
        return sent, [self.hop(sent[0], "y"), self.hop(sent[1], "z")]

    def most_of(self, first, sides, *after):
        near = jnp.concatenate([tie(first, *after), *sides], axis=0)
        return near, self.hop(near, "c")

    def corner_of(self, corners, after=()):
        near = jnp.concatenate(tie(corners, *after), axis=0)
        return near, self.hop(near, "c")

    def join(self, shard, parts, column):
        zb, y, c, x = self.place("z") % 2, self.place("y"), self.place("c"), self.place("x")
        rows, width = shard.shape
        unit = rows // 8
        pieces, places = [(0, 0, rows, 0)], [x * rows]
        for side in range(2):
            c_ = c if side == 0 else 1 - c
            for part in range(4):
                place = ((zb ^ (part // 2)) * 2 + (y ^ (part % 2))) * 2 + c_
                pieces.append((1 + 2 * side + part // 3, part % 3 * unit, unit, column))
                places.append((1 - x) * rows + place * unit)
        return assemble([shard, *parts], pieces, places, (2 * rows, width), 640)

    def places(self):
        return jnp.stack(
            [self.place("x"), self.place("z") % 2, self.place("y"), self.place("c")]
        ).astype(jnp.int32)


def added(*values):
    total = values[0].astype(F32)
    for value in values[1:]:
        total = total + value.astype(F32)
    return total.astype(BF16)


def added_wide(*values):
    total = values[0].astype(F32)
    for value in values[1:]:
        total = total + value.astype(F32)
    return total


class Sums:
    def __init__(self, grid, own, sent):
        self.grid, self.own, self.sent = grid, own, sent

    def core(self, *after):
        self.got = self.grid.hop(tie(self.sent, *after), "c")

    def add_first(self, *after):
        own, got = tie((self.own, self.got), *after)
        self.first_in = [added(own[1, k], got[1, k]) for k in (1, 0)]

    def add_turned(self, *after):
        own, got = tie((self.own, self.got), *after)
        self.one_in = added(own[1], got[1])

    def go_turned(self, *after):
        one = self.grid.turn_hop(tie(self.one_in, *after), 0)
        self.one = [one[1], one[0]]

    def add_second(self, *after):
        own, got, one = tie((self.own, self.got, self.one[0]), *after)
        self.two_in = added(own[0, 1], got[0, 1], one)

    def add_last(self, *after):
        own, got, one = tie((self.own, self.got, self.one[1]), *after)
        whole = added(own[0, 0], got[0, 0], one, self.two)
        size = self.grid.size["z"]
        self.last_in = whole.reshape(size, whole.shape[0] // size, whole.shape[1])

    def last(self, *after):
        self.sum = self.grid.scatter_z(tie(self.last_in, *after))

    def result(self, *after):
        value = tie(self.sum, *after)[0]
        value = value.reshape(2, value.shape[0] // 2, value.shape[1])
        mine, other = self.grid.cut_step(value, "c", 0)
        got = self.grid.hop(other, "c")
        first = self.grid.place("c") == 0
        return [
            jnp.where(first, mine, got).astype(F32),
            jnp.where(first, got, mine).astype(F32),
        ]


def make_shards(grid):
    def shards(
        tokens,
        cell_lengths,
        out_cotangent,
        ln_gains,
        ln_biases,
        proj_biases,
        ff_biases,
        w_qkv,
        w_out,
        w_up,
        w_down,
        dec_cell,
        dec_gene,
        dec_out,
        gene_table,
        query_ids,
        labels,
    ):
        row_count = tokens.shape[0]
        token_count = row_count * ROW_LEN
        dp_count, query_count = grid.dp, grid.query
        place = lax.axis_index("query")
        starts, segment = cell_layout(cell_lengths)
        local_cells = row_count * CELLS_ROW
        pair_cells, local_queries = query_ids.shape
        pairs = pair_cells * local_queries
        half_width = D // query_count

        flat_tokens = tokens.astype(F32).reshape(token_count, D)
        where = grid.places()
        ids = grid.share(query_ids.reshape(1, pairs)).reshape(query_count * pairs)
        qkv_first = grid.hop(grid.part_of([w_qkv]), "x")
        normed, first_pull = jax.vjp(layer_norm, flat_tokens, ln_gains[0], ln_biases[0])
        normed_low = normed.astype(BF16)
        table_rows = gene_table.shape[0]
        local_ids = ids - place * table_rows
        held = (local_ids[:, None] == jnp.arange(table_rows, dtype=jnp.int32)[None, :]).astype(BF16)
        gene_found = dot(held, gene_table).astype(BF16)
        up_part = grid.part_of([w_up, w_out])
        down_part = grid.part_of([w_down])
        qkv_first, normed_low, gene_found, up_part, down_part = sync(
            qkv_first, normed_low, gene_found, up_part, down_part
        )
        up_first = grid.hop(up_part, "x")
        qkv_sides = sync(*grid.sides_of(qkv_first))
        _, qkv_corners = grid.corners_of(qkv_sides)
        qkv_near, qkv_far = grid.most_of(qkv_first, qkv_sides)
        qkv_corners = sync(*qkv_corners, qkv_near)[:2]
        qkv_end, qkv_end_far = grid.corner_of(qkv_corners)
        qkv_end_far, qkv_far, up_first = sync(qkv_end_far, qkv_far, up_first)
        up_sides = grid.sides_of(up_first)
        gene_hop = grid.hop(tie(gene_found, up_first), "x")
        full_qkv = grid.join(w_qkv, (qkv_near, qkv_end, qkv_far, qkv_end_far), 0)
        zeroes = jnp.zeros((D,), F32)
        qkv_bias = jnp.concatenate([proj_biases[0], zeroes, proj_biases[1]])
        qkv_low = (dot(normed_low, full_qkv) + qkv_bias).astype(BF16)
        qkv_low, *up_sides, gene_hop = sync(qkv_low, *up_sides, gene_hop)
        qkv_rows = qkv_low.reshape(row_count, ROW_LEN, 3 * D)
        up_sent, up_corners = grid.corners_of(up_sides)
        down_first = grid.hop(tie(down_part, gene_hop), "x")
        cut = HEADS // 4
        mixed_one, totals_one = attend(tie(qkv_rows, up_sent), segment, 0, cut)
        gene_rows = added(gene_found, tie(gene_hop, mixed_one)) if query_count == 2 else gene_found
        up_near, up_far = grid.most_of(up_first, tie(up_sides, mixed_one))
        mixed_two, totals_two = attend(
            tie(qkv_rows, mixed_one, up_near), segment, cut, HEADS // 2 - cut
        )
        mixed_two, *up_corners, down_first = sync(mixed_two, *up_corners, down_first)
        down_sides = grid.sides_of(down_first)
        up_end, up_end_far = grid.corner_of(up_corners)
        mixed_rows = jnp.concatenate([mixed_one, mixed_two], axis=2)
        log_totals = jnp.concatenate([totals_one, totals_two], axis=1)
        mixed_low = mixed_rows.reshape(token_count, D)
        up_parts = (up_near, up_end, up_far, up_end_far)
        up_weights = (w_up, *up_parts)
        full_out = grid.join(w_out, up_parts, FF)
        middle = flat_tokens + dot(mixed_low, full_out) + proj_biases[2]
        second, second_pull = jax.vjp(layer_norm, middle, ln_gains[1], ln_biases[1])
        second_low = second.astype(BF16)
        gene_half = lax.dynamic_slice_in_dim(gene_rows, place * half_width, half_width, 1)
        gene_partial = dot(tie(gene_half, mixed_two), dec_gene).astype(BF16).reshape(query_count, pairs, FF)
        gene_mine, gene_sent = grid.cut_step(gene_partial, "x", 0)
        second_low, gene_sent = sync(second_low, gene_sent)
        gene_got = grid.hop(gene_sent, "x")
        active_low, slope = feed_up(where, second_low, ff_biases[0][None, :], up_weights)
        active_low, slope, *down_sides, gene_got = sync(active_low, slope, *down_sides, gene_got)
        places = jnp.arange(ROW_LEN, dtype=jnp.int32)
        leading = jnp.any(places[None, :, None] == starts[:, None, :], axis=2)
        early_low = jnp.where(
            leading[:, :, None], 0, out_cotangent
        ).reshape(token_count, D).astype(BF16)
        down_sent, down_corners = grid.corners_of(down_sides)
        down_near, down_far = grid.most_of(down_first, down_sides, down_sent)
        early_low = tie(early_low, down_near, down_sent)
        down_sums = Sums(grid, *tall_terms(where, active_low, early_low, grid.size["z"]))
        down_sums.sent, *down_corners, down_far = sync(down_sums.sent, *down_corners, down_far)
        down_end, down_end_far = grid.corner_of(down_corners)
        down_weights = (w_down, down_near, down_end, down_far, down_end_far)
        down_sums.core(down_end_far)
        encoded = feed_down(
            where, tie(active_low, down_sums.sent), middle + proj_biases[3], down_weights
        )
        encoded, down_sums.got = sync(encoded, down_sums.got)
        encoded_rows = encoded.reshape(row_count, ROW_LEN, D)
        heads_low = (
            jnp.take_along_axis(encoded_rows, starts[:, :, None], axis=1)
            .reshape(local_cells, D)
            .astype(BF16)
        )
        down_sums.add_first(heads_low)
        heads_hop = grid.hop(heads_low, "x") if query_count == 2 else heads_low
        one_b = grid.hop(down_sums.first_in[0], "y")
        cell_heads = grid.joined(heads_low, tie(heads_hop, down_sums.first_in))
        heads_half = lax.dynamic_slice_in_dim(cell_heads, place * half_width, half_width, 1)
        cell_part = grid.total(dot(heads_half, dec_cell))
        gene_part = added_wide(gene_mine, gene_got) + ff_biases[1]
        before = cell_part[:, None, :] + gene_part.reshape(pair_cells, local_queries, FF)
        gated_dec, gated_pull = jax.vjp(smooth_gate, before)
        logit_weight = dec_out.astype(F32)
        logits = jnp.sum(gated_dec * logit_weight, axis=-1)
        logit_slope = jax.nn.sigmoid(logits) - labels.astype(F32)
        (grad_before,) = gated_pull(logit_slope[:, :, None] * logit_weight)
        before_low = grad_before.astype(BF16)
        before_sums = jnp.sum(before_low, axis=1, dtype=F32)
        grad_dec_bias = jnp.sum(before_sums, axis=0)
        grad_logit = jnp.sum(gated_dec * logit_slope[:, :, None], axis=(0, 1))
        cell_total = grid.total(before_sums).astype(BF16)
        heads_part = dot_rt(cell_total, dec_cell).astype(BF16)
        heads_all = grid.share(heads_part, axis=1)
        heads_back = lax.dynamic_slice_in_dim(
            heads_all, place * local_cells, local_cells, 0
        ).astype(F32)
        picker = (places[None, :, None] == starts[:, None, :]).astype(F32)
        grad_encoded = out_cotangent.astype(F32) + jnp.sum(
            picker[:, :, :, None] * heads_back.reshape(row_count, 1, CELLS_ROW, D), axis=2
        )
        grad_flat = grad_encoded.reshape(token_count, D)
        branch_low = grad_flat.astype(BF16)
        branch_low, one_b, before_low = sync(branch_low, one_b, before_low)
        before_hop = grid.hop(before_low, "x") if query_count == 2 else before_low
        one_a = grid.hop(down_sums.first_in[1], "y")
        down_sums.one = [one_b, one_a]
        down_sums.add_second()
        down_sums.two = grid.hop(tie(down_sums.two_in, before_hop), "x")
        hidden_low, up_bias_sums, grad_second = feed_back(
            where, tie(branch_low, before_low, down_sums.two_in, before_hop), slope, up_weights, down_weights
        )
        hidden_low, grad_second, one_a = sync(hidden_low, grad_second, one_a)
        grad_up_bias = up_bias_sums[0]
        up_sums = Sums(grid, *weight_terms(where, (second_low, hidden_low)))
        up_sums.sent, down_sums.two, one_a = sync(up_sums.sent, down_sums.two, one_a)
        down_sums.one = [one_b, one_a]
        up_sums.core()

        middle_part, grad_gain_two, grad_shift_two = second_pull(tie(grad_second, up_sums.sent))
        grad_middle = grad_flat + middle_part
        attn_low = grad_middle.astype(BF16)
        mixed_back = dot_rt(attn_low, full_out).astype(BF16)
        before_all = grid.joined(before_low, tie(before_hop, mixed_back)).reshape(query_count * pairs, FF)
        gene_terms = dot_lt(grid.own_columns(gene_rows), before_all).astype(BF16)
        shape = [grid.size[axis] for axis in "zyc"]
        gene_mine, gene_sent = grid.cut_columns(gene_terms)
        up_sums.add_turned(gene_sent)
        up_sums.one_in, gene_sent, mixed_back = sync(up_sums.one_in, gene_sent, mixed_back)
        up_sums.go_turned()
        gene_got = grid.hop(gene_sent, "c")
        d_query, d_key, d_value = attend_back(
            qkv_rows, segment, mixed_rows, mixed_back.reshape(row_count, ROW_LEN, D), log_totals
        )
        d_query, d_key, d_value, gene_got = sync(d_query, d_key, d_value, gene_got)
        down_sums.add_last(d_query)
        down_sums.last()
        gene_sum = added(gene_mine, gene_got)
        gene_sum = grid.scatter_z(tie(gene_sum.reshape(grid.size["z"], -1, gene_sum.shape[1]), down_sums.last_in))
        qkv_back_low = jnp.concatenate([d_query, d_key, d_value], axis=2).reshape(token_count, 3 * D)
        attn_sums = Sums(
            grid,
            *weight_terms(
                where, (normed_low, tie(qkv_back_low, down_sums.last_in)), (mixed_low, attn_low)
            ),
        )
        attn_sums.sent, qkv_back_low, *up_sums.one = sync(attn_sums.sent, qkv_back_low, *up_sums.one)
        attn_sums.core()
        up_sums.add_second(attn_sums.sent)
        up_sums.two = grid.turn_hop(up_sums.two_in, 1)
        grad_normed = dot_rt(tie(qkv_back_low, up_sums.two_in), full_qkv)
        grad_normed, attn_sums.got = sync(grad_normed, attn_sums.got)
        attn_sums.add_turned()
        attn_sums.go_turned(up_sums.two)
        bias_sums = jnp.sum(qkv_back_low, axis=0, dtype=F32)
        token_part, grad_gain_one, grad_shift_one = first_pull(tie(grad_normed, attn_sums.one_in))
        grad_tokens = (grad_middle + token_part).reshape(row_count, ROW_LEN, D)
        grad_tokens, up_sums.two = sync(grad_tokens, up_sums.two)
        up_sums.add_last()
        up_sums.last()
        grad_attn_bias = jnp.sum(attn_low, axis=0, dtype=F32)
        grad_out_bias = jnp.sum(branch_low, axis=0, dtype=F32)

        leading_low = tie(picker.astype(BF16).transpose(0, 2, 1), up_sums.last_in)
        active_heads = jnp.einsum(
            "rcl,rlf->rcf", leading_low, active_low.reshape(row_count, ROW_LEN, FF), preferred_element_type=F32
        ).astype(BF16).reshape(local_cells, FF)
        branch_heads = jnp.einsum(
            "rcl,rld->rcd", leading_low, branch_low.reshape(row_count, ROW_LEN, D), preferred_element_type=F32
        ).astype(BF16).reshape(local_cells, D)
        late_low = jnp.concatenate([active_heads, branch_heads], axis=1)
        genes_part = dot_rt(tie(before_all, up_sums.last_in), dec_gene).astype(BF16)
        late_low, genes_part, *attn_sums.one = sync(late_low, genes_part, *attn_sums.one)
        attn_sums.add_second()
        attn_sums.two = grid.turn_hop(attn_sums.two_in, 1)
        late_low, genes_part = tie((late_low, genes_part), attn_sums.two_in)
        late = grid.share(late_low)
        gathered = lax.all_gather(
            jnp.concatenate([cell_heads, cell_total, late], axis=1), "dp", axis=0, tiled=True
        )
        genes_back = grid.share(genes_part, axis=1)
        choose = (ids[:, None] == jnp.arange(GENES, dtype=jnp.int32)[None, :]).astype(BF16)
        table_terms = dot_lt(grid.own_columns(choose), genes_back).astype(BF16)
        table_terms = table_terms.reshape(*shape, -1, D)
        table_terms = grid.scatter_step(table_terms, "c", 2, BF16)
        table_terms = grid.scatter_step(table_terms, "y", 1, BF16)
        attn_sums.two, table_terms = sync(attn_sums.two, table_terms)
        attn_sums.add_last()
        attn_sums.last()
        grad_table = grid.scatter_z(tie(table_terms, attn_sums.last_in))[0].astype(F32)

        gene_sum = tie(gene_sum, attn_sums.last_in).reshape(grid.size["y"], -1, gene_sum.shape[2])
        gene_sum = grid.scatter_step(gene_sum, "y", 0, BF16)
        grad_gene = grid.join_columns(gene_sum).astype(F32)
        gathered = tie(gathered, attn_sums.last_in)
        all_heads, all_cells, all_active, all_branch = jnp.split(
            gathered, [D, D + FF, D + 2 * FF], axis=1
        )
        owned = D // (dp_count * query_count)
        mine = lax.axis_index("dp") * query_count + place
        grad_cell = dot_lt(
            lax.dynamic_slice_in_dim(all_heads, mine * owned, owned, 1), all_cells
        )
        tall = FF // (dp_count * query_count)
        late_down = dot_lt(
            lax.dynamic_slice_in_dim(all_active, mine * tall, tall, 1), all_branch
        )

        owners = dp_count * query_count

        def owned_cols(values):
            return values.reshape(-1, owners, values.shape[-1] // owners).transpose(1, 0, 2).reshape(owners, -1)

        small = [
            jnp.stack([grad_gain_one, grad_gain_two]),
            jnp.stack([grad_shift_one, grad_shift_two]),
            jnp.stack([bias_sums[:D], bias_sums[2 * D :], grad_attn_bias, grad_out_bias]),
            jnp.stack([grad_up_bias, grad_dec_bias]),
            grad_logit[None, :],
        ]
        flat = [owned_cols(v) for v in small]
        joined = jnp.concatenate(flat, axis=1)
        summed = grid.scatter(grid.blocks(joined), "cxyz", F32).reshape(-1)
        outs = []
        start = 0
        for value, piece in zip(small, flat):
            size = piece.shape[1]
            outs.append(summed[start : start + size].reshape(value.shape[0], -1))
            start += size

        attn_sum = attn_sums.result()
        qkv_cut = 3 * D // 2

        return (
            encoded_rows,
            grad_tokens,
            outs[0],
            outs[1],
            outs[2],
            outs[3],
            jnp.concatenate([half[:, :qkv_cut] for half in attn_sum], axis=1),
            jnp.concatenate([half[:, qkv_cut:] for half in attn_sum], axis=1),
            jnp.concatenate(up_sums.result(attn_sums.last_in), axis=1),
            jnp.concatenate(down_sums.result(attn_sums.last_in), axis=1) + late_down,
            grad_cell,
            grad_gene,
            outs[4][0],
            grad_table,
        )

    return shards


def split_heads(qkv_row):
    queries = qkv_row[:, :D].reshape(ROW_LEN, HEADS, HEAD_DIM)
    keys_in = qkv_row[:, D : 2 * D].reshape(ROW_LEN, HEADS, HEAD_DIM)
    values_in = qkv_row[:, 2 * D :].reshape(ROW_LEN, HEADS, HEAD_DIM)
    return (queries, keys_in, values_in)


def row_scores(queries, keys_in, segment_row):
    scores = jnp.einsum("qhd,khd->hqk", queries, keys_in, preferred_element_type=jnp.float32) * (
        1.0 / math.sqrt(HEAD_DIM)
    )
    same_cell = segment_row[:, None] == segment_row[None, :]
    return jnp.where(same_cell[None], scores, -1e30)


def attend_any(member):
    qkv_row, segment_row = member
    queries, keys_in, values_in = split_heads(qkv_row)
    scores = row_scores(queries, keys_in, segment_row)
    highest_score = jnp.max(scores, axis=-1, keepdims=True)
    weights = jnp.exp(scores - highest_score)
    weight_sum = jnp.sum(weights, axis=-1, keepdims=True)
    attention = (weights / weight_sum).astype(jnp.bfloat16)
    mixed = jnp.einsum(
        "hqk,khd->qhd", attention, values_in, preferred_element_type=jnp.float32
    ).astype(jnp.bfloat16)
    return (mixed.reshape(ROW_LEN, D), (highest_score + jnp.log(weight_sum))[:, :, 0])


def attend_back_any(member):
    qkv_row, segment_row, log_total, grad_mixed = member
    queries, keys_in, values_in = split_heads(qkv_row)
    scores = row_scores(queries, keys_in, segment_row)
    attention = jnp.exp(scores - log_total[:, :, None])
    grad_heads = grad_mixed.reshape(ROW_LEN, HEADS, HEAD_DIM)
    grad_probs = jnp.einsum(
        "qhd,khd->hqk", grad_heads, values_in, preferred_element_type=jnp.float32
    )
    grad_scores = (
        attention * (grad_probs - jnp.sum(attention * grad_probs, axis=-1, keepdims=True))
    ).astype(jnp.bfloat16)
    scale_factor = 1.0 / math.sqrt(HEAD_DIM)
    grad_query = (
        jnp.einsum("hqk,khd->qhd", grad_scores, keys_in, preferred_element_type=jnp.float32)
        * scale_factor
    )
    grad_keys = (
        jnp.einsum("hqk,qhd->khd", grad_scores, queries, preferred_element_type=jnp.float32)
        * scale_factor
    )
    grad_values = jnp.einsum(
        "hqk,qhd->khd",
        attention.astype(jnp.bfloat16),
        grad_heads,
        preferred_element_type=jnp.float32,
    )
    return jnp.concatenate(
        [
            grad_query.reshape(ROW_LEN, D),
            grad_keys.reshape(ROW_LEN, D),
            grad_values.reshape(ROW_LEN, D),
        ],
        axis=1,
    )


def owned_cols(values_in, dp_count, query_count, place):
    width = values_in.shape[1] // (dp_count * query_count)
    shaped = values_in.reshape(values_in.shape[0], dp_count, query_count, width)
    return lax.dynamic_index_in_dim(shaped, place, axis=2, keepdims=False)


def owned_term(left, right, dp_count, query_count, place):
    return jnp.einsum(
        "ndr,ne->dre",
        owned_cols(left, dp_count, query_count, place),
        right,
        preferred_element_type=jnp.float32,
    )


def owner_blocks(values_in, dp_count, query_count):
    width = values_in.shape[0] // (dp_count * query_count)
    return values_in.reshape(dp_count, query_count, width, values_in.shape[1])


def shards_any(
    tokens,
    cell_lengths,
    out_cotangent,
    ln_gains,
    ln_biases,
    proj_biases,
    ff_biases,
    w_qkv,
    w_out,
    w_up,
    w_down,
    dec_cell,
    dec_gene,
    dec_out,
    gene_table,
    query_ids,
    labels,
):
    row_count = tokens.shape[0]
    token_count = row_count * ROW_LEN
    dp_count = lax.axis_size("dp")
    query_count = lax.axis_size("query")
    place = lax.axis_index("query")
    starts, segment = cell_layout(cell_lengths)
    gathered = (
        lax.all_gather(w_qkv, "query", axis=0, tiled=True),
        lax.all_gather(w_out, "query", axis=0, tiled=True),
        lax.all_gather(w_up, "query", axis=0, tiled=True),
        lax.all_gather(w_down, "query", axis=0, tiled=True),
        lax.all_gather(dec_cell, "query", axis=0, tiled=True),
        lax.all_gather(dec_gene, "query", axis=0, tiled=True),
        lax.all_gather(gene_table, "query", axis=0, tiled=True),
    )
    full_qkv, full_out, full_up, full_down, full_cell, full_gene, full_table = gathered
    flat_tokens = tokens.astype(jnp.float32).reshape(token_count, D)
    normed, first_pull = jax.vjp(layer_norm, flat_tokens, ln_gains[0], ln_biases[0])
    normed_low = normed.astype(jnp.bfloat16)
    zeroes = jnp.zeros((D,), jnp.float32)
    qkv_bias = jnp.concatenate([proj_biases[0], zeroes, proj_biases[1]])
    qkv_low = (jnp.dot(normed_low, full_qkv, preferred_element_type=jnp.float32) + qkv_bias).astype(
        jnp.bfloat16
    )
    qkv_rows = qkv_low.reshape(row_count, ROW_LEN, 3 * D)
    mixed_rows, log_totals = lax.map(attend_any, (qkv_rows, segment))
    mixed_low = mixed_rows.reshape(token_count, D)
    middle = (
        flat_tokens
        + jnp.dot(mixed_low, full_out, preferred_element_type=jnp.float32)
        + proj_biases[2]
    )
    second, second_pull = jax.vjp(layer_norm, middle, ln_gains[1], ln_biases[1])
    second_low = second.astype(jnp.bfloat16)
    hidden = jnp.dot(second_low, full_up, preferred_element_type=jnp.float32) + ff_biases[0]
    active, active_pull = jax.vjp(smooth_gate, hidden)
    active_low = active.astype(jnp.bfloat16)
    encoded = (
        middle + jnp.dot(active_low, full_down, preferred_element_type=jnp.float32) + proj_biases[3]
    )
    places = jnp.arange(ROW_LEN, dtype=jnp.int32)
    picker = (places[None, None, :] == starts[:, :, None]).astype(jnp.float32)
    local_cells = row_count * CELLS_ROW
    heads_low = (
        jnp.einsum(
            "rcl,rld->rcd", picker, encoded.reshape(row_count, ROW_LEN, D), precision=HIGHEST
        )
        .reshape(local_cells, D)
        .astype(jnp.bfloat16)
    )
    cell_heads = lax.all_gather(heads_low, "query", axis=0, tiled=True)
    cell_part = jnp.dot(cell_heads, full_cell, preferred_element_type=jnp.float32)
    gene_rows = jnp.take(full_table, query_ids, axis=0)
    before = (
        cell_part[:, None, :]
        + jnp.einsum("cqd,df->cqf", gene_rows, full_gene, preferred_element_type=jnp.float32)
        + ff_biases[1]
    )
    gated_dec, gated_pull = jax.vjp(smooth_gate, before)
    logit_weight = dec_out.astype(jnp.float32)
    logits = jnp.einsum("cqf,f->cq", gated_dec, logit_weight, precision=HIGHEST)
    logit_slope = jax.nn.sigmoid(logits) - labels.astype(jnp.float32)
    (grad_before,) = gated_pull(logit_slope[:, :, None] * logit_weight)
    before_low = grad_before.astype(jnp.bfloat16)
    grad_dec_bias = jnp.sum(before_low, axis=(0, 1), dtype=jnp.float32)
    grad_logit = jnp.einsum("cqf,cq->f", gated_dec, logit_slope, precision=HIGHEST)
    gene_terms = jnp.einsum(
        "cqd,cqf->df", gene_rows, before_low, preferred_element_type=jnp.float32
    )
    genes_back = jnp.einsum(
        "cqf,df->cqd", before_low, full_gene, preferred_element_type=jnp.float32
    ).astype(jnp.bfloat16)
    choose = (query_ids.reshape(-1)[:, None] == jnp.arange(GENES, dtype=jnp.int32)[None, :]).astype(
        jnp.bfloat16
    )
    table_terms = jnp.einsum(
        "ng,nd->gd", choose, genes_back.reshape(-1, D), preferred_element_type=jnp.float32
    )
    gene_parts, table_parts = (
        lax.all_to_all(
            owner_blocks(gene_terms, dp_count, query_count).astype(jnp.bfloat16),
            "query",
            split_axis=1,
            concat_axis=1,
            tiled=True,
        ).astype(jnp.float32),
        lax.all_to_all(
            owner_blocks(table_terms, dp_count, query_count).astype(jnp.bfloat16),
            "query",
            split_axis=1,
            concat_axis=1,
            tiled=True,
        ).astype(jnp.float32),
    )
    grad_gene = jnp.sum(gene_parts, axis=1)
    grad_table = jnp.sum(table_parts, axis=1)
    cell_total = lax.psum(
        jnp.sum(before_low, axis=1, dtype=jnp.float32).astype(jnp.bfloat16), "query"
    )
    grad_cell = owned_term(cell_heads, cell_total, dp_count, query_count, place)
    heads_all = jnp.einsum("cf,df->cd", cell_total, full_cell, preferred_element_type=jnp.float32)
    heads_back = (
        lax.dynamic_slice_in_dim(heads_all, place * local_cells, local_cells, 0)
        .astype(jnp.bfloat16)
        .astype(jnp.float32)
    )
    grad_encoded = out_cotangent.astype(jnp.float32) + jnp.einsum(
        "rcl,rcd->rld", picker, heads_back.reshape(row_count, CELLS_ROW, D), precision=HIGHEST
    )
    grad_flat = grad_encoded.reshape(token_count, D)

    def empty_term(left_width, right_width):
        return jnp.zeros(
            (dp_count, left_width // (dp_count * query_count), right_width), jnp.float32
        )

    branch_low = grad_flat.astype(jnp.bfloat16)
    grad_out_bias = jnp.sum(branch_low, axis=0, dtype=jnp.float32)
    grad_active = jnp.einsum("nd,fd->nf", branch_low, full_down, preferred_element_type=jnp.float32)
    (grad_hidden,) = active_pull(grad_active)
    hidden_low = grad_hidden.astype(jnp.bfloat16)
    grad_up_bias = jnp.sum(hidden_low, axis=0, dtype=jnp.float32)
    grad_second = jnp.einsum("nf,df->nd", hidden_low, full_up, preferred_element_type=jnp.float32)
    middle_part, grad_gain_two, grad_shift_two = second_pull(grad_second)
    grad_middle = grad_flat + middle_part
    ff_terms = jnp.stack([grad_up_bias, grad_dec_bias], axis=1)
    attn_low = grad_middle.astype(jnp.bfloat16)
    grad_attn_bias = jnp.sum(attn_low, axis=0, dtype=jnp.float32)
    mixed_back = jnp.einsum(
        "ne,de->nd", attn_low, full_out, preferred_element_type=jnp.float32
    ).astype(jnp.bfloat16)
    qkv_back = lax.map(
        attend_back_any, (qkv_rows, segment, log_totals, mixed_back.reshape(row_count, ROW_LEN, D))
    )
    qkv_back_low = qkv_back.reshape(token_count, 3 * D).astype(jnp.bfloat16)
    bias_sums = jnp.sum(qkv_back_low, axis=0, dtype=jnp.float32)
    grad_normed = jnp.einsum(
        "ne,de->nd", qkv_back_low, full_qkv, preferred_element_type=jnp.float32
    )
    token_part, grad_gain_one, grad_shift_one = first_pull(grad_normed)
    grad_tokens = (grad_middle + token_part).reshape(row_count, ROW_LEN, D)
    gain_terms = jnp.stack([grad_gain_one, grad_gain_two], axis=1)
    shift_terms = jnp.stack([grad_shift_one, grad_shift_two], axis=1)
    proj_terms = jnp.stack(
        [bias_sums[:D], bias_sums[2 * D :], grad_attn_bias, grad_out_bias], axis=1
    )
    totals = (empty_term(D, 3 * D), empty_term(D, D), empty_term(D, FF), empty_term(FF, D))
    pieces = (
        lax.all_gather(normed_low, "query", axis=0, tiled=True),
        lax.all_gather(qkv_back_low, "query", axis=0, tiled=True),
        lax.all_gather(mixed_low, "query", axis=0, tiled=True),
        lax.all_gather(attn_low, "query", axis=0, tiled=True),
        lax.all_gather(second_low, "query", axis=0, tiled=True),
        lax.all_gather(hidden_low, "query", axis=0, tiled=True),
        lax.all_gather(active_low, "query", axis=0, tiled=True),
        lax.all_gather(branch_low, "query", axis=0, tiled=True),
    )
    every_fold = tuple(
        (
            owned_term(pieces[2 * i], pieces[2 * i + 1], dp_count, query_count, place)
            for i in range(len(totals))
        )
    )
    every_sum = (
        lax.psum_scatter(
            every_fold[2].astype(jnp.bfloat16), "dp", scatter_dimension=0, tiled=True
        ).astype(jnp.float32),
        lax.psum_scatter(
            every_fold[3].astype(jnp.bfloat16), "dp", scatter_dimension=0, tiled=True
        ).astype(jnp.float32),
        lax.psum_scatter(
            grad_cell.astype(jnp.bfloat16), "dp", scatter_dimension=0, tiled=True
        ).astype(jnp.float32),
        lax.psum_scatter(
            grad_gene.astype(jnp.bfloat16), "dp", scatter_dimension=0, tiled=True
        ).astype(jnp.float32),
        lax.psum_scatter(
            grad_table.astype(jnp.bfloat16), "dp", scatter_dimension=0, tiled=True
        ).astype(jnp.float32),
        lax.psum_scatter(
            every_fold[0].astype(jnp.bfloat16), "dp", scatter_dimension=0, tiled=True
        ).astype(jnp.float32),
        lax.psum_scatter(
            every_fold[1].astype(jnp.bfloat16), "dp", scatter_dimension=0, tiled=True
        ).astype(jnp.float32),
    )
    ffn_sums = every_sum[:5]
    attn_sums = every_sum[5:]
    small_sums = (
        lax.psum_scatter(gain_terms, ("dp", "query"), scatter_dimension=0, tiled=True),
        lax.psum_scatter(shift_terms, ("dp", "query"), scatter_dimension=0, tiled=True),
        lax.psum_scatter(proj_terms, ("dp", "query"), scatter_dimension=0, tiled=True),
        lax.psum_scatter(ff_terms, ("dp", "query"), scatter_dimension=0, tiled=True),
        lax.psum_scatter(grad_logit, ("dp", "query"), scatter_dimension=0, tiled=True),
    )

    def flat_rows(values_in):
        return values_in.reshape(-1, values_in.shape[-1])

    return (
        encoded.reshape(row_count, ROW_LEN, D),
        grad_tokens,
        small_sums[0].T,
        small_sums[1].T,
        small_sums[2].T,
        small_sums[3].T,
        flat_rows(attn_sums[0]),
        flat_rows(attn_sums[1]),
        flat_rows(ffn_sums[0]),
        flat_rows(ffn_sums[1]),
        flat_rows(ffn_sums[2]),
        flat_rows(ffn_sums[3]),
        small_sums[4],
        flat_rows(ffn_sums[4]),
    )


def solution(mesh):
    placed = (
        P(("dp", "query"), None, None),
        P(("dp", "query"), None),
        P(("dp", "query"), None, None),
        P(),
        P(),
        P(),
        P(),
        P("query", None),
        P("query", None),
        P("query", None),
        P("query", None),
        P("query", None),
        P("query", None),
        P(),
        P("query", None),
        P("dp", "query"),
        P("dp", "query"),
    )
    rows = P(("dp", "query"), None)
    grid = Grid(mesh)
    return jax.shard_map(
        make_shards(grid) if grid.paired() else shards_any,
        mesh=mesh,
        in_specs=placed,
        out_specs=(
            P(("dp", "query"), None, None),
            P(("dp", "query"), None, None),
            P(None, ("dp", "query")),
            P(None, ("dp", "query")),
            P(None, ("dp", "query")),
            P(None, ("dp", "query")),
            rows,
            rows,
            rows,
            rows,
            rows,
            rows,
            P(("dp", "query")),
            rows,
        ),
        check_vma=False,
    )
```

```python
import math

import jax
import jax.numpy as jnp
from jax import lax
from jax.experimental import pallas as pl
from jax.experimental.pallas import tpu as pltpu
from jax.sharding import PartitionSpec as P

D = 1280
HEADS = 20
HEAD_DIM = 64
FF = 5120
ROW_LEN = 512
CELLS_ROW = 4
GENES = 1024
EPSILON = 1e-05
HIGHEST = lax.Precision.HIGHEST
F32 = jnp.float32
BF16 = jnp.bfloat16
VMEM_ASKED = 56 << 20


def layer_norm(values_in, scale_row, offset_row):
    center = values_in - jnp.mean(values_in, axis=-1, keepdims=True)
    spread = jnp.mean(center * center, axis=-1, keepdims=True)
    return center * lax.rsqrt(spread + EPSILON) * scale_row + offset_row


def smooth_gate(values_in):
    return jax.nn.gelu(values_in, approximate=False)


def dot(left, right):
    return jnp.dot(left, right, preferred_element_type=F32)


def dot_rt(left, right):
    return lax.dot_general(left, right, (((1,), (1,)), ((), ())), preferred_element_type=F32)


def dot_lt(left, right):
    return lax.dot_general(left, right, (((0,), (0,)), ((), ())), preferred_element_type=F32)


def cell_layout(lengths):
    cell_ends = jnp.cumsum(lengths, axis=-1, dtype=jnp.int32)
    starts = cell_ends - lengths
    places = jnp.arange(ROW_LEN, dtype=jnp.int32)
    segment = jnp.sum(
        (places[None, :, None] >= cell_ends[:, None, :]).astype(jnp.int32), axis=-1, dtype=jnp.int32
    )
    return (starts, segment)


def cell_mask(segment_row, segment_column, mask):
    same = segment_column[...] == segment_row[...]
    mask[...] = jnp.where(same, 0.0, -1e30)


PAIRS = 2
WIDE = PAIRS * 2 * HEAD_DIM


def attend_kernel(segment_row, segment_column, query, key, value, mixed, totals, mask):
    @pl.when(pl.program_id(1) == 0)
    def _():
        cell_mask(segment_row.at[0], segment_column.at[0], mask)

    ones = jnp.ones((8, ROW_LEN), BF16)
    value_t = value[0].T
    parts = []
    for head in range(2 * PAIRS):
        columns = slice(head * HEAD_DIM, (head + 1) * HEAD_DIM)
        scaled = query[0, :, columns] * jnp.asarray(1.0 / math.sqrt(HEAD_DIM), BF16)
        scores = dot_rt(key[0, :, columns], scaled) + mask[...]
        top = jnp.max(scores, axis=0, keepdims=True)
        weights = jnp.exp(scores - top).astype(BF16)
        left = jnp.concatenate([value_t[columns], ones], axis=0)
        product = dot(left, weights)
        total = product[HEAD_DIM : HEAD_DIM + 1]
        parts.append(product[:HEAD_DIM] / total)
        totals[0, 0, head : head + 1] = top + jnp.log(total)
    mixed[0] = jnp.concatenate(parts, axis=0).T.astype(BF16)


def attend(qkv, segment):
    rows = qkv.shape[0]
    pairs = HEADS // 2 // PAIRS
    wide = WIDE

    def part(offset):
        return pl.BlockSpec((1, ROW_LEN, wide), lambda r, i: (r, 0, offset + i))

    return pl.pallas_call(
        attend_kernel,
        grid=(rows, pairs),
        in_specs=[
            pl.BlockSpec((1, 1, ROW_LEN), lambda r, i: (r, 0, 0)),
            pl.BlockSpec((1, ROW_LEN, 1), lambda r, i: (r, 0, 0)),
            part(0),
            part(pairs),
            part(2 * pairs),
        ],
        out_specs=[
            pl.BlockSpec((1, ROW_LEN, wide), lambda r, i: (r, 0, i)),
            pl.BlockSpec((1, 1, 2 * PAIRS, ROW_LEN), lambda r, i: (r, i, 0, 0)),
        ],
        out_shape=[
            jax.ShapeDtypeStruct((rows, ROW_LEN, pairs * wide), BF16),
            jax.ShapeDtypeStruct((rows, pairs, 2 * PAIRS, ROW_LEN), F32),
        ],
        scratch_shapes=[pltpu.VMEM((ROW_LEN, ROW_LEN), F32)],
        compiler_params=pltpu.CompilerParams(vmem_limit_bytes=VMEM_ASKED),
        cost_estimate=pl.CostEstimate(flops=1, bytes_accessed=1, transcendentals=0),
    )(segment[:, None, :], segment[:, :, None], qkv, qkv, qkv)


def attend_back_kernel(
    segment_row, segment_column, query, key, value, mixed, back, totals, d_qkv, mask
):
    @pl.when(pl.program_id(1) == 0)
    def _():
        cell_mask(segment_row.at[0], segment_column.at[0], mask)

    scale = jnp.asarray(1.0 / math.sqrt(HEAD_DIM), BF16)
    key_t = key[0].T
    product_t = (back[0].astype(F32) * mixed[0].astype(F32)).T
    queries, keys, values = [], [], []
    for head in range(2 * PAIRS):
        columns = slice(head * HEAD_DIM, (head + 1) * HEAD_DIM)
        scaled = query[0, :, columns] * scale
        grad = back[0, :, columns]
        scores = dot_rt(key[0, :, columns], scaled) + mask[...]
        weights = jnp.exp(scores - totals[0, 0, head : head + 1])
        d_weights = dot_rt(value[0, :, columns], grad)
        shift = jnp.sum(product_t[columns], axis=0, keepdims=True)
        d_scores = (weights * (d_weights - shift)).astype(BF16)
        values.append(dot(weights.astype(BF16), grad))
        keys.append(dot(d_scores, scaled))
        queries.append(dot(key_t[columns], d_scores))
    pair = pl.program_id(1)
    parts = [
        jnp.concatenate(queries, axis=0).T * (1.0 / math.sqrt(HEAD_DIM)),
        jnp.concatenate(keys, axis=1),
        jnp.concatenate(values, axis=1),
    ]
    for i, part in enumerate(parts):
        columns = pl.ds(pl.multiple_of(i * D + pair * WIDE, 128), WIDE)
        d_qkv[0, :, columns] = part.astype(BF16)


def attend_back(qkv, segment, mixed, back, totals):
    rows = qkv.shape[0]
    pairs = HEADS // 2 // PAIRS
    wide = WIDE

    def part(offset):
        return pl.BlockSpec((1, ROW_LEN, wide), lambda r, i: (r, 0, offset + i))

    return pl.pallas_call(
        attend_back_kernel,
        grid=(rows, pairs),
        in_specs=[
            pl.BlockSpec((1, 1, ROW_LEN), lambda r, i: (r, 0, 0)),
            pl.BlockSpec((1, ROW_LEN, 1), lambda r, i: (r, 0, 0)),
            part(0),
            part(pairs),
            part(2 * pairs),
            part(0),
            part(0),
            pl.BlockSpec((1, 1, 2 * PAIRS, ROW_LEN), lambda r, i: (r, i, 0, 0)),
        ],
        out_specs=pl.BlockSpec((1, ROW_LEN, 3 * D), lambda r, i: (r, 0, 0)),
        out_shape=jax.ShapeDtypeStruct((rows, ROW_LEN, 3 * D), BF16),
        scratch_shapes=[pltpu.VMEM((ROW_LEN, ROW_LEN), F32)],
        compiler_params=pltpu.CompilerParams(vmem_limit_bytes=VMEM_ASKED),
        cost_estimate=pl.CostEstimate(flops=1, bytes_accessed=1, transcendentals=0),
    )(segment[:, None, :], segment[:, :, None], qkv, qkv, qkv, mixed, back, totals)


CHUNK = 1280
HALF_CHUNK = 640


def part_copies(sources, columns, place, buffer, sems, half_rows, act):
    shard, *parts = sources
    query, outer, inner, core = (place[i] for i in range(4))
    unit = parts[1].shape[0]
    act(
        pltpu.make_async_copy(
            shard.at[:, columns],
            buffer.at[pl.ds(pl.multiple_of(query * half_rows, 16), half_rows), :],
            sems.at[0],
        )
    )
    for side in range(2):
        c = core if side == 0 else 1 - core
        for part in range(4):
            zb, y = outer ^ (part // 2), inner ^ (part % 2)
            row = (1 - query) * half_rows + ((zb * 2 + y) * 2 + c) * unit
            source = parts[2 * side + part // 3]
            act(
                pltpu.make_async_copy(
                    source.at[pl.ds(part % 3 * unit, unit), columns],
                    buffer.at[pl.ds(pl.multiple_of(row, 16), unit), :],
                    sems.at[1 + side * 4 + part],
                )
            )


def chunk_place(step, place, half):
    steps = half // CHUNK
    own = step < steps
    return jnp.where(own, place[0] * steps + step, (1 - place[0]) * steps + step - steps)


def up_copies(sources, place, step, buffer, sems, act):
    half = FF // 2
    start = pl.multiple_of(chunk_place(step, place, half) * CHUNK, 128)
    columns = pl.ds(start, CHUNK)
    part_copies(sources, columns, place, buffer, sems, sources[0].shape[0], act)


def down_copies(sources, place, step, buffer, sems, act):
    shard, *parts = sources
    query, outer, inner, core = (place[i] for i in range(4))
    unit = parts[1].shape[0]
    fold = shard.shape[0] // (8 * unit)
    steps = shard.shape[0] // CHUNK
    own = step < steps
    local = jnp.where(own, step, step - steps)
    size = 2 * fold * unit

    @pl.when(own)
    def _():
        act(
            pltpu.make_async_copy(
                shard.at[pl.ds(pl.multiple_of(local * CHUNK, 16), CHUNK), :], buffer, sems.at[0]
            )
        )

    for piece in range(CHUNK // size):
        at = local * (CHUNK // size) + piece
        part = ((at // 2) ^ outer) * 2 + ((at % 2) ^ inner)
        for corner in range(2):

            @pl.when(jnp.logical_and(jnp.logical_not(own), (part == 3) == (corner == 1)))
            def _():
                row = 0 if corner else pl.multiple_of(part * unit, 16)
                for side in range(2):
                    c = core if side == 0 else 1 - core
                    for k in range(fold):
                        start = pl.multiple_of(piece * size + (c * fold + k) * unit, 16)
                        act(
                            pltpu.make_async_copy(
                                parts[2 * side + corner].at[pl.ds(row, unit), pl.ds(k * D, D)],
                                buffer.at[pl.ds(start, unit), :],
                                sems.at[1 + (piece * 2 + side) * fold + k],
                            )
                        )


def stream(copies, buffer, sems):
    step, steps = pl.program_id(0), pl.num_programs(0)
    slot = lax.rem(step, 2)

    @pl.when(step == 0)
    def _():
        copies(step, buffer.at[slot], sems.at[slot], lambda copy: copy.start())

    @pl.when(step + 1 < steps)
    def _():
        copies(step + 1, buffer.at[1 - slot], sems.at[1 - slot], lambda copy: copy.start())

    copies(step, buffer.at[slot], sems.at[slot], lambda copy: copy.wait())
    return buffer.at[slot]


def gate(values):
    inner = 0.5 * lax.erf(values * math.sqrt(0.5)) + 0.5
    bell = jnp.exp(values * values * -0.5) * (1.0 / math.sqrt(2.0 * math.pi))
    return values * inner, inner + values * bell


def up_kernel(place, second, bias, *refs):
    sources, (active, slope, buffer, sems) = refs[:5], refs[5:]
    weights = stream(lambda *at: up_copies(sources, place, *at), buffer, sems)
    value, rise = gate(dot(second[...], weights[...]) + bias[...])
    active[...] = value.astype(BF16)
    slope[...] = rise.astype(BF16)


def down_kernel(place, active, middle, bias, picker, *refs):
    sources, (out, heads, buffer, sems) = refs[:5], refs[5:]
    weights = stream(lambda *at: down_copies(sources, place, *at), buffer, sems)

    @pl.when(pl.program_id(0) == 0)
    def _():
        out[...] = middle[...] + bias[...]

    out[...] += dot(active[...], weights[...])

    @pl.when(pl.program_id(0) == pl.num_programs(0) - 1)
    def _():
        heads[...] = dot(picker[...], out[...].astype(BF16)).astype(BF16)


def back_kernel(place, branch, slope, *refs):
    up, down = refs[:5], refs[5:10]
    d_hidden, sums, out, buffer, sems, buffer_two, sems_two = refs[10:]
    up_part = stream(lambda *at: up_copies(up, place, *at), buffer, sems)
    down_part = stream(lambda *at: down_copies(down, place, *at), buffer_two, sems_two)

    @pl.when(pl.program_id(0) == 0)
    def _():
        out[...] = jnp.zeros_like(out)

    d_active = dot_rt(branch[...], down_part[...])
    low = (d_active * slope[...].astype(F32)).astype(BF16)
    d_hidden[...] = low
    sums[...] = jnp.sum(low.astype(F32), axis=0, keepdims=True)
    out[...] += dot_rt(low, up_part[...])


def qkv_kernel(place, normed, bias, *refs):
    sources, (out, buffer, sems) = refs[:5], refs[5:]

    def copies(step, *at):
        columns = pl.ds(pl.multiple_of(step * CHUNK, 128), CHUNK)
        part_copies(sources, columns, place, *at[:2], sources[0].shape[0], at[2])

    weights = stream(copies, buffer, sems)
    out[...] = (dot(normed[...], weights[...]) + bias[...]).astype(BF16)


def qkv_back_kernel(place, back, *refs):
    sources, (out, buffer, sems) = refs[:5], refs[5:]

    def copies(step, *at):
        columns = pl.ds(pl.multiple_of(step * CHUNK, 128), CHUNK)
        part_copies(sources, columns, place, *at[:2], sources[0].shape[0], at[2])

    weights = stream(copies, buffer, sems)
    terms = dot_rt(back[...], weights[...])

    @pl.when(pl.program_id(0) == 0)
    def _():
        out[...] = terms

    @pl.when(pl.program_id(0) > 0)
    def _():
        out[...] += terms


def qkv_call(kernel, place, inputs, specs, out_shape, out_spec, columns, weights):
    return pl.pallas_call(
        kernel,
        grid_spec=pltpu.PrefetchScalarGridSpec(
            num_scalar_prefetch=1,
            grid=(columns // CHUNK,),
            in_specs=specs + [pl.BlockSpec(memory_space=pl.ANY)] * 5,
            out_specs=out_spec,
            scratch_shapes=[pltpu.VMEM((2, D, CHUNK), BF16), pltpu.SemaphoreType.DMA((2, 9))],
        ),
        out_shape=out_shape,
        compiler_params=pltpu.CompilerParams(vmem_limit_bytes=VMEM_ASKED),
        cost_estimate=pl.CostEstimate(flops=1, bytes_accessed=1, transcendentals=0),
    )(place, *inputs, *weights)


def project(place, normed, bias, weights):
    count, columns = normed.shape[0], weights[0].shape[1]
    whole = pl.BlockSpec((count, D), lambda j, place: (0, 0))
    row = pl.BlockSpec((1, CHUNK), lambda j, place: (0, j))
    out = pl.BlockSpec((count, CHUNK), lambda j, place: (0, j))
    shape = jax.ShapeDtypeStruct((count, columns), BF16)
    return qkv_call(
        qkv_kernel, place, [normed, bias], [whole, row], shape, out, columns, weights
    )


def project_back(place, back, weights):
    count, columns = back.shape
    whole = pl.BlockSpec((count, D), lambda j, place: (0, 0))
    chunk = pl.BlockSpec((count, CHUNK), lambda j, place: (0, j))
    shape = jax.ShapeDtypeStruct((count, D), F32)
    return qkv_call(qkv_back_kernel, place, [back], [chunk], shape, whole, columns, weights)


def feed_call(kernel, count, inputs, outputs, slots, place, *values, keep=()):
    def at(j, place):
        return chunk_place(j, place, FF // 2)

    specs = {
        "hidden": pl.BlockSpec((count, CHUNK), lambda j, place: (0, at(j, place))),
        "row": pl.BlockSpec((1, CHUNK), lambda j, place: (0, at(j, place))),
        "whole": pl.BlockSpec((count, D), lambda j, place: (0, 0)),
        "any": pl.BlockSpec(memory_space=pl.ANY),
        "vector": pl.BlockSpec((1, D), lambda j, place: (0, 0)),
    }
    shapes = {
        "hidden": jax.ShapeDtypeStruct((count, FF), BF16),
        "row": jax.ShapeDtypeStruct((1, FF), F32),
        "whole": jax.ShapeDtypeStruct((count, D), F32),
    }
    for name, array in keep:
        block = array.shape
        specs[name] = pl.BlockSpec(block, lambda j, place: (0, 0))
        shapes[name] = jax.ShapeDtypeStruct(block, BF16)
    scratch = []
    for slot in slots:
        scratch += [pltpu.VMEM((2, *slot), BF16), pltpu.SemaphoreType.DMA((2, 17))]
    return pl.pallas_call(
        kernel,
        grid_spec=pltpu.PrefetchScalarGridSpec(
            num_scalar_prefetch=1,
            grid=(FF // CHUNK,),
            in_specs=[specs[name] for name in inputs],
            out_specs=[specs[name] for name in outputs],
            scratch_shapes=scratch,
        ),
        out_shape=[shapes[name] for name in outputs],
        compiler_params=pltpu.CompilerParams(vmem_limit_bytes=VMEM_ASKED),
        cost_estimate=pl.CostEstimate(flops=1, bytes_accessed=1, transcendentals=0),
    )(place, *values)


UP_SLOT, DOWN_SLOT = (D, CHUNK), (CHUNK, D)


def feed_up(place, second, bias, up):
    names = ["whole", "row"] + ["any"] * 5
    return feed_call(
        up_kernel, second.shape[0], names, ["hidden", "hidden"], [UP_SLOT], place, second, bias, *up
    )


def feed_down(place, active, middle, bias, picker, down):
    names = ["hidden", "whole", "vector", "picker"] + ["any"] * 5
    heads = jax.ShapeDtypeStruct((picker.shape[0], D), BF16)
    return feed_call(
        down_kernel, active.shape[0], names, ["whole", "heads"], [DOWN_SLOT],
        place, active, middle, bias, picker, *down, keep=(("picker", picker), ("heads", heads)),
    )


def feed_back(place, branch, slope, up, down):
    names = ["whole", "hidden"] + ["any"] * 10
    return feed_call(
        back_kernel, branch.shape[0], names, ["hidden", "row", "whole"], [UP_SLOT, DOWN_SLOT],
        place, branch, slope, *up, *down,
    )


def decode_kernel(mine, other, gene, got, bias, weight, labels, low, sums, by_weight):
    cells = mine.shape[0]
    shape = (cells, gene.shape[0] // cells, gene.shape[1])
    parts = (gene[...].astype(F32) + got[...].astype(F32) + bias[...]).reshape(shape)
    before = (mine[...] + other[...])[:, None, :] + parts
    value, rise = gate(before)
    row = weight[...].astype(F32)[None]
    logits = jnp.sum(value * row, axis=2, keepdims=True)
    slope = jax.nn.sigmoid(logits) - labels[...].astype(F32)
    grad = (rise * (slope * row)).astype(BF16)
    low[...] = grad.reshape(low.shape)
    sums[...] = jnp.sum(grad.astype(F32), axis=1)
    by_weight[...] = jnp.sum(jnp.sum(value * slope, axis=0), axis=0, keepdims=True)


def decode(mine, other, gene, got, bias, weight, labels):
    cells, queries = labels.shape
    return pl.pallas_call(
        decode_kernel,
        out_shape=[
            jax.ShapeDtypeStruct((cells * queries, FF), BF16),
            jax.ShapeDtypeStruct((cells, FF), F32),
            jax.ShapeDtypeStruct((1, FF), F32),
        ],
        compiler_params=pltpu.CompilerParams(vmem_limit_bytes=VMEM_ASKED),
        cost_estimate=pl.CostEstimate(flops=1, bytes_accessed=1, transcendentals=0),
    )(mine, other, gene, got, bias, weight, labels[:, :, None])


def term_kernel(count, mine, units, place, *refs):
    query, _, inner, core = (place[i] for i in range(4))
    inputs = 1 + max(source for unit in units for _, source in unit)
    lefts, rights, (out, blocks), turned = (
        refs[:count],
        refs[count : count + inputs],
        refs[count + inputs : count + inputs + 2],
        refs[count + inputs + 2 :],
    )
    step = pl.program_id(0)
    half = core if mine else 1 - core

    @pl.when(step == 0)
    def _():
        outer = blocks.shape[0] // 8
        size = 2 * outer * blocks.shape[1]
        for left, into in zip(lefts, turned):
            blocks[...] = left[...].astype(F32).T.reshape(blocks.shape)
            for to in range(4):
                first, second = to // 2, to % 2
                x = query ^ jnp.where(half == 0, first, second)
                y = inner ^ jnp.where(half == 0, second, first)
                rows = [
                    blocks[((z * 2 + y) * 2 + c) * 2 + x] for z in range(outer) for c in range(2)
                ]
                into[pl.ds(to * size, size), :] = jnp.concatenate(rows, axis=0).astype(BF16)

    for at, unit in enumerate(units):

        @pl.when(step == at)
        def _():
            for side, (pair, source) in enumerate(unit):
                terms = dot(turned[pair][...], rights[source][...]).astype(BF16)
                columns = slice(side * HALF_CHUNK, (side + 1) * HALF_CHUNK)
                out[:, :, :, columns] = terms.reshape(*out.shape[:3], HALF_CHUNK)


def weight_terms(place, mine, *pairs):
    count, rows = pairs[0][0].shape
    sizes = [right.shape[1] // 2 // HALF_CHUNK for _, right in pairs]
    blocks = [(i, block) for i, size in enumerate(sizes) for block in range(size)]
    plan = [blocks[i : i + 2] for i in range(0, len(blocks), 2)]
    steps = len(plan)
    sources = sorted({(side, unit[side][0]) for unit in plan for side in range(2)})

    def right_spec(side, pair):
        wanted = [unit[side][1] if unit[side][0] == pair else None for unit in plan]
        known = [block for block in wanted if block is not None]

        def at(j, place):
            half = place[3] if mine else 1 - place[3]
            index = known[0]
            for step, block in enumerate(wanted):
                if block is not None:
                    index = jnp.where(j >= step, block, index)
            return (0, half * sizes[pair] + index)

        return pl.BlockSpec((count, HALF_CHUNK), at)

    units = [
        [(pair, sources.index((side, pair))) for side, (pair, _) in enumerate(unit)] for unit in plan
    ]
    left_spec = pl.BlockSpec((count, rows), lambda j, place: (0, 0))
    return pl.pallas_call(
        lambda *refs: term_kernel(len(pairs), mine, units, *refs),
        grid_spec=pltpu.PrefetchScalarGridSpec(
            num_scalar_prefetch=1,
            grid=(steps,),
            in_specs=[left_spec] * len(pairs) + [right_spec(*source) for source in sources],
            out_specs=pl.BlockSpec((2, 2, rows // 4, CHUNK), lambda j, place: (0, 0, 0, j)),
            scratch_shapes=[pltpu.VMEM((32, rows // 32, count), F32)]
            + [pltpu.VMEM((rows, count), BF16)] * len(pairs),
        ),
        out_shape=jax.ShapeDtypeStruct((2, 2, rows // 4, steps * CHUNK), BF16),
        compiler_params=pltpu.CompilerParams(vmem_limit_bytes=VMEM_ASKED),
        cost_estimate=pl.CostEstimate(flops=1, bytes_accessed=1, transcendentals=0),
    )(place, *[left for left, _ in pairs], *[pairs[pair][1] for _, pair in sources])


def tall_kernel(place, left, right, own, sent, blocks, turned):
    query, _, inner, core = (place[i] for i in range(4))
    width = blocks.shape[1]
    blocks[...] = left[...].astype(F32).T.reshape(blocks.shape)
    for to in range(4):
        source = (to % 2) * 2 + to // 2
        turned[pl.ds(to * width, width), :] = blocks[source].astype(BF16)
    terms = dot(turned[...], right[...]).astype(BF16)
    size = terms.shape[1] // 2
    y_place = (pl.program_id(0) % 2) ^ inner
    for half in range(2):
        for x in range(2):
            x_place = x ^ query
            at = (x_place, y_place) if half == 0 else (y_place, x_place)
            value = terms[2 * x * width : 2 * (x + 1) * width, half * size : (half + 1) * size]

            @pl.when(core == half)
            def _():
                own[at[0], at[1], 0] = value

            @pl.when(core != half)
            def _():
                sent[at[0], at[1], 0] = value


def tall_terms(place, left, right, outer):
    count, rows = left.shape
    columns = right.shape[1]
    wide = rows // (2 * outer)
    shape = (2, 2, outer, wide // 2, columns // 2)
    out = pl.BlockSpec(
        (2, 2, 1, wide // 2, columns // 2), lambda j, place: (0, 0, j // 2, 0, 0)
    )
    own, sent = pl.pallas_call(
        tall_kernel,
        grid_spec=pltpu.PrefetchScalarGridSpec(
            num_scalar_prefetch=1,
            grid=(2 * outer,),
            in_specs=[
                pl.BlockSpec((count, wide), lambda j, place: (0, j)),
                pl.BlockSpec((count, columns), lambda j, place: (0, 0)),
            ],
            out_specs=[out, out],
            scratch_shapes=[
                pltpu.VMEM((4, wide // 4, count), F32),
                pltpu.VMEM((wide, count), BF16),
            ],
        ),
        out_shape=[jax.ShapeDtypeStruct(shape, BF16)] * 2,
        compiler_params=pltpu.CompilerParams(vmem_limit_bytes=VMEM_ASKED),
        cost_estimate=pl.CostEstimate(flops=1, bytes_accessed=1, transcendentals=0),
    )(place, left, right)
    flat = (2, 2, outer * wide // 2, columns // 2)
    return own.reshape(flat), sent.reshape(flat)


def small_cost():
    return pl.CostEstimate(flops=1, bytes_accessed=1, transcendentals=0)


def add_kernel(count, *refs):
    ins, outs = refs[: len(refs) - count], refs[len(refs) - count :]
    each = len(ins) // count
    for i, out in enumerate(outs):
        total = ins[i * each][...].astype(F32)
        for other in ins[i * each + 1 : (i + 1) * each]:
            total = total + other[...].astype(F32)
        out[...] = total.astype(BF16)


def add_call(*groups):
    first, _ = groups[0][0]
    rows, columns = first.shape[-2:]
    steps = 2
    size = rows // steps
    specs, arrays = [], []
    for group in groups:
        for array, at in group:
            lead = (None,) * len(at)
            specs.append(
                pl.BlockSpec((*lead, size, columns), lambda r, at=at: (*at, r, 0))
            )
            arrays.append(array)
    out = pl.BlockSpec((size, columns), lambda r: (r, 0))
    shape = jax.ShapeDtypeStruct((rows, columns), BF16)
    return pl.pallas_call(
        lambda *refs: add_kernel(len(groups), *refs),
        grid=(steps,),
        in_specs=specs,
        out_specs=[out] * len(groups),
        out_shape=[shape] * len(groups),
        compiler_params=pltpu.CompilerParams(vmem_limit_bytes=VMEM_ASKED),
        cost_estimate=small_cost(),
    )(*arrays)


def out_kernel(mixed, weight, tokens, bias, gain, shift, middle, second):
    values = tokens[...].astype(F32) + dot(mixed[...], weight[...]) + bias[...]
    middle[...] = values
    second[...] = layer_norm(values, gain[...], shift[...]).astype(BF16)


def attend_out(mixed, weight, tokens, bias, gain, shift):
    count = tokens.shape[0]
    size = 256
    row = pl.BlockSpec((size, D), lambda r: (r, 0))
    vector = pl.BlockSpec((1, D), lambda r: (0, 0))
    whole = pl.BlockSpec((D, D), lambda r: (0, 0))
    return pl.pallas_call(
        out_kernel,
        grid=(count // size,),
        in_specs=[row, whole, row, vector, vector, vector],
        out_specs=[row, row],
        out_shape=[
            jax.ShapeDtypeStruct((count, D), F32),
            jax.ShapeDtypeStruct((count, D), BF16),
        ],
        compiler_params=pltpu.CompilerParams(vmem_limit_bytes=VMEM_ASKED),
        cost_estimate=small_cost(),
    )(mixed, weight, tokens, bias[None, :], gain[None, :], shift[None, :])


def spread_kernel(left, right, out):
    out[...] = dot(left[...], right[...]).astype(BF16)


def spread(left, right):
    count, depth = left.shape
    columns = right.shape[1]
    return pl.pallas_call(
        spread_kernel,
        grid=(columns // CHUNK,),
        in_specs=[
            pl.BlockSpec((count, depth), lambda j: (0, 0)),
            pl.BlockSpec((depth, CHUNK), lambda j: (0, j)),
        ],
        out_specs=pl.BlockSpec((count, CHUNK), lambda j: (0, j)),
        out_shape=jax.ShapeDtypeStruct((count, columns), BF16),
        compiler_params=pltpu.CompilerParams(vmem_limit_bytes=VMEM_ASKED),
        cost_estimate=small_cost(),
    )(left, right)


def gather_kernel(left, right, out, total):
    terms = dot_rt(left[...], right[...])
    step = pl.program_id(0)

    @pl.when(step == 0)
    def _():
        total[...] = terms

    @pl.when(step > 0)
    def _():
        total[...] += terms

    @pl.when(step == pl.num_programs(0) - 1)
    def _():
        out[...] = total[...].astype(BF16)


def gather(left, right):
    count, columns = left.shape
    rows = right.shape[0]
    return pl.pallas_call(
        gather_kernel,
        grid=(columns // CHUNK,),
        in_specs=[
            pl.BlockSpec((count, CHUNK), lambda j: (0, j)),
            pl.BlockSpec((rows, CHUNK), lambda j: (0, j)),
        ],
        out_specs=pl.BlockSpec((count, rows), lambda j: (0, 0)),
        out_shape=jax.ShapeDtypeStruct((count, rows), BF16),
        scratch_shapes=[pltpu.VMEM((count, rows), F32)],
        compiler_params=pltpu.CompilerParams(vmem_limit_bytes=VMEM_ASKED),
        cost_estimate=small_cost(),
    )(left, right)


def norm_terms(values, grad, gain):
    center = values - jnp.mean(values, axis=-1, keepdims=True)
    spread = jnp.mean(center * center, axis=-1, keepdims=True)
    rise = lax.rsqrt(spread + EPSILON)
    unit = center * rise
    scaled = grad * gain
    first = jnp.mean(scaled, axis=-1, keepdims=True)
    second = jnp.mean(scaled * unit, axis=-1, keepdims=True)
    return (
        (scaled - first - unit * second) * rise,
        jnp.sum(grad * unit, axis=0, keepdims=True),
        jnp.sum(grad, axis=0, keepdims=True),
    )


def out_back_kernel(
    grad, middle, gain, flat, weight, grad_middle, low, back, gain_sum, shift_sum
):
    part, by_gain, by_shift = norm_terms(middle[...], grad[...], gain[...])
    total = flat[...] + part
    grad_middle[...] = total
    low[...] = total.astype(BF16)
    back[...] = dot_rt(total.astype(BF16), weight[...]).astype(BF16)

    @pl.when(pl.program_id(0) == 0)
    def _():
        gain_sum[...] = jnp.zeros_like(gain_sum)
        shift_sum[...] = jnp.zeros_like(shift_sum)

    gain_sum[...] += by_gain
    shift_sum[...] += by_shift


def attend_out_back(grad, middle, gain, flat, weight):
    count = grad.shape[0]
    size = 256
    row = pl.BlockSpec((size, D), lambda r: (r, 0))
    vector = pl.BlockSpec((1, D), lambda r: (0, 0))
    whole = pl.BlockSpec((D, D), lambda r: (0, 0))
    wide = jax.ShapeDtypeStruct((count, D), F32)
    low = jax.ShapeDtypeStruct((count, D), BF16)
    return pl.pallas_call(
        out_back_kernel,
        grid=(count // size,),
        in_specs=[row, row, vector, row, whole],
        out_specs=[row, row, row, vector, vector],
        out_shape=[wide, low, low] + [jax.ShapeDtypeStruct((1, D), F32)] * 2,
        compiler_params=pltpu.CompilerParams(vmem_limit_bytes=VMEM_ASKED),
        cost_estimate=small_cost(),
    )(grad, middle, gain[None, :], flat, weight)


def tokens_back_kernel(grad, tokens, gain, flat, out, gain_sum, shift_sum):
    part, by_gain, by_shift = norm_terms(tokens[...].astype(F32), grad[...], gain[...])
    out[...] = flat[...] + part

    @pl.when(pl.program_id(0) == 0)
    def _():
        gain_sum[...] = jnp.zeros_like(gain_sum)
        shift_sum[...] = jnp.zeros_like(shift_sum)

    gain_sum[...] += by_gain
    shift_sum[...] += by_shift


def tokens_back(grad, tokens, gain, flat):
    count = grad.shape[0]
    size = 256
    row = pl.BlockSpec((size, D), lambda r: (r, 0))
    vector = pl.BlockSpec((1, D), lambda r: (0, 0))
    return pl.pallas_call(
        tokens_back_kernel,
        grid=(count // size,),
        in_specs=[row, row, vector, row],
        out_specs=[row, vector, vector],
        out_shape=[jax.ShapeDtypeStruct((count, D), F32)]
        + [jax.ShapeDtypeStruct((1, D), F32)] * 2,
        compiler_params=pltpu.CompilerParams(vmem_limit_bytes=VMEM_ASKED),
        cost_estimate=small_cost(),
    )(grad, tokens, gain[None, :], flat)


def assemble_kernel(pieces, width, count, place_ref, *refs):
    sources, full, sems = refs[:count], refs[count], refs[count + 1]
    step = pl.program_id(0)
    copies = []
    for i, (source, row, rows, column) in enumerate(pieces):
        start = pl.multiple_of(place_ref[i], 16)
        columns = pl.ds(pl.multiple_of(column + step * width, 128), width)
        copies.append(
            pltpu.make_async_copy(
                sources[source].at[pl.ds(row, rows), columns],
                full.at[pl.ds(start, rows), :],
                sems.at[i],
            )
        )
    for copy in copies:
        copy.start()
    for copy in copies:
        copy.wait()


def assemble(sources, pieces, places, shape, width):
    count = len(sources)
    rows, columns = shape
    return pl.pallas_call(
        lambda *refs: assemble_kernel(pieces, width, count, *refs),
        grid=(columns // width,),
        out_shape=jax.ShapeDtypeStruct(shape, BF16),
        in_specs=[pl.BlockSpec(memory_space=pltpu.SMEM)]
        + [pl.BlockSpec(memory_space=pl.ANY)] * count,
        out_specs=pl.BlockSpec((rows, width), lambda j: (0, j)),
        scratch_shapes=[pltpu.SemaphoreType.DMA((len(pieces),))],
        compiler_params=pltpu.CompilerParams(vmem_limit_bytes=32 << 20),
        cost_estimate=pl.CostEstimate(flops=1, bytes_accessed=1, transcendentals=0),
    )(jnp.stack(places).astype(jnp.int32), *sources)


def sync(*values):
    return lax.optimization_barrier(values)


def tie(value, *others):
    return lax.optimization_barrier((value, others))[0] if others else value


class Grid:
    def __init__(self, mesh):
        dp, query = mesh.shape["dp"], mesh.shape["query"]
        core = 2 if dp % 2 == 0 else 1
        rest = dp // core
        outer = 4 if rest % 4 == 0 else rest
        inner = rest // outer
        self.dp, self.query = dp, query
        self.size = {"z": outer, "y": inner, "c": core, "x": query}
        self.stride = {"z": inner * core, "y": core, "c": 1}
        self.order = ["z", "y", "c", "x"]

    def paired(self):
        size = self.size
        pairs = size["x"] == 2 and size["y"] == 2 and size["c"] == 2
        return pairs and size["z"] == 4 and D % (self.dp * self.query * 8) == 0

    def place(self, axis):
        if axis == "zb":
            return self.place("z") % 2
        if axis == "zh":
            return self.place("z") // 2
        if axis == "x":
            return lax.axis_index("query")
        return (lax.axis_index("dp") // self.stride[axis]) % self.size[axis]

    def partner(self, axis, at, step):
        size = self.size[axis]
        return at ^ step if size & (size - 1) == 0 else (at + step) % size

    def sender(self, axis, at, step):
        size = self.size[axis]
        return at ^ step if size & (size - 1) == 0 else (at + size - step) % size

    def hop(self, value, axis, step=1):
        if axis == "x":
            pairs = [(i, self.partner("x", i, step)) for i in range(self.query)]
            return lax.ppermute(value, "query", pairs)
        stride, size = self.stride[axis], self.size[axis]
        pairs = []
        for i in range(self.dp):
            at = (i // stride) % size
            pairs.append((i, i + (self.partner(axis, at, step) - at) * stride))
        return lax.ppermute(value, "dp", pairs)

    def turn_hop(self, value, turn):
        pairs = []
        for i in range(self.dp):
            core = i % 2
            y = (i // self.stride["y"]) % 2
            for x in range(2):
                if core == turn:
                    to = i * 2 + 1 - x
                else:
                    to = (i + (1 - 2 * y) * self.stride["y"]) * 2 + x
                pairs.append((i * 2 + x, to))
        return lax.ppermute(value, ("dp", "query"), pairs)

    def share(self, value, axis=0, after=()):
        if self.query == 1:
            return value
        if self.query != 2:
            return lax.all_gather(value, "query", axis=axis, tiled=True)
        other = tie(self.hop(value, "x"), *after)
        first = lax.axis_index("query") == 0
        return jnp.concatenate(
            [jnp.where(first, value, other), jnp.where(first, other, value)], axis=axis
        )

    def joined_along(self, mine, other, axis):
        first = self.place(axis) == 0
        return jnp.concatenate(
            [jnp.where(first, mine, other), jnp.where(first, other, mine)], axis=0
        )

    def cut_half(self, value, axis):
        half = value.shape[1] // 2
        first = self.place(axis) == 0
        left, right = value[:, :half], value[:, half:]
        return jnp.where(first, left, right), jnp.where(first, right, left)

    def cut_fold(self, value, step):
        bits = value.reshape(value.shape[0] // 2, 2, *value.shape[1:])
        me = self.place("z") // step % 2
        return (
            lax.dynamic_index_in_dim(bits, me, axis=1, keepdims=False),
            lax.dynamic_index_in_dim(bits, 1 - me, axis=1, keepdims=False),
        )

    def joined(self, mine, other, axis=0):
        first = lax.axis_index("query") == 0
        return jnp.concatenate(
            [jnp.where(first, mine, other), jnp.where(first, other, mine)], axis=axis
        )

    def total(self, value):
        if self.query == 1:
            return value
        if self.query != 2:
            return lax.psum(value, "query")
        return value + self.hop(value, "x")

    def cut_step(self, value, axis, dim):
        me = self.place(axis)
        return (
            lax.dynamic_index_in_dim(value, me, axis=dim, keepdims=False),
            lax.dynamic_index_in_dim(value, 1 - me, axis=dim, keepdims=False),
        )

    def cut_columns(self, terms):
        half = terms.shape[1] // 2
        first = self.place("c") == 0
        left, right = terms[:, :half], terms[:, half:]
        return jnp.where(first, left, right), jnp.where(first, right, left)

    def trade(self, value, axis, dim, column):
        mine, other = self.cut_step(value, axis, dim)
        got = self.hop(other, axis) if axis != "zb" else self.hop(other, "z")
        first = self.place(axis) == 0
        return jnp.concatenate(
            [jnp.where(first, mine, got), jnp.where(first, got, mine)], axis=column
        )

    def join_columns(self, value):
        value = value.reshape(2, -1, value.shape[-1])
        mine, other = self.cut_step(value, "c", 0)
        got = self.hop(other, "c")
        first = self.place("c") == 0
        return jnp.concatenate(
            [jnp.where(first, mine, got), jnp.where(first, got, mine)], axis=1
        )

    def scatter_step(self, value, axis, dim, kind):
        size = self.size[axis]
        me = self.place(axis)

        def part(index):
            return lax.dynamic_index_in_dim(value, index, axis=dim, keepdims=False)

        if size == 1:
            return part(0)
        sent = [
            self.hop(part(self.partner(axis, me, step)), axis, step) for step in range(1, size)
        ]
        total = part(me).astype(F32)
        for received in sent:
            total = total + received.astype(F32)
        return total.astype(kind)

    def scatter(self, value, order, kind=BF16):
        dims = [axis for axis in self.order if axis in order]
        for axis in order:
            dim = dims.index(axis)
            value = self.scatter_step(value, axis, dim, kind)
            dims.pop(dim)
        return value

    def scatter_z(self, value):
        stride, size = self.stride["z"], self.size["z"]
        groups = [[k * stride + i for k in range(size)] for i in range(stride)]
        return lax.psum_scatter(
            value, "dp", scatter_dimension=0, axis_index_groups=groups, tiled=True
        )

    def scatter_high(self, value):
        stride, size = self.stride["z"], self.size["z"]
        groups = [
            [(high * 2 + low) * stride + i for high in range(size // 2)]
            for low in range(2)
            for i in range(stride)
        ]
        return lax.psum_scatter(
            value, "dp", scatter_dimension=0, axis_index_groups=groups, tiled=True
        )

    def blocks(self, value):
        shape = [self.size[axis] for axis in self.order]
        rows = value.shape[0] // math.prod(shape)
        return value.reshape(*shape, rows, *value.shape[1:])

    def own_columns(self, value):
        width = value.shape[1] // (self.dp * self.query)
        shaped = value.reshape(value.shape[0], self.dp, self.query, width)
        mine = lax.dynamic_index_in_dim(shaped, self.place("x"), axis=2, keepdims=False)
        return mine.reshape(value.shape[0], self.dp * width)

    def part_of(self, shards):
        zb, y, c = self.place("z") % 2, self.place("y"), self.place("c")
        unit = min(shard.shape[0] for shard in shards) // 8
        mine = (zb * 2 + y) * 2 + c
        columns = []
        for shard in shards:
            fold = shard.shape[0] // (8 * unit)
            for k in range(fold):
                columns.append(
                    lax.dynamic_slice_in_dim(shard, (mine * fold + k) * unit, unit, 0)
                )
        return jnp.concatenate(columns, axis=1) if len(columns) > 1 else columns[0]

    def sides_of(self, first, after=()):
        first = tie(first, *after)
        return [self.hop(first, "y"), self.hop(first, "z")]

    def corners_of(self, sides, after=()):
        by_y, by_z = tie(sides, *after)
        cut = by_y.shape[0] // 2 // 16 * 16
        sent = (by_z[:cut], by_y[cut:])
        return sent, [self.hop(sent[0], "y"), self.hop(sent[1], "z")]

    def corner_cuts(self, sides):
        by_y, by_z = sides
        cut = by_y.shape[0] // 2 // 16 * 16
        return [by_z[:cut], by_y[cut:]]

    def most_of(self, first, sides, *after):
        near = jnp.concatenate([tie(first, *after), *sides], axis=0)
        return near, self.hop(near, "c")

    def corner_of(self, corners, after=()):
        near = jnp.concatenate(tie(corners, *after), axis=0)
        return near, self.hop(near, "c")

    def join(self, shard, parts, column):
        zb, y, c, x = self.place("z") % 2, self.place("y"), self.place("c"), self.place("x")
        rows, width = shard.shape
        unit = rows // 8
        pieces, places = [(0, 0, rows, 0)], [x * rows]
        for side in range(2):
            c_ = c if side == 0 else 1 - c
            for part in range(4):
                place = ((zb ^ (part // 2)) * 2 + (y ^ (part % 2))) * 2 + c_
                pieces.append((1 + 2 * side + part // 3, part % 3 * unit, unit, column))
                places.append((1 - x) * rows + place * unit)
        return assemble([shard, *parts], pieces, places, (2 * rows, width), 640)

    def places(self):
        return jnp.stack(
            [self.place("x"), self.place("z") % 2, self.place("y"), self.place("c")]
        ).astype(jnp.int32)


def added(*values):
    total = values[0].astype(F32)
    for value in values[1:]:
        total = total + value.astype(F32)
    return total.astype(BF16)


def added_wide(*values):
    total = values[0].astype(F32)
    for value in values[1:]:
        total = total + value.astype(F32)
    return total


class Sums:
    def __init__(self, grid):
        self.grid = grid

    def core(self, *after):
        self.got = self.grid.hop(tie(self.sent, *after), "c")

    def add_first(self, *after):
        own, got = tie((self.own, self.got), *after)
        self.parts = add_call(*[[(own, (1, k)), (got, (1, k))] for k in (1, 0)])

    def go_first(self, part):
        return self.grid.turn_hop(self.parts[part], 0)

    def add_second(self, one, *after):
        own, got, one = tie((self.own, self.got, one), *after)
        (self.two_in,) = add_call([(own, (0, 1)), (got, (0, 1)), (one, ())])

    def go_second(self):
        return self.grid.turn_hop(self.two_in, 1)

    def add_last(self, one, two, *after):
        own, got, one = tie((self.own, self.got, one), *after)
        (whole,) = add_call([(own, (0, 0)), (got, (0, 0)), (one, ()), (two, ())])
        size = self.grid.size["z"]
        self.last_in = whole.reshape(size, whole.shape[0] // size, whole.shape[1])

    def last(self):
        self.sum = self.grid.scatter_z(self.last_in)

    def result(self, *after):
        value = tie(self.sum, *after)[0]
        value = value.reshape(2, value.shape[0] // 2, value.shape[1])
        mine, other = self.grid.cut_step(value, "c", 0)
        got = self.grid.hop(other, "c")
        first = self.grid.place("c") == 0
        return [
            jnp.where(first, mine, got).astype(F32),
            jnp.where(first, got, mine).astype(F32),
        ]


def make_shards(grid):
    def shards(
        tokens,
        cell_lengths,
        out_cotangent,
        ln_gains,
        ln_biases,
        proj_biases,
        ff_biases,
        w_qkv,
        w_out,
        w_up,
        w_down,
        dec_cell,
        dec_gene,
        dec_out,
        gene_table,
        query_ids,
        labels,
    ):
        row_count = tokens.shape[0]
        token_count = row_count * ROW_LEN
        dp_count, query_count = grid.dp, grid.query
        place = lax.axis_index("query")
        starts, segment = cell_layout(cell_lengths)
        local_cells = row_count * CELLS_ROW
        pair_cells, local_queries = query_ids.shape
        pairs = pair_cells * local_queries
        half_width = D // query_count

        row_tokens = tokens.reshape(token_count, D)
        where = grid.places()
        ids = grid.share(query_ids.reshape(1, pairs)).reshape(query_count * pairs)
        qkv_first = grid.hop(grid.part_of([w_qkv]), "x")
        normed_low = layer_norm(row_tokens.astype(F32), ln_gains[0], ln_biases[0]).astype(BF16)
        table_rows = gene_table.shape[0]
        local_ids = ids - place * table_rows
        held = (local_ids[:, None] == jnp.arange(table_rows, dtype=jnp.int32)[None, :]).astype(BF16)
        gene_found = dot(held, gene_table).astype(BF16)
        up_part = grid.part_of([w_up, w_out])
        down_part = grid.part_of([w_down])
        qkv_first, normed_low, gene_found, up_part, down_part = sync(
            qkv_first, normed_low, gene_found, up_part, down_part
        )
        up_first = grid.hop(up_part, "x")
        qkv_sides = sync(*grid.sides_of(qkv_first))
        qkv_sent = sync(*grid.corner_cuts(qkv_sides))
        qkv_corners = [grid.hop(qkv_sent[0], "y"), grid.hop(qkv_sent[1], "z")]
        qkv_near, qkv_far = grid.most_of(qkv_first, qkv_sides, qkv_sent)
        *qkv_corners, qkv_near, up_first = sync(*qkv_corners, qkv_near, up_first)
        up_sides = grid.sides_of(up_first)
        qkv_end, qkv_end_far = grid.corner_of(qkv_corners)
        qkv_end_far, qkv_far, up_first = sync(qkv_end_far, qkv_far, up_first)
        gene_hop = grid.hop(gene_found, "x")
        down_first = grid.hop(tie(down_part, up_first), "x")
        qkv_weights = (w_qkv, qkv_near, qkv_end, qkv_far, qkv_end_far)
        zeroes = jnp.zeros((D,), F32)
        qkv_bias = jnp.concatenate([proj_biases[0], zeroes, proj_biases[1]])
        qkv_low = project(where, normed_low, qkv_bias[None, :], qkv_weights)
        qkv_rows = qkv_low.reshape(row_count, ROW_LEN, 3 * D)
        mixed_rows, log_totals = attend(qkv_rows, segment)
        mixed_rows, *up_sides, down_first, gene_hop = sync(mixed_rows, *up_sides, down_first, gene_hop)
        up_sent = sync(*grid.corner_cuts(up_sides))
        up_corners = [grid.hop(up_sent[0], "y"), grid.hop(up_sent[1], "z")]
        up_near, up_far = grid.most_of(up_first, up_sides, up_sent)
        down_sides = grid.sides_of(down_first, (up_near,))
        mixed_low = mixed_rows.reshape(token_count, D)
        gene_rows = added(gene_found, gene_hop) if query_count == 2 else gene_found
        gene_half = lax.dynamic_slice_in_dim(gene_rows, place * half_width, half_width, 1)
        gene_partial = spread(tie(gene_half, up_near), dec_gene).reshape(query_count, pairs, FF)
        gene_mine, gene_sent = grid.cut_step(gene_partial, "x", 0)
        *up_corners, up_far, gene_sent = sync(*up_corners, up_far, gene_sent)
        up_end, up_end_far = grid.corner_of(up_corners)
        up_parts = (up_near, up_end, up_far, up_end_far)
        up_weights = (w_up, *up_parts)
        full_out = grid.join(w_out, up_parts, FF)
        middle, second_low = attend_out(
            mixed_low, full_out, row_tokens, proj_biases[2], ln_gains[1], ln_biases[1]
        )
        second_low, down_first, *down_sides = sync(second_low, down_first, *down_sides)
        down_sent = sync(*grid.corner_cuts(down_sides))
        down_corners = [grid.hop(down_sent[0], "y"), grid.hop(down_sent[1], "z")]
        down_near, down_far = grid.most_of(down_first, down_sides, down_sent)
        gene_got = grid.hop(gene_sent, "x")
        gene_pair = grid.hop(gene_rows, "z")
        active_low, slope = feed_up(
            where, tie(second_low, down_near), ff_biases[0][None, :], up_weights
        )
        active_low, slope, *down_corners, down_far, gene_got, gene_pair = sync(
            active_low, slope, *down_corners, down_far, gene_got, gene_pair
        )
        down_end, down_end_far = grid.corner_of(down_corners)
        down_weights = (w_down, down_near, down_end, down_far, down_end_far)
        places = jnp.arange(ROW_LEN, dtype=jnp.int32)
        picker = (places[None, :, None] == starts[:, None, :]).astype(F32)
        rows_apart = jnp.arange(row_count)
        choice = jnp.where(
            rows_apart[:, None, None, None] == rows_apart[None, None, :, None],
            picker.transpose(0, 2, 1)[:, :, None, :],
            0,
        ).reshape(local_cells, token_count).astype(BF16)
        encoded, heads_low = feed_down(
            where, active_low, middle, proj_biases[3:], choice, down_weights
        )
        encoded_rows = encoded.reshape(row_count, ROW_LEN, D)
        cell_heads = grid.share(heads_low)
        heads_half = lax.dynamic_slice_in_dim(cell_heads, place * half_width, half_width, 1)
        cell_half = dot(heads_half, dec_cell)
        cell_hop = grid.hop(cell_half, "x") if query_count == 2 else cell_half
        before_low, before_sums, grad_logit = decode(
            cell_half, cell_hop, gene_mine, gene_got, ff_biases[1][None, :], dec_out[None, :], labels
        )
        before_low = before_low.reshape(pair_cells, local_queries, FF)
        cell_total = grid.total(before_sums).astype(BF16)
        heads_part = dot_rt(cell_total, dec_cell).astype(BF16)
        heads_all = grid.share(heads_part, axis=1)
        heads_back = lax.dynamic_slice_in_dim(
            heads_all, place * local_cells, local_cells, 0
        ).astype(F32)
        grad_encoded = out_cotangent.astype(F32) + jnp.sum(
            picker[:, :, :, None] * heads_back.reshape(row_count, 1, CELLS_ROW, D), axis=2
        )
        grad_flat = grad_encoded.reshape(token_count, D)
        branch_low = grad_flat.astype(BF16)
        branch_low, before_low = sync(branch_low, before_low)
        before_hop = grid.hop(before_low, "x") if query_count == 2 else before_low
        gathered = lax.all_gather(
            jnp.concatenate([cell_heads, cell_total], axis=1), "dp", axis=0, tiled=True
        )
        down_sums = Sums(grid)
        down_sums.own, down_sums.sent = tall_terms(where, active_low, branch_low, grid.size["z"])
        down_sums.own, down_sums.sent, before_hop = sync(down_sums.own, down_sums.sent, before_hop)
        down_sums.core()
        before_all = grid.joined(before_low, before_hop).reshape(query_count * pairs, FF)
        before_mine, before_sent = grid.cut_half(before_all, "zb")
        before_got = grid.hop(before_sent, "z")
        hidden_low, up_bias_sums, grad_second = feed_back(
            where, tie(branch_low, down_sums.sent, before_sent), slope, up_weights, down_weights
        )
        hidden_low, grad_second, before_got, down_sums.got = sync(
            hidden_low, grad_second, before_got, down_sums.got
        )
        down_sums.add_first()
        gene_wide = grid.joined_along(gene_rows, gene_pair, "zb")
        before_wide = grid.joined_along(before_mine, before_got, "zb")
        gene_left = grid.own_columns(gene_wide)
        gene_half = before_wide.shape[1] // 2
        core = grid.place("c")
        gene_mine, gene_sent = [
            dot_lt(
                gene_left,
                lax.dynamic_slice_in_dim(before_wide, at * gene_half, gene_half, 1),
            ).astype(BF16)
            for at in (core, 1 - core)
        ]
        *down_sums.parts, gene_sent, gene_mine = sync(*down_sums.parts, gene_sent, gene_mine)
        one = down_sums.go_first(0)
        gene_got = grid.hop(gene_sent, "c")
        grad_middle, attn_low, mixed_back, grad_gain_two, grad_shift_two = attend_out_back(
            tie(grad_second, down_sums.parts), middle, ln_gains[1], grad_flat, full_out
        )
        up_sums = Sums(grid)
        up_sums.sent = weight_terms(where, False, (second_low, tie(hidden_low, mixed_back)))
        up_sums.sent, one, gene_got, gathered = sync(up_sums.sent, one, gene_got, gathered)
        one_more = down_sums.go_first(1)
        down_sums.add_second(one)
        up_sums.core()
        two = down_sums.go_second()
        up_sums.own = weight_terms(
            where, True, (second_low, tie(hidden_low, up_sums.sent, down_sums.two_in))
        )
        (gene_sum,) = add_call([(gene_mine, ()), (tie(gene_got, up_sums.own), ())])
        mixed_back, up_sums.own, up_sums.got, gene_sum = sync(
            mixed_back, up_sums.own, up_sums.got, gene_sum
        )
        gene_sum = grid.scatter_high(gene_sum)
        up_sums.add_first()
        *up_sums.parts, mixed_back = sync(*up_sums.parts, mixed_back)
        up_one, up_more = up_sums.go_first(0), up_sums.go_first(1)
        qkv_back = attend_back(
            qkv_rows,
            segment,
            mixed_rows,
            mixed_back.reshape(row_count, ROW_LEN, D),
            log_totals,
        )
        qkv_back, one_more, two = sync(qkv_back, one_more, two)
        down_sums.add_last(one_more, two)
        down_sums.last()
        qkv_back_low = qkv_back.reshape(token_count, 3 * D)
        attn_sums = Sums(grid)
        attn_sums.sent = weight_terms(
            where,
            False,
            (normed_low, tie(qkv_back_low, down_sums.last_in)),
            (mixed_low, attn_low),
        )
        attn_sums.sent, qkv_back_low, up_one, gene_sum = sync(
            attn_sums.sent, qkv_back_low, up_one, gene_sum
        )
        gene_sum = gene_sum.reshape(2, grid.size["y"], -1, gene_sum.shape[-1])
        gene_mine, gene_sent = grid.cut_step(gene_sum, "y", 1)
        up_sums.add_second(up_one, gene_sent)
        up_two = up_sums.go_second()
        attn_sums.core()
        gene_got = grid.hop(gene_sent, "y")
        attn_sums.own = weight_terms(
            where, True, (normed_low, tie(qkv_back_low, up_sums.two_in)), (mixed_low, attn_low)
        )
        attn_sums.own, attn_sums.got = sync(attn_sums.own, attn_sums.got)
        attn_sums.add_first()
        attn_sums.parts = sync(*attn_sums.parts)
        one, one_more = attn_sums.go_first(0), attn_sums.go_first(1)
        grad_normed = project_back(where, tie(qkv_back_low, attn_sums.parts), qkv_weights)
        grad_normed, up_more, up_two, gene_got, down_sums.sum = sync(
            grad_normed, up_more, up_two, gene_got, down_sums.sum
        )
        up_sums.add_last(up_more, up_two)
        up_sums.last()
        grad_tokens, grad_gain_one, grad_shift_one = tokens_back(
            tie(grad_normed, up_sums.last_in), row_tokens, ln_gains[0], grad_middle
        )
        gene_sum = added(tie(gene_mine, grad_tokens), gene_got).reshape(2, 2, -1, gene_mine.shape[-1])
        genes_part = gather(tie(before_all, grad_tokens), dec_gene)
        genes_part, gene_sum, one = sync(genes_part, gene_sum, one)
        attn_sums.add_second(one)
        two = attn_sums.go_second()

        gene_sum, genes_part = tie((gene_sum, genes_part), attn_sums.two_in)
        gene_sum = grid.trade(gene_sum, "c", 1, 2)
        grad_tokens = grad_tokens.reshape(row_count, ROW_LEN, D)
        choose = (
            tie(ids, genes_part)[:, None] == jnp.arange(GENES, dtype=jnp.int32)[None, :]
        ).astype(BF16)
        table_terms = dot_lt(choose, genes_part).astype(BF16)
        shape = [grid.size[axis] for axis in "zycx"]
        table_terms = table_terms.reshape(*shape, -1, half_width)
        table_mine, table_sent = grid.cut_step(table_terms, "c", 2)
        table_sum = added(table_mine, grid.hop(table_sent, "c"))
        late_ties = (qkv_back_low, attn_low, branch_low, up_bias_sums, before_sums)
        qkv_late, attn_late, branch_late, up_bias_sums, sums_late = tie(late_ties, table_sent)
        grad_up_bias = up_bias_sums[0]
        bias_sums = jnp.sum(qkv_late, axis=0, dtype=F32)
        grad_attn_bias = jnp.sum(attn_late, axis=0, dtype=F32)
        grad_out_bias = jnp.sum(branch_late, axis=0, dtype=F32)
        grad_dec_bias = jnp.sum(sums_late, axis=0)
        owners = dp_count * query_count

        def owned_cols(values):
            return values.reshape(-1, owners, values.shape[-1] // owners).transpose(1, 0, 2).reshape(owners, -1)

        small = [
            jnp.concatenate([grad_gain_one, grad_gain_two]),
            jnp.concatenate([grad_shift_one, grad_shift_two]),
            jnp.stack([bias_sums[:D], bias_sums[2 * D :], grad_attn_bias, grad_out_bias]),
            jnp.stack([grad_up_bias, grad_dec_bias]),
            grad_logit,
        ]
        flat = [owned_cols(value) for value in small]
        sums = grid.scatter_step(grid.blocks(jnp.concatenate(flat, axis=1)), "c", 2, F32)
        sums, table_sum, gene_sum, one_more, two, up_sums.sum = sync(
            sums, table_sum, gene_sum, one_more, two, up_sums.sum
        )
        attn_sums.add_last(one_more, two)
        attn_sums.last()

        sums, table_sum, gene_sum = tie((sums, table_sum, gene_sum), attn_sums.last_in)
        sums = grid.scatter_step(sums, "x", 2, F32)
        table_sum = grid.scatter_step(table_sum, "y", 1, BF16)
        grad_gene = grid.trade(gene_sum, "zb", 0, 1).astype(F32)
        up_result, down_result = up_sums.result(attn_sums.last_in), down_sums.result(attn_sums.last_in)
        sums, table_sum, grad_gene, up_result, down_result = sync(
            sums, table_sum, grad_gene, up_result, down_result
        )
        sums = grid.scatter_step(sums, "y", 1, F32)
        table_mine, table_sent = grid.cut_fold(table_sum, 1)
        table_sum = added(table_mine, grid.hop(table_sent, "z", 1))
        sums, table_sum = sync(sums, table_sum)
        summed = grid.scatter_step(sums, "z", 0, F32).reshape(-1)
        table_mine, table_sent = grid.cut_fold(table_sum, 2)
        table_sum = added(table_mine, grid.hop(table_sent, "z", 2))[0]
        grad_table = grid.trade(table_sum, "x", 0, 1).astype(F32)
        all_heads, all_cells = jnp.split(tie(gathered, attn_sums.last_in), [D], axis=1)
        owned = D // (dp_count * query_count)
        mine = lax.axis_index("dp") * query_count + place
        grad_cell = dot_lt(
            lax.dynamic_slice_in_dim(all_heads, mine * owned, owned, 1), all_cells
        )
        outs = []
        start = 0
        for value, piece in zip(small, flat):
            size = piece.shape[1]
            outs.append(summed[start : start + size].reshape(value.shape[0], -1))
            start += size

        attn_sum = attn_sums.result()
        qkv_cut = 3 * D // 2

        return (
            encoded_rows,
            grad_tokens,
            outs[0],
            outs[1],
            outs[2],
            outs[3],
            jnp.concatenate([half[:, :qkv_cut] for half in attn_sum], axis=1),
            jnp.concatenate([half[:, qkv_cut:] for half in attn_sum], axis=1),
            jnp.concatenate(up_result, axis=1),
            jnp.concatenate(down_result, axis=1),
            grad_cell,
            grad_gene,
            outs[4][0],
            grad_table,
        )

    return shards


def split_heads(qkv_row):
    queries = qkv_row[:, :D].reshape(ROW_LEN, HEADS, HEAD_DIM)
    keys_in = qkv_row[:, D : 2 * D].reshape(ROW_LEN, HEADS, HEAD_DIM)
    values_in = qkv_row[:, 2 * D :].reshape(ROW_LEN, HEADS, HEAD_DIM)
    return (queries, keys_in, values_in)


def row_scores(queries, keys_in, segment_row):
    scores = jnp.einsum("qhd,khd->hqk", queries, keys_in, preferred_element_type=jnp.float32) * (
        1.0 / math.sqrt(HEAD_DIM)
    )
    same_cell = segment_row[:, None] == segment_row[None, :]
    return jnp.where(same_cell[None], scores, -1e30)


def attend_any(member):
    qkv_row, segment_row = member
    queries, keys_in, values_in = split_heads(qkv_row)
    scores = row_scores(queries, keys_in, segment_row)
    highest_score = jnp.max(scores, axis=-1, keepdims=True)
    weights = jnp.exp(scores - highest_score)
    weight_sum = jnp.sum(weights, axis=-1, keepdims=True)
    attention = (weights / weight_sum).astype(jnp.bfloat16)
    mixed = jnp.einsum(
        "hqk,khd->qhd", attention, values_in, preferred_element_type=jnp.float32
    ).astype(jnp.bfloat16)
    return (mixed.reshape(ROW_LEN, D), (highest_score + jnp.log(weight_sum))[:, :, 0])


def attend_back_any(member):
    qkv_row, segment_row, log_total, grad_mixed = member
    queries, keys_in, values_in = split_heads(qkv_row)
    scores = row_scores(queries, keys_in, segment_row)
    attention = jnp.exp(scores - log_total[:, :, None])
    grad_heads = grad_mixed.reshape(ROW_LEN, HEADS, HEAD_DIM)
    grad_probs = jnp.einsum(
        "qhd,khd->hqk", grad_heads, values_in, preferred_element_type=jnp.float32
    )
    grad_scores = (
        attention * (grad_probs - jnp.sum(attention * grad_probs, axis=-1, keepdims=True))
    ).astype(jnp.bfloat16)
    scale_factor = 1.0 / math.sqrt(HEAD_DIM)
    grad_query = (
        jnp.einsum("hqk,khd->qhd", grad_scores, keys_in, preferred_element_type=jnp.float32)
        * scale_factor
    )
    grad_keys = (
        jnp.einsum("hqk,qhd->khd", grad_scores, queries, preferred_element_type=jnp.float32)
        * scale_factor
    )
    grad_values = jnp.einsum(
        "hqk,qhd->khd",
        attention.astype(jnp.bfloat16),
        grad_heads,
        preferred_element_type=jnp.float32,
    )
    return jnp.concatenate(
        [
            grad_query.reshape(ROW_LEN, D),
            grad_keys.reshape(ROW_LEN, D),
            grad_values.reshape(ROW_LEN, D),
        ],
        axis=1,
    )


def owned_cols(values_in, dp_count, query_count, place):
    width = values_in.shape[1] // (dp_count * query_count)
    shaped = values_in.reshape(values_in.shape[0], dp_count, query_count, width)
    return lax.dynamic_index_in_dim(shaped, place, axis=2, keepdims=False)


def owned_term(left, right, dp_count, query_count, place):
    return jnp.einsum(
        "ndr,ne->dre",
        owned_cols(left, dp_count, query_count, place),
        right,
        preferred_element_type=jnp.float32,
    )


def owner_blocks(values_in, dp_count, query_count):
    width = values_in.shape[0] // (dp_count * query_count)
    return values_in.reshape(dp_count, query_count, width, values_in.shape[1])


def shards_any(
    tokens,
    cell_lengths,
    out_cotangent,
    ln_gains,
    ln_biases,
    proj_biases,
    ff_biases,
    w_qkv,
    w_out,
    w_up,
    w_down,
    dec_cell,
    dec_gene,
    dec_out,
    gene_table,
    query_ids,
    labels,
):
    row_count = tokens.shape[0]
    token_count = row_count * ROW_LEN
    dp_count = lax.axis_size("dp")
    query_count = lax.axis_size("query")
    place = lax.axis_index("query")
    starts, segment = cell_layout(cell_lengths)
    gathered = (
        lax.all_gather(w_qkv, "query", axis=0, tiled=True),
        lax.all_gather(w_out, "query", axis=0, tiled=True),
        lax.all_gather(w_up, "query", axis=0, tiled=True),
        lax.all_gather(w_down, "query", axis=0, tiled=True),
        lax.all_gather(dec_cell, "query", axis=0, tiled=True),
        lax.all_gather(dec_gene, "query", axis=0, tiled=True),
        lax.all_gather(gene_table, "query", axis=0, tiled=True),
    )
    full_qkv, full_out, full_up, full_down, full_cell, full_gene, full_table = gathered
    flat_tokens = tokens.astype(jnp.float32).reshape(token_count, D)
    normed, first_pull = jax.vjp(layer_norm, flat_tokens, ln_gains[0], ln_biases[0])
    normed_low = normed.astype(jnp.bfloat16)
    zeroes = jnp.zeros((D,), jnp.float32)
    qkv_bias = jnp.concatenate([proj_biases[0], zeroes, proj_biases[1]])
    qkv_low = (jnp.dot(normed_low, full_qkv, preferred_element_type=jnp.float32) + qkv_bias).astype(
        jnp.bfloat16
    )
    qkv_rows = qkv_low.reshape(row_count, ROW_LEN, 3 * D)
    mixed_rows, log_totals = lax.map(attend_any, (qkv_rows, segment))
    mixed_low = mixed_rows.reshape(token_count, D)
    middle = (
        flat_tokens
        + jnp.dot(mixed_low, full_out, preferred_element_type=jnp.float32)
        + proj_biases[2]
    )
    second, second_pull = jax.vjp(layer_norm, middle, ln_gains[1], ln_biases[1])
    second_low = second.astype(jnp.bfloat16)
    hidden = jnp.dot(second_low, full_up, preferred_element_type=jnp.float32) + ff_biases[0]
    active, active_pull = jax.vjp(smooth_gate, hidden)
    active_low = active.astype(jnp.bfloat16)
    encoded = (
        middle + jnp.dot(active_low, full_down, preferred_element_type=jnp.float32) + proj_biases[3]
    )
    places = jnp.arange(ROW_LEN, dtype=jnp.int32)
    picker = (places[None, None, :] == starts[:, :, None]).astype(jnp.float32)
    local_cells = row_count * CELLS_ROW
    heads_low = (
        jnp.einsum(
            "rcl,rld->rcd", picker, encoded.reshape(row_count, ROW_LEN, D), precision=HIGHEST
        )
        .reshape(local_cells, D)
        .astype(jnp.bfloat16)
    )
    cell_heads = lax.all_gather(heads_low, "query", axis=0, tiled=True)
    cell_part = jnp.dot(cell_heads, full_cell, preferred_element_type=jnp.float32)
    gene_rows = jnp.take(full_table, query_ids, axis=0)
    before = (
        cell_part[:, None, :]
        + jnp.einsum("cqd,df->cqf", gene_rows, full_gene, preferred_element_type=jnp.float32)
        + ff_biases[1]
    )
    gated_dec, gated_pull = jax.vjp(smooth_gate, before)
    logit_weight = dec_out.astype(jnp.float32)
    logits = jnp.einsum("cqf,f->cq", gated_dec, logit_weight, precision=HIGHEST)
    logit_slope = jax.nn.sigmoid(logits) - labels.astype(jnp.float32)
    (grad_before,) = gated_pull(logit_slope[:, :, None] * logit_weight)
    before_low = grad_before.astype(jnp.bfloat16)
    grad_dec_bias = jnp.sum(before_low, axis=(0, 1), dtype=jnp.float32)
    grad_logit = jnp.einsum("cqf,cq->f", gated_dec, logit_slope, precision=HIGHEST)
    gene_terms = jnp.einsum(
        "cqd,cqf->df", gene_rows, before_low, preferred_element_type=jnp.float32
    )
    genes_back = jnp.einsum(
        "cqf,df->cqd", before_low, full_gene, preferred_element_type=jnp.float32
    ).astype(jnp.bfloat16)
    choose = (query_ids.reshape(-1)[:, None] == jnp.arange(GENES, dtype=jnp.int32)[None, :]).astype(
        jnp.bfloat16
    )
    table_terms = jnp.einsum(
        "ng,nd->gd", choose, genes_back.reshape(-1, D), preferred_element_type=jnp.float32
    )
    gene_parts, table_parts = (
        lax.all_to_all(
            owner_blocks(gene_terms, dp_count, query_count).astype(jnp.bfloat16),
            "query",
            split_axis=1,
            concat_axis=1,
            tiled=True,
        ).astype(jnp.float32),
        lax.all_to_all(
            owner_blocks(table_terms, dp_count, query_count).astype(jnp.bfloat16),
            "query",
            split_axis=1,
            concat_axis=1,
            tiled=True,
        ).astype(jnp.float32),
    )
    grad_gene = jnp.sum(gene_parts, axis=1)
    grad_table = jnp.sum(table_parts, axis=1)
    cell_total = lax.psum(
        jnp.sum(before_low, axis=1, dtype=jnp.float32).astype(jnp.bfloat16), "query"
    )
    grad_cell = owned_term(cell_heads, cell_total, dp_count, query_count, place)
    heads_all = jnp.einsum("cf,df->cd", cell_total, full_cell, preferred_element_type=jnp.float32)
    heads_back = (
        lax.dynamic_slice_in_dim(heads_all, place * local_cells, local_cells, 0)
        .astype(jnp.bfloat16)
        .astype(jnp.float32)
    )
    grad_encoded = out_cotangent.astype(jnp.float32) + jnp.einsum(
        "rcl,rcd->rld", picker, heads_back.reshape(row_count, CELLS_ROW, D), precision=HIGHEST
    )
    grad_flat = grad_encoded.reshape(token_count, D)

    def empty_term(left_width, right_width):
        return jnp.zeros(
            (dp_count, left_width // (dp_count * query_count), right_width), jnp.float32
        )

    branch_low = grad_flat.astype(jnp.bfloat16)
    grad_out_bias = jnp.sum(branch_low, axis=0, dtype=jnp.float32)
    grad_active = jnp.einsum("nd,fd->nf", branch_low, full_down, preferred_element_type=jnp.float32)
    (grad_hidden,) = active_pull(grad_active)
    hidden_low = grad_hidden.astype(jnp.bfloat16)
    grad_up_bias = jnp.sum(hidden_low, axis=0, dtype=jnp.float32)
    grad_second = jnp.einsum("nf,df->nd", hidden_low, full_up, preferred_element_type=jnp.float32)
    middle_part, grad_gain_two, grad_shift_two = second_pull(grad_second)
    grad_middle = grad_flat + middle_part
    ff_terms = jnp.stack([grad_up_bias, grad_dec_bias], axis=1)
    attn_low = grad_middle.astype(jnp.bfloat16)
    grad_attn_bias = jnp.sum(attn_low, axis=0, dtype=jnp.float32)
    mixed_back = jnp.einsum(
        "ne,de->nd", attn_low, full_out, preferred_element_type=jnp.float32
    ).astype(jnp.bfloat16)
    qkv_back = lax.map(
        attend_back_any, (qkv_rows, segment, log_totals, mixed_back.reshape(row_count, ROW_LEN, D))
    )
    qkv_back_low = qkv_back.reshape(token_count, 3 * D).astype(jnp.bfloat16)
    bias_sums = jnp.sum(qkv_back_low, axis=0, dtype=jnp.float32)
    grad_normed = jnp.einsum(
        "ne,de->nd", qkv_back_low, full_qkv, preferred_element_type=jnp.float32
    )
    token_part, grad_gain_one, grad_shift_one = first_pull(grad_normed)
    grad_tokens = (grad_middle + token_part).reshape(row_count, ROW_LEN, D)
    gain_terms = jnp.stack([grad_gain_one, grad_gain_two], axis=1)
    shift_terms = jnp.stack([grad_shift_one, grad_shift_two], axis=1)
    proj_terms = jnp.stack(
        [bias_sums[:D], bias_sums[2 * D :], grad_attn_bias, grad_out_bias], axis=1
    )
    totals = (empty_term(D, 3 * D), empty_term(D, D), empty_term(D, FF), empty_term(FF, D))
    pieces = (
        lax.all_gather(normed_low, "query", axis=0, tiled=True),
        lax.all_gather(qkv_back_low, "query", axis=0, tiled=True),
        lax.all_gather(mixed_low, "query", axis=0, tiled=True),
        lax.all_gather(attn_low, "query", axis=0, tiled=True),
        lax.all_gather(second_low, "query", axis=0, tiled=True),
        lax.all_gather(hidden_low, "query", axis=0, tiled=True),
        lax.all_gather(active_low, "query", axis=0, tiled=True),
        lax.all_gather(branch_low, "query", axis=0, tiled=True),
    )
    every_fold = tuple(
        (
            owned_term(pieces[2 * i], pieces[2 * i + 1], dp_count, query_count, place)
            for i in range(len(totals))
        )
    )
    every_sum = (
        lax.psum_scatter(
            every_fold[2].astype(jnp.bfloat16), "dp", scatter_dimension=0, tiled=True
        ).astype(jnp.float32),
        lax.psum_scatter(
            every_fold[3].astype(jnp.bfloat16), "dp", scatter_dimension=0, tiled=True
        ).astype(jnp.float32),
        lax.psum_scatter(
            grad_cell.astype(jnp.bfloat16), "dp", scatter_dimension=0, tiled=True
        ).astype(jnp.float32),
        lax.psum_scatter(
            grad_gene.astype(jnp.bfloat16), "dp", scatter_dimension=0, tiled=True
        ).astype(jnp.float32),
        lax.psum_scatter(
            grad_table.astype(jnp.bfloat16), "dp", scatter_dimension=0, tiled=True
        ).astype(jnp.float32),
        lax.psum_scatter(
            every_fold[0].astype(jnp.bfloat16), "dp", scatter_dimension=0, tiled=True
        ).astype(jnp.float32),
        lax.psum_scatter(
            every_fold[1].astype(jnp.bfloat16), "dp", scatter_dimension=0, tiled=True
        ).astype(jnp.float32),
    )
    ffn_sums = every_sum[:5]
    attn_sums = every_sum[5:]
    small_sums = (
        lax.psum_scatter(gain_terms, ("dp", "query"), scatter_dimension=0, tiled=True),
        lax.psum_scatter(shift_terms, ("dp", "query"), scatter_dimension=0, tiled=True),
        lax.psum_scatter(proj_terms, ("dp", "query"), scatter_dimension=0, tiled=True),
        lax.psum_scatter(ff_terms, ("dp", "query"), scatter_dimension=0, tiled=True),
        lax.psum_scatter(grad_logit, ("dp", "query"), scatter_dimension=0, tiled=True),
    )

    def flat_rows(values_in):
        return values_in.reshape(-1, values_in.shape[-1])

    return (
        encoded.reshape(row_count, ROW_LEN, D),
        grad_tokens,
        small_sums[0].T,
        small_sums[1].T,
        small_sums[2].T,
        small_sums[3].T,
        flat_rows(attn_sums[0]),
        flat_rows(attn_sums[1]),
        flat_rows(ffn_sums[0]),
        flat_rows(ffn_sums[1]),
        flat_rows(ffn_sums[2]),
        flat_rows(ffn_sums[3]),
        small_sums[4],
        flat_rows(ffn_sums[4]),
    )


def solution(mesh):
    placed = (
        P(("dp", "query"), None, None),
        P(("dp", "query"), None),
        P(("dp", "query"), None, None),
        P(),
        P(),
        P(),
        P(),
        P("query", None),
        P("query", None),
        P("query", None),
        P("query", None),
        P("query", None),
        P("query", None),
        P(),
        P("query", None),
        P("dp", "query"),
        P("dp", "query"),
    )
    rows = P(("dp", "query"), None)
    grid = Grid(mesh)
    return jax.shard_map(
        make_shards(grid) if grid.paired() else shards_any,
        mesh=mesh,
        in_specs=placed,
        out_specs=(
            P(("dp", "query"), None, None),
            P(("dp", "query"), None, None),
            P(None, ("dp", "query")),
            P(None, ("dp", "query")),
            P(None, ("dp", "query")),
            P(None, ("dp", "query")),
            rows,
            rows,
            rows,
            rows,
            rows,
            rows,
            P(("dp", "query")),
            rows,
        ),
        check_vma=False,
    )
```

```python
import math

import jax
import jax.numpy as jnp
from jax import lax
from jax.experimental import pallas as pl
from jax.experimental.pallas import tpu as pltpu
from jax.sharding import PartitionSpec as P

D = 1280
HEADS = 20
HEAD_DIM = 64
FF = 5120
ROW_LEN = 512
CELLS_ROW = 4
GENES = 1024
EPSILON = 1e-05
HIGHEST = lax.Precision.HIGHEST
F32 = jnp.float32
BF16 = jnp.bfloat16
VMEM_ASKED = 56 << 20


def layer_norm(values_in, scale_row, offset_row):
    center = values_in - jnp.mean(values_in, axis=-1, keepdims=True)
    spread = jnp.mean(center * center, axis=-1, keepdims=True)
    return center * lax.rsqrt(spread + EPSILON) * scale_row + offset_row


def smooth_gate(values_in):
    return jax.nn.gelu(values_in, approximate=False)


def dot(left, right):
    return jnp.dot(left, right, preferred_element_type=F32)


def dot_rt(left, right):
    return lax.dot_general(left, right, (((1,), (1,)), ((), ())), preferred_element_type=F32)


def dot_lt(left, right):
    return lax.dot_general(left, right, (((0,), (0,)), ((), ())), preferred_element_type=F32)


def cell_layout(lengths):
    cell_ends = jnp.cumsum(lengths, axis=-1, dtype=jnp.int32)
    starts = cell_ends - lengths
    places = jnp.arange(ROW_LEN, dtype=jnp.int32)
    segment = jnp.sum(
        (places[None, :, None] >= cell_ends[:, None, :]).astype(jnp.int32), axis=-1, dtype=jnp.int32
    )
    return (starts, segment)


def cell_mask(segment_row, segment_column, mask):
    same = segment_column[...] == segment_row[...]
    mask[...] = jnp.where(same, 0.0, -1e30)


PAIRS = 2
WIDE = PAIRS * 2 * HEAD_DIM


def attend_kernel(segment_row, segment_column, query, key, value, mixed, totals, mask):
    @pl.when(pl.program_id(1) == 0)
    def _():
        cell_mask(segment_row.at[0], segment_column.at[0], mask)

    ones = jnp.ones((8, ROW_LEN), BF16)
    value_t = value[0].T
    parts = []
    for head in range(2 * PAIRS):
        columns = slice(head * HEAD_DIM, (head + 1) * HEAD_DIM)
        scaled = query[0, :, columns] * jnp.asarray(1.0 / math.sqrt(HEAD_DIM), BF16)
        scores = dot_rt(key[0, :, columns], scaled) + mask[...]
        top = jnp.max(scores, axis=0, keepdims=True)
        weights = jnp.exp(scores - top).astype(BF16)
        left = jnp.concatenate([value_t[columns], ones], axis=0)
        product = dot(left, weights)
        total = product[HEAD_DIM : HEAD_DIM + 1]
        parts.append(product[:HEAD_DIM] / total)
        totals[0, 0, head : head + 1] = top + jnp.log(total)
    mixed[0] = jnp.concatenate(parts, axis=0).T.astype(BF16)


def attend(qkv, segment):
    rows = qkv.shape[0]
    pairs = HEADS // 2 // PAIRS
    wide = WIDE

    def part(offset):
        return pl.BlockSpec((1, ROW_LEN, wide), lambda r, i: (r, 0, offset + i))

    return pl.pallas_call(
        attend_kernel,
        grid=(rows, pairs),
        in_specs=[
            pl.BlockSpec((1, 1, ROW_LEN), lambda r, i: (r, 0, 0)),
            pl.BlockSpec((1, ROW_LEN, 1), lambda r, i: (r, 0, 0)),
            part(0),
            part(pairs),
            part(2 * pairs),
        ],
        out_specs=[
            pl.BlockSpec((1, ROW_LEN, wide), lambda r, i: (r, 0, i)),
            pl.BlockSpec((1, 1, 2 * PAIRS, ROW_LEN), lambda r, i: (r, i, 0, 0)),
        ],
        out_shape=[
            jax.ShapeDtypeStruct((rows, ROW_LEN, pairs * wide), BF16),
            jax.ShapeDtypeStruct((rows, pairs, 2 * PAIRS, ROW_LEN), F32),
        ],
        scratch_shapes=[pltpu.VMEM((ROW_LEN, ROW_LEN), F32)],
        compiler_params=pltpu.CompilerParams(vmem_limit_bytes=VMEM_ASKED),
        cost_estimate=pl.CostEstimate(flops=1, bytes_accessed=1, transcendentals=0),
    )(segment[:, None, :], segment[:, :, None], qkv, qkv, qkv)


def attend_back_kernel(
    segment_row, segment_column, query, key, value, mixed, back, totals, d_qkv, mask
):
    @pl.when(pl.program_id(1) == 0)
    def _():
        cell_mask(segment_row.at[0], segment_column.at[0], mask)

    scale = jnp.asarray(1.0 / math.sqrt(HEAD_DIM), BF16)
    key_t = key[0].T
    product_t = (back[0].astype(F32) * mixed[0].astype(F32)).T
    queries, keys, values = [], [], []
    for head in range(2 * PAIRS):
        columns = slice(head * HEAD_DIM, (head + 1) * HEAD_DIM)
        scaled = query[0, :, columns] * scale
        grad = back[0, :, columns]
        scores = dot_rt(key[0, :, columns], scaled) + mask[...]
        weights = jnp.exp(scores - totals[0, 0, head : head + 1])
        d_weights = dot_rt(value[0, :, columns], grad)
        shift = jnp.sum(product_t[columns], axis=0, keepdims=True)
        d_scores = (weights * (d_weights - shift)).astype(BF16)
        values.append(dot(weights.astype(BF16), grad))
        keys.append(dot(d_scores, scaled))
        queries.append(dot(key_t[columns], d_scores))
    pair = pl.program_id(1)
    parts = [
        jnp.concatenate(queries, axis=0).T * (1.0 / math.sqrt(HEAD_DIM)),
        jnp.concatenate(keys, axis=1),
        jnp.concatenate(values, axis=1),
    ]
    for i, part in enumerate(parts):
        columns = pl.ds(pl.multiple_of(i * D + pair * WIDE, 128), WIDE)
        d_qkv[0, :, columns] = part.astype(BF16)


def attend_back(qkv, segment, mixed, back, totals):
    rows = qkv.shape[0]
    pairs = HEADS // 2 // PAIRS
    wide = WIDE

    def part(offset):
        return pl.BlockSpec((1, ROW_LEN, wide), lambda r, i: (r, 0, offset + i))

    return pl.pallas_call(
        attend_back_kernel,
        grid=(rows, pairs),
        in_specs=[
            pl.BlockSpec((1, 1, ROW_LEN), lambda r, i: (r, 0, 0)),
            pl.BlockSpec((1, ROW_LEN, 1), lambda r, i: (r, 0, 0)),
            part(0),
            part(pairs),
            part(2 * pairs),
            part(0),
            part(0),
            pl.BlockSpec((1, 1, 2 * PAIRS, ROW_LEN), lambda r, i: (r, i, 0, 0)),
        ],
        out_specs=pl.BlockSpec((1, ROW_LEN, 3 * D), lambda r, i: (r, 0, 0)),
        out_shape=jax.ShapeDtypeStruct((rows, ROW_LEN, 3 * D), BF16),
        scratch_shapes=[pltpu.VMEM((ROW_LEN, ROW_LEN), F32)],
        compiler_params=pltpu.CompilerParams(vmem_limit_bytes=VMEM_ASKED),
        cost_estimate=pl.CostEstimate(flops=1, bytes_accessed=1, transcendentals=0),
    )(segment[:, None, :], segment[:, :, None], qkv, qkv, qkv, mixed, back, totals)


CHUNK = 1280
HALF_CHUNK = 640


def unit_places(outer, inner, core):
    mine = (outer ^ core, inner ^ (1 - core))
    theirs = (outer ^ (1 - core), inner ^ core)
    corner = (outer ^ 1, inner ^ 1)
    return [
        (outer, inner, core),
        (outer, inner, 1 - core),
        (*mine, core),
        (*mine, 1 - core),
        (*corner, core),
        (*theirs, 1 - core),
        (*theirs, core),
        (*corner, 1 - core),
    ]


def part_copies(sources, columns, place, buffer, sems, half_rows, act):
    shard, *units = sources
    query, outer, inner, core = (place[i] for i in range(4))
    size = units[0].shape[0]
    act(
        pltpu.make_async_copy(
            shard.at[:, columns],
            buffer.at[pl.ds(pl.multiple_of(query * half_rows, 16), half_rows), :],
            sems.at[0],
        )
    )
    for i, (unit, (zb, y, c)) in enumerate(zip(units, unit_places(outer, inner, core))):
        row = (1 - query) * half_rows + ((zb * 2 + y) * 2 + c) * size
        act(
            pltpu.make_async_copy(
                unit.at[:, columns],
                buffer.at[pl.ds(pl.multiple_of(row, 16), size), :],
                sems.at[1 + i],
            )
        )


def chunk_place(step, place, half):
    steps = half // CHUNK
    own = step < steps
    return jnp.where(own, place[0] * steps + step, (1 - place[0]) * steps + step - steps)


def up_copies(sources, place, step, buffer, sems, act):
    half = FF // 2
    start = pl.multiple_of(chunk_place(step, place, half) * CHUNK, 128)
    columns = pl.ds(start, CHUNK)
    part_copies(sources, columns, place, buffer, sems, sources[0].shape[0], act)


def down_copies(sources, place, step, buffer, sems, act):
    shard, *units = sources
    query, outer, inner, core = (place[i] for i in range(4))
    size = units[0].shape[0]
    steps = shard.shape[0] // CHUNK
    own = step < steps
    local = jnp.where(own, step, step - steps)

    @pl.when(own)
    def _():
        act(
            pltpu.make_async_copy(
                shard.at[pl.ds(pl.multiple_of(local * CHUNK, 16), CHUNK), :], buffer, sems.at[0]
            )
        )

    for piece in range(CHUNK // (2 * size)):
        at = local * (CHUNK // (2 * size)) + piece
        for i, (unit, (zb, y, c)) in enumerate(zip(units, unit_places(outer, inner, core))):

            @pl.when(jnp.logical_and(jnp.logical_not(own), at == zb * 2 + y))
            def _():
                row = pl.multiple_of((piece * 2 + c) * size, 16)
                act(
                    pltpu.make_async_copy(unit, buffer.at[pl.ds(row, size), :], sems.at[1 + i])
                )


def stream(copies, buffer, sems):
    step, steps = pl.program_id(0), pl.num_programs(0)
    slot = lax.rem(step, 2)

    @pl.when(step == 0)
    def _():
        copies(step, buffer.at[slot], sems.at[slot], lambda copy: copy.start())

    @pl.when(step + 1 < steps)
    def _():
        copies(step + 1, buffer.at[1 - slot], sems.at[1 - slot], lambda copy: copy.start())

    copies(step, buffer.at[slot], sems.at[slot], lambda copy: copy.wait())
    return buffer.at[slot]


def gate(values):
    inner = 0.5 * lax.erf(values * math.sqrt(0.5)) + 0.5
    bell = jnp.exp(values * values * -0.5) * (1.0 / math.sqrt(2.0 * math.pi))
    return values * inner, inner + values * bell


def up_kernel(place, second, bias, *refs):
    sources, (active, slope, buffer, sems) = refs[:9], refs[9:]
    weights = stream(lambda *at: up_copies(sources, place, *at), buffer, sems)
    value, rise = gate(dot(second[...], weights[...]) + bias[...])
    active[...] = value.astype(BF16)
    slope[...] = rise.astype(BF16)


def down_kernel(place, active, middle, bias, picker, *refs):
    sources, (out, heads, buffer, sems) = refs[:9], refs[9:]
    weights = stream(lambda *at: down_copies(sources, place, *at), buffer, sems)

    @pl.when(pl.program_id(0) == 0)
    def _():
        out[...] = middle[...] + bias[...]

    out[...] += dot(active[...], weights[...])

    @pl.when(pl.program_id(0) == pl.num_programs(0) - 1)
    def _():
        heads[...] = dot(picker[...], out[...].astype(BF16)).astype(BF16)


def back_kernel(place, branch, slope, *refs):
    up, down = refs[:9], refs[9:18]
    d_hidden, sums, out, buffer, sems, buffer_two, sems_two = refs[18:]
    up_part = stream(lambda *at: up_copies(up, place, *at), buffer, sems)
    down_part = stream(lambda *at: down_copies(down, place, *at), buffer_two, sems_two)

    @pl.when(pl.program_id(0) == 0)
    def _():
        out[...] = jnp.zeros_like(out)

    d_active = dot_rt(branch[...], down_part[...])
    low = (d_active * slope[...].astype(F32)).astype(BF16)
    d_hidden[...] = low
    sums[...] = jnp.sum(low.astype(F32), axis=0, keepdims=True)
    out[...] += dot_rt(low, up_part[...])


def qkv_kernel(place, normed, bias, *refs):
    sources, (out, buffer, sems) = refs[:9], refs[9:]

    def copies(step, *at):
        columns = pl.ds(pl.multiple_of(step * CHUNK, 128), CHUNK)
        part_copies(sources, columns, place, *at[:2], sources[0].shape[0], at[2])

    weights = stream(copies, buffer, sems)
    out[...] = (dot(normed[...], weights[...]) + bias[...]).astype(BF16)


def qkv_back_kernel(place, back, *refs):
    sources, (out, buffer, sems) = refs[:9], refs[9:]

    def copies(step, *at):
        columns = pl.ds(pl.multiple_of(step * CHUNK, 128), CHUNK)
        part_copies(sources, columns, place, *at[:2], sources[0].shape[0], at[2])

    weights = stream(copies, buffer, sems)
    terms = dot_rt(back[...], weights[...])

    @pl.when(pl.program_id(0) == 0)
    def _():
        out[...] = terms

    @pl.when(pl.program_id(0) > 0)
    def _():
        out[...] += terms


def qkv_call(kernel, place, inputs, specs, out_shape, out_spec, columns, weights):
    return pl.pallas_call(
        kernel,
        grid_spec=pltpu.PrefetchScalarGridSpec(
            num_scalar_prefetch=1,
            grid=(columns // CHUNK,),
            in_specs=specs + [pl.BlockSpec(memory_space=pl.ANY)] * 9,
            out_specs=out_spec,
            scratch_shapes=[pltpu.VMEM((2, D, CHUNK), BF16), pltpu.SemaphoreType.DMA((2, 9))],
        ),
        out_shape=out_shape,
        compiler_params=pltpu.CompilerParams(vmem_limit_bytes=VMEM_ASKED),
        cost_estimate=pl.CostEstimate(flops=1, bytes_accessed=1, transcendentals=0),
    )(place, *inputs, *weights)


def project(place, normed, bias, weights):
    count, columns = normed.shape[0], weights[0].shape[1]
    whole = pl.BlockSpec((count, D), lambda j, place: (0, 0))
    row = pl.BlockSpec((1, CHUNK), lambda j, place: (0, j))
    out = pl.BlockSpec((count, CHUNK), lambda j, place: (0, j))
    shape = jax.ShapeDtypeStruct((count, columns), BF16)
    return qkv_call(
        qkv_kernel, place, [normed, bias], [whole, row], shape, out, columns, weights
    )


def project_back(place, back, weights):
    count, columns = back.shape
    whole = pl.BlockSpec((count, D), lambda j, place: (0, 0))
    chunk = pl.BlockSpec((count, CHUNK), lambda j, place: (0, j))
    shape = jax.ShapeDtypeStruct((count, D), F32)
    return qkv_call(qkv_back_kernel, place, [back], [chunk], shape, whole, columns, weights)


def feed_call(kernel, count, inputs, outputs, slots, place, *values, keep=()):
    def at(j, place):
        return chunk_place(j, place, FF // 2)

    specs = {
        "hidden": pl.BlockSpec((count, CHUNK), lambda j, place: (0, at(j, place))),
        "row": pl.BlockSpec((1, CHUNK), lambda j, place: (0, at(j, place))),
        "whole": pl.BlockSpec((count, D), lambda j, place: (0, 0)),
        "any": pl.BlockSpec(memory_space=pl.ANY),
        "vector": pl.BlockSpec((1, D), lambda j, place: (0, 0)),
    }
    shapes = {
        "hidden": jax.ShapeDtypeStruct((count, FF), BF16),
        "row": jax.ShapeDtypeStruct((1, FF), F32),
        "whole": jax.ShapeDtypeStruct((count, D), F32),
    }
    for name, array in keep:
        block = array.shape
        specs[name] = pl.BlockSpec(block, lambda j, place: (0, 0))
        shapes[name] = jax.ShapeDtypeStruct(block, BF16)
    scratch = []
    for slot in slots:
        scratch += [pltpu.VMEM((2, *slot), BF16), pltpu.SemaphoreType.DMA((2, 9))]
    return pl.pallas_call(
        kernel,
        grid_spec=pltpu.PrefetchScalarGridSpec(
            num_scalar_prefetch=1,
            grid=(FF // CHUNK,),
            in_specs=[specs[name] for name in inputs],
            out_specs=[specs[name] for name in outputs],
            scratch_shapes=scratch,
        ),
        out_shape=[shapes[name] for name in outputs],
        compiler_params=pltpu.CompilerParams(vmem_limit_bytes=VMEM_ASKED),
        cost_estimate=pl.CostEstimate(flops=1, bytes_accessed=1, transcendentals=0),
    )(place, *values)


UP_SLOT, DOWN_SLOT = (D, CHUNK), (CHUNK, D)


def feed_up(place, second, bias, up):
    names = ["whole", "row"] + ["any"] * 9
    return feed_call(
        up_kernel, second.shape[0], names, ["hidden", "hidden"], [UP_SLOT], place, second, bias, *up
    )


def feed_down(place, active, middle, bias, picker, down):
    names = ["hidden", "whole", "vector", "picker"] + ["any"] * 9
    heads = jax.ShapeDtypeStruct((picker.shape[0], D), BF16)
    return feed_call(
        down_kernel, active.shape[0], names, ["whole", "heads"], [DOWN_SLOT],
        place, active, middle, bias, picker, *down, keep=(("picker", picker), ("heads", heads)),
    )


def feed_back(place, branch, slope, up, down):
    names = ["whole", "hidden"] + ["any"] * 18
    return feed_call(
        back_kernel, branch.shape[0], names, ["hidden", "row", "whole"], [UP_SLOT, DOWN_SLOT],
        place, branch, slope, *up, *down,
    )


def decode_kernel(mine, other, gene, got, bias, weight, labels, low, sums, by_weight):
    cells = mine.shape[0]
    shape = (cells, gene.shape[0] // cells, gene.shape[1])
    parts = (gene[...].astype(F32) + got[...].astype(F32) + bias[...]).reshape(shape)
    before = (mine[...].astype(F32) + other[...].astype(F32))[:, None, :] + parts
    value, rise = gate(before)
    row = weight[...].astype(F32)[None]
    logits = jnp.sum(value * row, axis=2, keepdims=True)
    slope = jax.nn.sigmoid(logits) - labels[...].astype(F32)
    grad = (rise * (slope * row)).astype(BF16)
    low[...] = grad.reshape(low.shape)
    sums[...] = jnp.sum(grad.astype(F32), axis=1).astype(BF16)
    by_weight[...] = jnp.sum(jnp.sum(value * slope, axis=0), axis=0, keepdims=True)


def decode(mine, other, gene, got, bias, weight, labels):
    cells, queries = labels.shape
    return pl.pallas_call(
        decode_kernel,
        out_shape=[
            jax.ShapeDtypeStruct((cells * queries, FF), BF16),
            jax.ShapeDtypeStruct((cells, FF), BF16),
            jax.ShapeDtypeStruct((1, FF), F32),
        ],
        compiler_params=pltpu.CompilerParams(vmem_limit_bytes=VMEM_ASKED),
        cost_estimate=pl.CostEstimate(flops=1, bytes_accessed=1, transcendentals=0),
    )(mine, other, gene, got, bias, weight, labels[:, :, None])


def term_kernel(count, mine, units, place, *refs):
    query, _, inner, core = (place[i] for i in range(4))
    inputs = 1 + max(source for unit in units for _, source in unit)
    lefts, rights, (out, blocks), turned = (
        refs[:count],
        refs[count : count + inputs],
        refs[count + inputs : count + inputs + 2],
        refs[count + inputs + 2 :],
    )
    step = pl.program_id(0)
    half = core if mine else 1 - core

    @pl.when(step == 0)
    def _():
        outer = blocks.shape[0] // 8
        size = 2 * outer * blocks.shape[1]
        for left, into in zip(lefts, turned):
            blocks[...] = left[...].astype(F32).T.reshape(blocks.shape)
            for to in range(4):
                first, second = to // 2, to % 2
                x = query ^ jnp.where(half == 0, first, second)
                y = inner ^ jnp.where(half == 0, second, first)
                rows = [
                    blocks[((z * 2 + y) * 2 + c) * 2 + x] for z in range(outer) for c in range(2)
                ]
                into[pl.ds(to * size, size), :] = jnp.concatenate(rows, axis=0).astype(BF16)

    for at, unit in enumerate(units):

        @pl.when(step == at)
        def _():
            for side, (pair, source) in enumerate(unit):
                terms = dot(turned[pair][...], rights[source][...]).astype(BF16)
                columns = slice(side * HALF_CHUNK, (side + 1) * HALF_CHUNK)
                out[:, :, :, columns] = terms.reshape(*out.shape[:3], HALF_CHUNK)


def weight_terms(place, mine, *pairs):
    count, rows = pairs[0][0].shape
    sizes = [right.shape[1] // 2 // HALF_CHUNK for _, right in pairs]
    blocks = [(i, block) for i, size in enumerate(sizes) for block in range(size)]
    plan = [blocks[i : i + 2] for i in range(0, len(blocks), 2)]
    steps = len(plan)
    sources = sorted({(side, unit[side][0]) for unit in plan for side in range(2)})

    def right_spec(side, pair):
        wanted = [unit[side][1] if unit[side][0] == pair else None for unit in plan]
        known = [block for block in wanted if block is not None]

        def at(j, place):
            half = place[3] if mine else 1 - place[3]
            index = known[0]
            for step, block in enumerate(wanted):
                if block is not None:
                    index = jnp.where(j >= step, block, index)
            return (0, half * sizes[pair] + index)

        return pl.BlockSpec((count, HALF_CHUNK), at)

    units = [
        [(pair, sources.index((side, pair))) for side, (pair, _) in enumerate(unit)] for unit in plan
    ]
    left_spec = pl.BlockSpec((count, rows), lambda j, place: (0, 0))
    return pl.pallas_call(
        lambda *refs: term_kernel(len(pairs), mine, units, *refs),
        grid_spec=pltpu.PrefetchScalarGridSpec(
            num_scalar_prefetch=1,
            grid=(steps,),
            in_specs=[left_spec] * len(pairs) + [right_spec(*source) for source in sources],
            out_specs=pl.BlockSpec((2, 2, rows // 4, CHUNK), lambda j, place: (0, 0, 0, j)),
            scratch_shapes=[pltpu.VMEM((32, rows // 32, count), F32)]
            + [pltpu.VMEM((rows, count), BF16)] * len(pairs),
        ),
        out_shape=jax.ShapeDtypeStruct((2, 2, rows // 4, steps * CHUNK), BF16),
        compiler_params=pltpu.CompilerParams(vmem_limit_bytes=VMEM_ASKED),
        cost_estimate=pl.CostEstimate(flops=1, bytes_accessed=1, transcendentals=0),
    )(place, *[left for left, _ in pairs], *[pairs[pair][1] for _, pair in sources])


def tall_kernel(place, left, right, own, sent, blocks, turned):
    query, _, inner, core = (place[i] for i in range(4))
    width = blocks.shape[1]
    blocks[...] = left[...].astype(F32).T.reshape(blocks.shape)
    for to in range(4):
        source = (to % 2) * 2 + to // 2
        turned[pl.ds(to * width, width), :] = blocks[source].astype(BF16)
    terms = dot(turned[...], right[...]).astype(BF16)
    size = terms.shape[1] // 2
    y_place = (pl.program_id(0) % 2) ^ inner
    for half in range(2):
        for x in range(2):
            x_place = x ^ query
            at = (x_place, y_place) if half == 0 else (y_place, x_place)
            value = terms[2 * x * width : 2 * (x + 1) * width, half * size : (half + 1) * size]

            @pl.when(core == half)
            def _():
                own[at[0], at[1], 0] = value

            @pl.when(core != half)
            def _():
                sent[at[0], at[1], 0] = value


def tall_terms(place, left, right, outer):
    count, rows = left.shape
    columns = right.shape[1]
    wide = rows // (2 * outer)
    shape = (2, 2, outer, wide // 2, columns // 2)
    out = pl.BlockSpec(
        (2, 2, 1, wide // 2, columns // 2), lambda j, place: (0, 0, j // 2, 0, 0)
    )
    own, sent = pl.pallas_call(
        tall_kernel,
        grid_spec=pltpu.PrefetchScalarGridSpec(
            num_scalar_prefetch=1,
            grid=(2 * outer,),
            in_specs=[
                pl.BlockSpec((count, wide), lambda j, place: (0, j)),
                pl.BlockSpec((count, columns), lambda j, place: (0, 0)),
            ],
            out_specs=[out, out],
            scratch_shapes=[
                pltpu.VMEM((4, wide // 4, count), F32),
                pltpu.VMEM((wide, count), BF16),
            ],
        ),
        out_shape=[jax.ShapeDtypeStruct(shape, BF16)] * 2,
        compiler_params=pltpu.CompilerParams(vmem_limit_bytes=VMEM_ASKED),
        cost_estimate=pl.CostEstimate(flops=1, bytes_accessed=1, transcendentals=0),
    )(place, left, right)
    flat = (2, 2, outer * wide // 2, columns // 2)
    return own.reshape(flat), sent.reshape(flat)


def small_cost():
    return pl.CostEstimate(flops=1, bytes_accessed=1, transcendentals=0)


def add_kernel(count, *refs):
    ins, outs = refs[: len(refs) - count], refs[len(refs) - count :]
    each = len(ins) // count
    for i, out in enumerate(outs):
        total = ins[i * each][...].astype(F32)
        for other in ins[i * each + 1 : (i + 1) * each]:
            total = total + other[...].astype(F32)
        out[...] = total.astype(BF16)


def add_call(*groups):
    first, _ = groups[0][0]
    rows, columns = first.shape[-2:]
    steps = 2
    size = rows // steps
    specs, arrays = [], []
    for group in groups:
        for array, at in group:
            lead = (None,) * len(at)
            specs.append(
                pl.BlockSpec((*lead, size, columns), lambda r, at=at: (*at, r, 0))
            )
            arrays.append(array)
    out = pl.BlockSpec((size, columns), lambda r: (r, 0))
    shape = jax.ShapeDtypeStruct((rows, columns), BF16)
    return pl.pallas_call(
        lambda *refs: add_kernel(len(groups), *refs),
        grid=(steps,),
        in_specs=specs,
        out_specs=[out] * len(groups),
        out_shape=[shape] * len(groups),
        compiler_params=pltpu.CompilerParams(vmem_limit_bytes=VMEM_ASKED),
        cost_estimate=small_cost(),
    )(*arrays)


def first_kernel(own, got, out):
    out[...] = (own[...].astype(F32) + got[...].astype(F32)).astype(BF16)


def add_first_call(own, got):
    rows, columns = own.shape[-2:]
    steps = 2
    size = rows // steps
    half = pl.BlockSpec((None, 2, size, columns), lambda r: (1, 0, r, 0))
    return pl.pallas_call(
        first_kernel,
        grid=(steps,),
        in_specs=[half, half],
        out_specs=pl.BlockSpec((2, size, columns), lambda r: (0, r, 0)),
        out_shape=jax.ShapeDtypeStruct((2, rows, columns), BF16),
        compiler_params=pltpu.CompilerParams(vmem_limit_bytes=VMEM_ASKED),
        cost_estimate=small_cost(),
    )(own, got)


def out_kernel(mixed, weight, tokens, bias, gain, shift, middle, second):
    values = tokens[...].astype(F32) + dot(mixed[...], weight[...]) + bias[...]
    middle[...] = values
    second[...] = layer_norm(values, gain[...], shift[...]).astype(BF16)


def attend_out(mixed, weight, tokens, bias, gain, shift):
    count = tokens.shape[0]
    size = 256
    row = pl.BlockSpec((size, D), lambda r: (r, 0))
    vector = pl.BlockSpec((1, D), lambda r: (0, 0))
    whole = pl.BlockSpec((D, D), lambda r: (0, 0))
    return pl.pallas_call(
        out_kernel,
        grid=(count // size,),
        in_specs=[row, whole, row, vector, vector, vector],
        out_specs=[row, row],
        out_shape=[
            jax.ShapeDtypeStruct((count, D), F32),
            jax.ShapeDtypeStruct((count, D), BF16),
        ],
        compiler_params=pltpu.CompilerParams(vmem_limit_bytes=VMEM_ASKED),
        cost_estimate=small_cost(),
    )(mixed, weight, tokens, bias[None, :], gain[None, :], shift[None, :])


def spread_kernel(left, right, out):
    out[...] = dot(left[...], right[...]).astype(BF16)


def spread(left, right):
    count, depth = left.shape
    columns = right.shape[1]
    return pl.pallas_call(
        spread_kernel,
        grid=(columns // CHUNK,),
        in_specs=[
            pl.BlockSpec((count, depth), lambda j: (0, 0)),
            pl.BlockSpec((depth, CHUNK), lambda j: (0, j)),
        ],
        out_specs=pl.BlockSpec((count, CHUNK), lambda j: (0, j)),
        out_shape=jax.ShapeDtypeStruct((count, columns), BF16),
        compiler_params=pltpu.CompilerParams(vmem_limit_bytes=VMEM_ASKED),
        cost_estimate=small_cost(),
    )(left, right)


def gather_kernel(left, right, out, total):
    terms = dot_rt(left[...], right[...])
    step = pl.program_id(0)

    @pl.when(step == 0)
    def _():
        total[...] = terms

    @pl.when(step > 0)
    def _():
        total[...] += terms

    @pl.when(step == pl.num_programs(0) - 1)
    def _():
        out[...] = total[...].astype(BF16)


def gather(left, right):
    count, columns = left.shape
    rows = right.shape[0]
    return pl.pallas_call(
        gather_kernel,
        grid=(columns // CHUNK,),
        in_specs=[
            pl.BlockSpec((count, CHUNK), lambda j: (0, j)),
            pl.BlockSpec((rows, CHUNK), lambda j: (0, j)),
        ],
        out_specs=pl.BlockSpec((count, rows), lambda j: (0, 0)),
        out_shape=jax.ShapeDtypeStruct((count, rows), BF16),
        scratch_shapes=[pltpu.VMEM((count, rows), F32)],
        compiler_params=pltpu.CompilerParams(vmem_limit_bytes=VMEM_ASKED),
        cost_estimate=small_cost(),
    )(left, right)


def norm_terms(values, grad, gain):
    center = values - jnp.mean(values, axis=-1, keepdims=True)
    spread = jnp.mean(center * center, axis=-1, keepdims=True)
    rise = lax.rsqrt(spread + EPSILON)
    unit = center * rise
    scaled = grad * gain
    first = jnp.mean(scaled, axis=-1, keepdims=True)
    second = jnp.mean(scaled * unit, axis=-1, keepdims=True)
    return (
        (scaled - first - unit * second) * rise,
        jnp.sum(grad * unit, axis=0, keepdims=True),
        jnp.sum(grad, axis=0, keepdims=True),
    )


def out_back_kernel(
    grad, middle, gain, flat, weight, grad_middle, low, back, gain_sum, shift_sum
):
    part, by_gain, by_shift = norm_terms(middle[...], grad[...], gain[...])
    total = flat[...] + part
    grad_middle[...] = total
    low[...] = total.astype(BF16)
    back[...] = dot_rt(total.astype(BF16), weight[...]).astype(BF16)

    @pl.when(pl.program_id(0) == 0)
    def _():
        gain_sum[...] = jnp.zeros_like(gain_sum)
        shift_sum[...] = jnp.zeros_like(shift_sum)

    gain_sum[...] += by_gain
    shift_sum[...] += by_shift


def attend_out_back(grad, middle, gain, flat, weight):
    count = grad.shape[0]
    size = 256
    row = pl.BlockSpec((size, D), lambda r: (r, 0))
    vector = pl.BlockSpec((1, D), lambda r: (0, 0))
    whole = pl.BlockSpec((D, D), lambda r: (0, 0))
    wide = jax.ShapeDtypeStruct((count, D), F32)
    low = jax.ShapeDtypeStruct((count, D), BF16)
    return pl.pallas_call(
        out_back_kernel,
        grid=(count // size,),
        in_specs=[row, row, vector, row, whole],
        out_specs=[row, row, row, vector, vector],
        out_shape=[wide, low, low] + [jax.ShapeDtypeStruct((1, D), F32)] * 2,
        compiler_params=pltpu.CompilerParams(vmem_limit_bytes=VMEM_ASKED),
        cost_estimate=small_cost(),
    )(grad, middle, gain[None, :], flat, weight)


def tokens_back_kernel(grad, tokens, gain, flat, out, gain_sum, shift_sum):
    part, by_gain, by_shift = norm_terms(tokens[...].astype(F32), grad[...], gain[...])
    out[...] = flat[...] + part

    @pl.when(pl.program_id(0) == 0)
    def _():
        gain_sum[...] = jnp.zeros_like(gain_sum)
        shift_sum[...] = jnp.zeros_like(shift_sum)

    gain_sum[...] += by_gain
    shift_sum[...] += by_shift


def tokens_back(grad, tokens, gain, flat):
    count = grad.shape[0]
    size = 256
    row = pl.BlockSpec((size, D), lambda r: (r, 0))
    vector = pl.BlockSpec((1, D), lambda r: (0, 0))
    return pl.pallas_call(
        tokens_back_kernel,
        grid=(count // size,),
        in_specs=[row, row, vector, row],
        out_specs=[row, vector, vector],
        out_shape=[jax.ShapeDtypeStruct((count, D), F32)]
        + [jax.ShapeDtypeStruct((1, D), F32)] * 2,
        compiler_params=pltpu.CompilerParams(vmem_limit_bytes=VMEM_ASKED),
        cost_estimate=small_cost(),
    )(grad, tokens, gain[None, :], flat)


def assemble_kernel(pieces, width, count, place_ref, *refs):
    sources, full, sems = refs[:count], refs[count], refs[count + 1]
    step = pl.program_id(0)
    copies = []
    for i, (source, row, rows, column) in enumerate(pieces):
        start = pl.multiple_of(place_ref[i], 16)
        columns = pl.ds(pl.multiple_of(column + step * width, 128), width)
        copies.append(
            pltpu.make_async_copy(
                sources[source].at[pl.ds(row, rows), columns],
                full.at[pl.ds(start, rows), :],
                sems.at[i],
            )
        )
    for copy in copies:
        copy.start()
    for copy in copies:
        copy.wait()


def assemble(sources, pieces, places, shape, width):
    count = len(sources)
    rows, columns = shape
    return pl.pallas_call(
        lambda *refs: assemble_kernel(pieces, width, count, *refs),
        grid=(columns // width,),
        out_shape=jax.ShapeDtypeStruct(shape, BF16),
        in_specs=[pl.BlockSpec(memory_space=pltpu.SMEM)]
        + [pl.BlockSpec(memory_space=pl.ANY)] * count,
        out_specs=pl.BlockSpec((rows, width), lambda j: (0, j)),
        scratch_shapes=[pltpu.SemaphoreType.DMA((len(pieces),))],
        compiler_params=pltpu.CompilerParams(vmem_limit_bytes=32 << 20),
        cost_estimate=pl.CostEstimate(flops=1, bytes_accessed=1, transcendentals=0),
    )(jnp.stack(places).astype(jnp.int32), *sources)


def sync(*values):
    return lax.optimization_barrier(values)


def tie(value, *others):
    return lax.optimization_barrier((value, others))[0] if others else value


class Grid:
    def __init__(self, mesh):
        dp, query = mesh.shape["dp"], mesh.shape["query"]
        core = 2 if dp % 2 == 0 else 1
        rest = dp // core
        outer = 4 if rest % 4 == 0 else rest
        inner = rest // outer
        self.dp, self.query = dp, query
        self.size = {"z": outer, "y": inner, "c": core, "x": query}
        self.stride = {"z": inner * core, "y": core, "c": 1}
        self.order = ["z", "y", "c", "x"]

    def paired(self):
        size = self.size
        pairs = size["x"] == 2 and size["y"] == 2 and size["c"] == 2
        return pairs and size["z"] == 4 and D % (self.dp * self.query * 8) == 0

    def place(self, axis):
        if axis == "zb":
            return self.place("z") % 2
        if axis == "zh":
            return self.place("z") // 2
        if axis == "x":
            return lax.axis_index("query")
        return (lax.axis_index("dp") // self.stride[axis]) % self.size[axis]

    def partner(self, axis, at, step):
        size = self.size[axis]
        return at ^ step if size & (size - 1) == 0 else (at + step) % size

    def sender(self, axis, at, step):
        size = self.size[axis]
        return at ^ step if size & (size - 1) == 0 else (at + size - step) % size

    def hop(self, value, axis, step=1):
        if axis == "x":
            pairs = [(i, self.partner("x", i, step)) for i in range(self.query)]
            return lax.ppermute(value, "query", pairs)
        stride, size = self.stride[axis], self.size[axis]
        pairs = []
        for i in range(self.dp):
            at = (i // stride) % size
            pairs.append((i, i + (self.partner(axis, at, step) - at) * stride))
        return lax.ppermute(value, "dp", pairs)

    def turn_hop(self, value, turn):
        pairs = []
        for i in range(self.dp):
            core = i % 2
            y = (i // self.stride["y"]) % 2
            for x in range(2):
                if core == turn:
                    to = i * 2 + 1 - x
                else:
                    to = (i + (1 - 2 * y) * self.stride["y"]) * 2 + x
                pairs.append((i * 2 + x, to))
        return lax.ppermute(value, ("dp", "query"), pairs)

    def share(self, value, axis=0, after=()):
        if self.query == 1:
            return value
        if self.query != 2:
            return lax.all_gather(value, "query", axis=axis, tiled=True)
        other = tie(self.hop(value, "x"), *after)
        first = lax.axis_index("query") == 0
        return jnp.concatenate(
            [jnp.where(first, value, other), jnp.where(first, other, value)], axis=axis
        )

    def joined_along(self, mine, other, axis):
        first = self.place(axis) == 0
        return jnp.concatenate(
            [jnp.where(first, mine, other), jnp.where(first, other, mine)], axis=0
        )

    def cut_half(self, value, axis):
        half = value.shape[1] // 2
        first = self.place(axis) == 0
        left, right = value[:, :half], value[:, half:]
        return jnp.where(first, left, right), jnp.where(first, right, left)

    def cut_fold(self, value, step):
        bits = value.reshape(value.shape[0] // 2, 2, *value.shape[1:])
        me = self.place("z") // step % 2
        return (
            lax.dynamic_index_in_dim(bits, me, axis=1, keepdims=False),
            lax.dynamic_index_in_dim(bits, 1 - me, axis=1, keepdims=False),
        )

    def joined(self, mine, other, axis=0):
        first = lax.axis_index("query") == 0
        return jnp.concatenate(
            [jnp.where(first, mine, other), jnp.where(first, other, mine)], axis=axis
        )

    def total(self, value):
        if self.query == 1:
            return value
        if self.query != 2:
            return lax.psum(value, "query")
        return value + self.hop(value, "x")

    def cut_step(self, value, axis, dim):
        me = self.place(axis)
        return (
            lax.dynamic_index_in_dim(value, me, axis=dim, keepdims=False),
            lax.dynamic_index_in_dim(value, 1 - me, axis=dim, keepdims=False),
        )

    def cut_columns(self, terms):
        half = terms.shape[1] // 2
        first = self.place("c") == 0
        left, right = terms[:, :half], terms[:, half:]
        return jnp.where(first, left, right), jnp.where(first, right, left)

    def trade(self, value, axis, dim, column):
        mine, other = self.cut_step(value, axis, dim)
        got = self.hop(other, axis) if axis != "zh" else self.hop(other, "z", 2)
        first = self.place(axis) == 0
        return jnp.concatenate(
            [jnp.where(first, mine, got), jnp.where(first, got, mine)], axis=column
        )

    def join_columns(self, value):
        value = value.reshape(2, -1, value.shape[-1])
        mine, other = self.cut_step(value, "c", 0)
        got = self.hop(other, "c")
        first = self.place("c") == 0
        return jnp.concatenate(
            [jnp.where(first, mine, got), jnp.where(first, got, mine)], axis=1
        )

    def scatter_step(self, value, axis, dim, kind):
        size = self.size[axis]
        me = self.place(axis)

        def part(index):
            return lax.dynamic_index_in_dim(value, index, axis=dim, keepdims=False)

        if size == 1:
            return part(0)
        sent = [
            self.hop(part(self.partner(axis, me, step)), axis, step) for step in range(1, size)
        ]
        total = part(me).astype(F32)
        for received in sent:
            total = total + received.astype(F32)
        return total.astype(kind)

    def scatter(self, value, order, kind=BF16):
        dims = [axis for axis in self.order if axis in order]
        for axis in order:
            dim = dims.index(axis)
            value = self.scatter_step(value, axis, dim, kind)
            dims.pop(dim)
        return value

    def scatter_z(self, value):
        stride, size = self.stride["z"], self.size["z"]
        groups = [[k * stride + i for k in range(size)] for i in range(stride)]
        return lax.psum_scatter(
            value, "dp", scatter_dimension=0, axis_index_groups=groups, tiled=True
        )

    def scatter_low(self, value):
        stride, size = self.stride["z"], self.size["z"]
        groups = [
            [(high * 2 + low) * stride + i for low in range(2)]
            for high in range(size // 2)
            for i in range(stride)
        ]
        return lax.psum_scatter(
            value, "dp", scatter_dimension=0, axis_index_groups=groups, tiled=True
        )

    def blocks(self, value):
        shape = [self.size[axis] for axis in self.order]
        rows = value.shape[0] // math.prod(shape)
        return value.reshape(*shape, rows, *value.shape[1:])

    def own_columns(self, value):
        width = value.shape[1] // (self.dp * self.query)
        shaped = value.reshape(value.shape[0], self.dp, self.query, width)
        mine = lax.dynamic_index_in_dim(shaped, self.place("x"), axis=2, keepdims=False)
        return mine.reshape(value.shape[0], self.dp * width)

    def part_of(self, shards):
        zb, y, c = self.place("z") % 2, self.place("y"), self.place("c")
        unit = min(shard.shape[0] for shard in shards) // 8
        mine = (zb * 2 + y) * 2 + c
        columns = []
        for shard in shards:
            fold = shard.shape[0] // (8 * unit)
            for k in range(fold):
                columns.append(
                    lax.dynamic_slice_in_dim(shard, (mine * fold + k) * unit, unit, 0)
                )
        return jnp.concatenate(columns, axis=1) if len(columns) > 1 else columns[0]

    def side_hop(self, value, turn):
        pairs = []
        for i in range(self.dp):
            axis = "y" if i % 2 == turn else "z"
            stride = self.stride[axis]
            at = (i // stride) % self.size[axis]
            pairs.append((i, i + ((at ^ 1) - at) * stride))
        return lax.ppermute(value, "dp", pairs)

    def join(self, shard, units, column):
        zb, y, c, x = self.place("z") % 2, self.place("y"), self.place("c"), self.place("x")
        rows, width = shard.shape
        size = rows // 8
        pieces, places = [(0, 0, rows, 0)], [x * rows]
        for i, (zb_, y_, c_) in enumerate(unit_places(zb, y, c)):
            pieces.append((1 + i, 0, size, column))
            places.append((1 - x) * rows + ((zb_ * 2 + y_) * 2 + c_) * size)
        return assemble([shard, *units], pieces, places, (2 * rows, width), 640)

    def places(self):
        return jnp.stack(
            [self.place("x"), self.place("z") % 2, self.place("y"), self.place("c")]
        ).astype(jnp.int32)


def added(*values):
    total = values[0].astype(F32)
    for value in values[1:]:
        total = total + value.astype(F32)
    return total.astype(BF16)


def added_wide(*values):
    total = values[0].astype(F32)
    for value in values[1:]:
        total = total + value.astype(F32)
    return total


class Sums:
    def __init__(self, grid):
        self.grid = grid

    def core(self, *after):
        self.got = self.grid.hop(tie(self.sent, *after), "c")

    def add_first(self, *after):
        own, got = tie((self.own, self.got), *after)
        self.one_in = add_first_call(own, got)

    def add_parts(self, *after):
        own, got = tie((self.own, self.got), *after)
        self.parts = add_call(*[[(own, (1, k)), (got, (1, k))] for k in (1, 0)])

    def go_part(self, part):
        return self.grid.turn_hop(self.parts[part], 0)

    def go_first(self):
        return self.grid.turn_hop(self.one_in, 0)

    def add_second(self, one):
        (self.two_in,) = add_call([(self.own, (0, 1)), (self.got, (0, 1)), one])

    def go_second(self):
        return self.grid.turn_hop(self.two_in, 1)

    def add_last(self, one, two):
        (whole,) = add_call([(self.own, (0, 0)), (self.got, (0, 0)), one, (two, ())])
        size = self.grid.size["z"]
        self.last_in = whole.reshape(size, whole.shape[0] // size, whole.shape[1])

    def last(self):
        self.sum = self.grid.scatter_z(self.last_in)

    def result(self, *after):
        value = tie(self.sum, *after)[0]
        value = value.reshape(2, value.shape[0] // 2, value.shape[1])
        mine, other = self.grid.cut_step(value, "c", 0)
        got = self.grid.hop(other, "c")
        first = self.grid.place("c") == 0
        return [
            jnp.where(first, mine, got).astype(F32),
            jnp.where(first, got, mine).astype(F32),
        ]


def make_shards(grid):
    def shards(
        tokens,
        cell_lengths,
        out_cotangent,
        ln_gains,
        ln_biases,
        proj_biases,
        ff_biases,
        w_qkv,
        w_out,
        w_up,
        w_down,
        dec_cell,
        dec_gene,
        dec_out,
        gene_table,
        query_ids,
        labels,
    ):
        row_count = tokens.shape[0]
        token_count = row_count * ROW_LEN
        dp_count, query_count = grid.dp, grid.query
        place = lax.axis_index("query")
        starts, segment = cell_layout(cell_lengths)
        local_cells = row_count * CELLS_ROW
        pair_cells, local_queries = query_ids.shape
        pairs = pair_cells * local_queries
        half_width = D // query_count

        row_tokens = tokens.reshape(token_count, D)
        where = grid.places()
        ids = grid.share(query_ids.reshape(1, pairs)).reshape(query_count * pairs)
        qkv_first = grid.hop(grid.part_of([w_qkv]), "x")
        normed_low = layer_norm(row_tokens.astype(F32), ln_gains[0], ln_biases[0]).astype(BF16)
        table_rows = gene_table.shape[0]
        local_ids = ids - place * table_rows
        held = (local_ids[:, None] == jnp.arange(table_rows, dtype=jnp.int32)[None, :]).astype(BF16)
        gene_found = dot(held, gene_table).astype(BF16)
        up_part = grid.part_of([w_up, w_out])
        down_part = grid.part_of([w_down])
        qkv_first, normed_low, gene_found, up_part, down_part = sync(
            qkv_first, normed_low, gene_found, up_part, down_part
        )
        up_first = grid.hop(up_part, "x")
        qkv_near = grid.hop(qkv_first, "c")
        qkv_side = grid.side_hop(qkv_first, 0)
        qkv_near, qkv_side = sync(qkv_near, qkv_side)
        qkv_side_two, qkv_corner = grid.side_hop(qkv_near, 0), grid.side_hop(qkv_side, 1)
        qkv_far = grid.hop(qkv_side, "c")
        qkv_side_two, qkv_corner, up_first = sync(qkv_side_two, qkv_corner, up_first)
        up_near = grid.hop(up_first, "c")
        up_side = grid.side_hop(up_first, 0)
        qkv_far_two, qkv_far_corner = grid.hop(qkv_side_two, "c"), grid.hop(qkv_corner, "c")
        qkv_far, qkv_far_two, qkv_far_corner = sync(qkv_far, qkv_far_two, qkv_far_corner)
        gene_hop = grid.hop(gene_found, "x")
        down_first = grid.hop(tie(down_part, up_first), "x")
        qkv_weights = (
            w_qkv, qkv_first, qkv_near, qkv_side, qkv_side_two, qkv_corner,
            qkv_far, qkv_far_two, qkv_far_corner,
        )
        zeroes = jnp.zeros((D,), F32)
        qkv_bias = jnp.concatenate([proj_biases[0], zeroes, proj_biases[1]])
        qkv_low = project(where, normed_low, qkv_bias[None, :], qkv_weights)
        qkv_low, up_near, up_side, gene_hop = sync(qkv_low, up_near, up_side, gene_hop)
        up_side_two, up_corner = grid.side_hop(up_near, 0), grid.side_hop(up_side, 1)
        up_far = grid.hop(up_side, "c")
        qkv_rows = qkv_low.reshape(row_count, ROW_LEN, 3 * D)
        mixed_rows, log_totals = attend(qkv_rows, segment)
        mixed_low = mixed_rows.reshape(token_count, D)
        gene_rows = added(gene_found, tie(gene_hop, mixed_low)) if query_count == 2 else gene_found
        gene_half = lax.dynamic_slice_in_dim(gene_rows, place * half_width, half_width, 1)
        gene_partial = spread(gene_half, dec_gene).reshape(query_count, pairs, FF)
        mixed_low, gene_partial, up_side_two, up_corner, up_far, down_first = sync(
            mixed_low, gene_partial, up_side_two, up_corner, up_far, down_first
        )
        gene_mine, gene_sent = grid.cut_step(gene_partial, "x", 0)
        down_near = grid.hop(down_first, "c")
        down_side = grid.side_hop(down_first, 0)
        up_far_two, up_far_corner = grid.hop(up_side_two, "c"), grid.hop(up_corner, "c")
        up_units = (
            up_first, up_near, up_side, up_side_two, up_corner, up_far, up_far_two, up_far_corner
        )
        up_weights = (w_up, *up_units)
        full_out = grid.join(w_out, up_units, FF)
        middle, second_low = attend_out(
            mixed_low, full_out, row_tokens, proj_biases[2], ln_gains[1], ln_biases[1]
        )
        second_low, down_near, down_side, gene_sent = sync(second_low, down_near, down_side, gene_sent)
        down_side_two, down_corner = grid.side_hop(down_near, 0), grid.side_hop(down_side, 1)
        down_far = grid.hop(down_side, "c")
        gene_got = grid.hop(gene_sent, "x")
        gene_pair = grid.hop(gene_rows, "z", 2)
        active_low, slope = feed_up(where, second_low, ff_biases[0][None, :], up_weights)
        active_low, slope, down_side_two, down_corner, down_far, gene_got, gene_pair = sync(
            active_low, slope, down_side_two, down_corner, down_far, gene_got, gene_pair
        )
        down_far_two, down_far_corner = grid.hop(down_side_two, "c"), grid.hop(down_corner, "c")
        down_weights = (
            w_down, down_first, down_near, down_side, down_side_two, down_corner,
            down_far, down_far_two, down_far_corner,
        )
        places = jnp.arange(ROW_LEN, dtype=jnp.int32)
        picker = (places[None, :, None] == starts[:, None, :]).astype(F32)
        rows_apart = jnp.arange(row_count)
        choice = jnp.where(
            rows_apart[:, None, None, None] == rows_apart[None, None, :, None],
            picker.transpose(0, 2, 1)[:, :, None, :],
            0,
        ).reshape(local_cells, token_count).astype(BF16)
        encoded, heads_low = feed_down(
            where, active_low, middle, proj_biases[3:], choice, down_weights
        )
        encoded_rows = encoded.reshape(row_count, ROW_LEN, D)
        cell_heads = grid.share(heads_low)
        heads_half = lax.dynamic_slice_in_dim(cell_heads, place * half_width, half_width, 1)
        cell_half = dot(heads_half, dec_cell).astype(BF16)
        cell_hop = grid.hop(cell_half, "x") if query_count == 2 else cell_half
        before_low, before_sums, grad_logit = decode(
            cell_half, cell_hop, gene_mine, gene_got, ff_biases[1][None, :], dec_out[None, :], labels
        )
        before_low = before_low.reshape(pair_cells, local_queries, FF)
        cell_total = grid.total(before_sums)
        heads_part = dot_rt(cell_total, dec_cell).astype(BF16)
        heads_all = grid.share(heads_part, axis=1)
        heads_back = lax.dynamic_slice_in_dim(
            heads_all, place * local_cells, local_cells, 0
        ).astype(F32)
        grad_encoded = out_cotangent.astype(F32) + jnp.sum(
            picker[:, :, :, None] * heads_back.reshape(row_count, 1, CELLS_ROW, D), axis=2
        )
        grad_flat = grad_encoded.reshape(token_count, D)
        branch_low = grad_flat.astype(BF16)
        branch_low, before_low = sync(branch_low, before_low)
        before_hop = grid.hop(before_low, "x") if query_count == 2 else before_low
        gathered = lax.all_gather(
            jnp.concatenate([cell_heads, cell_total], axis=1), "dp", axis=0, tiled=True
        )
        down_sums = Sums(grid)
        down_sums.own, down_sums.sent = tall_terms(where, active_low, branch_low, grid.size["z"])
        down_sums.own, down_sums.sent, before_hop = sync(down_sums.own, down_sums.sent, before_hop)
        down_sums.core()
        before_all = grid.joined(before_low, before_hop).reshape(query_count * pairs, FF)
        before_mine, before_sent = grid.cut_half(before_all, "zh")
        before_got = grid.hop(before_sent, "z", 2)
        hidden_low, up_bias_sums, grad_second = feed_back(
            where, tie(branch_low, down_sums.sent, before_sent), slope, up_weights, down_weights
        )
        hidden_low, grad_second, down_sums.got = sync(hidden_low, grad_second, down_sums.got)
        down_sums.add_parts()
        down_sums.parts = sync(*down_sums.parts)
        one, one_more = down_sums.go_part(0), down_sums.go_part(1)
        grad_middle, attn_low, mixed_back, grad_gain_two, grad_shift_two = attend_out_back(
            tie(grad_second, down_sums.parts), middle, ln_gains[1], grad_flat, full_out
        )
        gene_wide = grid.joined_along(gene_rows, gene_pair, "zh")
        before_wide = grid.joined_along(before_mine, tie(before_got, mixed_back), "zh")
        gene_left = grid.own_columns(gene_wide).reshape(gene_wide.shape[0], 2, 2, -1)
        gene_left = gene_left.transpose(0, 2, 1, 3).reshape(gene_wide.shape[0], -1)
        gene_half = before_wide.shape[1] // 2
        core = grid.place("c")
        gene_mine, gene_sent = [
            dot_lt(
                gene_left,
                lax.dynamic_slice_in_dim(before_wide, at * gene_half, gene_half, 1),
            ).astype(BF16)
            for at in (core, 1 - core)
        ]
        gene_got = grid.hop(gene_sent, "c")
        up_sums = Sums(grid)
        up_sums.sent = weight_terms(where, False, (second_low, tie(hidden_low, mixed_back, gene_sent)))
        up_sums.own = weight_terms(where, True, (second_low, tie(hidden_low, up_sums.sent)))
        up_sums.sent, up_sums.own, one, one_more, gene_got, gathered = sync(
            up_sums.sent, up_sums.own, one, one_more, gene_got, gathered
        )
        up_sums.core()
        down_sums.add_second((one, ()))
        two = down_sums.go_second()
        (gene_sum,) = add_call([(gene_mine, ()), (tie(gene_got, down_sums.two_in), ())])
        genes_part = gather(tie(before_all, gene_sum), dec_gene)
        choose = (
            tie(ids, genes_part)[:, None] == jnp.arange(GENES, dtype=jnp.int32)[None, :]
        ).astype(BF16)
        table_terms = dot_lt(choose, genes_part).astype(BF16)
        shape = [grid.size[axis] for axis in "zycx"]
        table_terms = table_terms.reshape(*shape, -1, half_width)
        table_mine, table_sent = grid.cut_step(table_terms, "c", 2)
        mixed_back, up_sums.got, gene_sum, table_mine, table_sent = sync(
            mixed_back, up_sums.got, gene_sum, table_mine, table_sent
        )
        gene_sum = grid.scatter_low(gene_sum)
        table_got = grid.hop(table_sent, "c")
        up_sums.add_first()
        up_sums.one_in, mixed_back, two = sync(up_sums.one_in, mixed_back, two)
        up_one = up_sums.go_first()
        qkv_back = attend_back(
            qkv_rows,
            segment,
            mixed_rows,
            mixed_back.reshape(row_count, ROW_LEN, D),
            log_totals,
        )
        qkv_back, table_got = sync(qkv_back, table_got)
        down_sums.add_last((one_more, ()), two)
        down_sums.last()
        qkv_back_low = qkv_back.reshape(token_count, 3 * D)
        attn_sums = Sums(grid)
        attn_sums.sent = weight_terms(
            where,
            False,
            (normed_low, tie(qkv_back_low, down_sums.last_in)),
            (mixed_low, attn_low),
        )
        attn_sums.sent, qkv_back_low, up_one, gene_sum = sync(
            attn_sums.sent, qkv_back_low, up_one, gene_sum
        )
        up_sums.add_second((up_one, (1,)))
        up_two = up_sums.go_second()
        attn_sums.core()
        attn_sums.own = weight_terms(
            where, True, (normed_low, tie(qkv_back_low, up_sums.two_in)), (mixed_low, attn_low)
        )
        attn_sums.own, attn_sums.got = sync(attn_sums.own, attn_sums.got)
        attn_sums.add_first()
        attn_sums.one_in, qkv_back_low, up_two = sync(attn_sums.one_in, qkv_back_low, up_two)
        one = attn_sums.go_first()
        table_mine, table_sent = grid.cut_fold(added(tie(table_mine, attn_sums.one_in), table_got), 1)
        table_got = grid.hop(table_sent, "z", 1)
        grad_normed = project_back(where, qkv_back_low, qkv_weights)
        grad_normed, down_sums.sum = sync(grad_normed, down_sums.sum)
        up_sums.add_last((up_one, (0,)), up_two)
        up_sums.last()
        grad_tokens, grad_gain_one, grad_shift_one = tokens_back(
            tie(grad_normed, up_sums.last_in), row_tokens, ln_gains[0], grad_middle
        )
        one, grad_tokens, table_got = sync(one, grad_tokens, table_got)
        attn_sums.add_second((one, (1,)))
        two = attn_sums.go_second()

        table_mine, table_sent = grid.cut_fold(added(tie(table_mine, attn_sums.two_in), table_got), 2)
        table_got = grid.hop(table_sent, "z", 2)
        grad_tokens = grad_tokens.reshape(row_count, ROW_LEN, D)
        late_ties = (qkv_back_low, attn_low, branch_low, up_bias_sums, before_sums)
        qkv_late, attn_late, branch_late, up_bias_sums, sums_late = tie(late_ties, attn_sums.two_in)
        grad_up_bias = up_bias_sums[0]
        bias_sums = jnp.sum(qkv_late, axis=0, dtype=F32)
        grad_attn_bias = jnp.sum(attn_late, axis=0, dtype=F32)
        grad_out_bias = jnp.sum(branch_late, axis=0, dtype=F32)
        grad_dec_bias = jnp.sum(sums_late, axis=0, dtype=F32)
        owners = dp_count * query_count

        def owned_cols(values):
            return values.reshape(-1, owners, values.shape[-1] // owners).transpose(1, 0, 2).reshape(owners, -1)

        small = [
            jnp.concatenate([grad_gain_one, grad_gain_two]),
            jnp.concatenate([grad_shift_one, grad_shift_two]),
            jnp.stack([bias_sums[:D], bias_sums[2 * D :], grad_attn_bias, grad_out_bias]),
            jnp.stack([grad_up_bias, grad_dec_bias]),
            grad_logit,
        ]
        flat = [owned_cols(value) for value in small]
        sums = grid.scatter_step(grid.blocks(jnp.concatenate(flat, axis=1)), "c", 2, F32)
        sums, table_got, two, up_sums.sum = sync(sums, table_got, two, up_sums.sum)
        attn_sums.add_last((one, (0,)), two)
        attn_sums.last()

        sums, table_got, gene_sum = tie((sums, table_got, gene_sum), attn_sums.last_in)
        sums = grid.scatter_step(sums, "x", 2, F32)
        table_sum = grid.scatter_step(added(table_mine, table_got)[0], "y", 0, BF16)
        gene_sum = grid.scatter_step(
            gene_sum.reshape(2, grid.size["y"], -1, gene_sum.shape[-1]), "y", 1, BF16
        )
        up_result, down_result = up_sums.result(attn_sums.last_in), down_sums.result(attn_sums.last_in)
        sums, table_sum, gene_sum, up_result, down_result = sync(
            sums, table_sum, gene_sum, up_result, down_result
        )
        sums = grid.scatter_step(sums, "y", 1, F32)
        gene_sum = grid.trade(gene_sum.reshape(2, 2, -1, gene_sum.shape[-1]), "c", 1, 2)
        grad_table = grid.trade(table_sum, "x", 0, 1).astype(F32)
        sums, grad_table, gene_sum = sync(sums, grad_table, gene_sum)
        summed = grid.scatter_step(sums, "z", 0, F32).reshape(-1)
        grad_gene = grid.trade(gene_sum, "zh", 0, 1).astype(F32)
        all_heads, all_cells = jnp.split(tie(gathered, attn_sums.last_in), [D], axis=1)
        owned = D // (dp_count * query_count)
        mine = lax.axis_index("dp") * query_count + place
        grad_cell = dot_lt(
            lax.dynamic_slice_in_dim(all_heads, mine * owned, owned, 1), all_cells
        )
        outs = []
        start = 0
        for value, piece in zip(small, flat):
            size = piece.shape[1]
            outs.append(summed[start : start + size].reshape(value.shape[0], -1))
            start += size

        attn_sum = attn_sums.result()
        qkv_cut = 3 * D // 2

        return (
            encoded_rows,
            grad_tokens,
            outs[0],
            outs[1],
            outs[2],
            outs[3],
            jnp.concatenate([half[:, :qkv_cut] for half in attn_sum], axis=1),
            jnp.concatenate([half[:, qkv_cut:] for half in attn_sum], axis=1),
            jnp.concatenate(up_result, axis=1),
            jnp.concatenate(down_result, axis=1),
            grad_cell,
            grad_gene,
            outs[4][0],
            grad_table,
        )

    return shards


def split_heads(qkv_row):
    queries = qkv_row[:, :D].reshape(ROW_LEN, HEADS, HEAD_DIM)
    keys_in = qkv_row[:, D : 2 * D].reshape(ROW_LEN, HEADS, HEAD_DIM)
    values_in = qkv_row[:, 2 * D :].reshape(ROW_LEN, HEADS, HEAD_DIM)
    return (queries, keys_in, values_in)


def row_scores(queries, keys_in, segment_row):
    scores = jnp.einsum("qhd,khd->hqk", queries, keys_in, preferred_element_type=jnp.float32) * (
        1.0 / math.sqrt(HEAD_DIM)
    )
    same_cell = segment_row[:, None] == segment_row[None, :]
    return jnp.where(same_cell[None], scores, -1e30)


def attend_any(member):
    qkv_row, segment_row = member
    queries, keys_in, values_in = split_heads(qkv_row)
    scores = row_scores(queries, keys_in, segment_row)
    highest_score = jnp.max(scores, axis=-1, keepdims=True)
    weights = jnp.exp(scores - highest_score)
    weight_sum = jnp.sum(weights, axis=-1, keepdims=True)
    attention = (weights / weight_sum).astype(jnp.bfloat16)
    mixed = jnp.einsum(
        "hqk,khd->qhd", attention, values_in, preferred_element_type=jnp.float32
    ).astype(jnp.bfloat16)
    return (mixed.reshape(ROW_LEN, D), (highest_score + jnp.log(weight_sum))[:, :, 0])


def attend_back_any(member):
    qkv_row, segment_row, log_total, grad_mixed = member
    queries, keys_in, values_in = split_heads(qkv_row)
    scores = row_scores(queries, keys_in, segment_row)
    attention = jnp.exp(scores - log_total[:, :, None])
    grad_heads = grad_mixed.reshape(ROW_LEN, HEADS, HEAD_DIM)
    grad_probs = jnp.einsum(
        "qhd,khd->hqk", grad_heads, values_in, preferred_element_type=jnp.float32
    )
    grad_scores = (
        attention * (grad_probs - jnp.sum(attention * grad_probs, axis=-1, keepdims=True))
    ).astype(jnp.bfloat16)
    scale_factor = 1.0 / math.sqrt(HEAD_DIM)
    grad_query = (
        jnp.einsum("hqk,khd->qhd", grad_scores, keys_in, preferred_element_type=jnp.float32)
        * scale_factor
    )
    grad_keys = (
        jnp.einsum("hqk,qhd->khd", grad_scores, queries, preferred_element_type=jnp.float32)
        * scale_factor
    )
    grad_values = jnp.einsum(
        "hqk,qhd->khd",
        attention.astype(jnp.bfloat16),
        grad_heads,
        preferred_element_type=jnp.float32,
    )
    return jnp.concatenate(
        [
            grad_query.reshape(ROW_LEN, D),
            grad_keys.reshape(ROW_LEN, D),
            grad_values.reshape(ROW_LEN, D),
        ],
        axis=1,
    )


def owned_cols(values_in, dp_count, query_count, place):
    width = values_in.shape[1] // (dp_count * query_count)
    shaped = values_in.reshape(values_in.shape[0], dp_count, query_count, width)
    return lax.dynamic_index_in_dim(shaped, place, axis=2, keepdims=False)


def owned_term(left, right, dp_count, query_count, place):
    return jnp.einsum(
        "ndr,ne->dre",
        owned_cols(left, dp_count, query_count, place),
        right,
        preferred_element_type=jnp.float32,
    )


def owner_blocks(values_in, dp_count, query_count):
    width = values_in.shape[0] // (dp_count * query_count)
    return values_in.reshape(dp_count, query_count, width, values_in.shape[1])


def shards_any(
    tokens,
    cell_lengths,
    out_cotangent,
    ln_gains,
    ln_biases,
    proj_biases,
    ff_biases,
    w_qkv,
    w_out,
    w_up,
    w_down,
    dec_cell,
    dec_gene,
    dec_out,
    gene_table,
    query_ids,
    labels,
):
    row_count = tokens.shape[0]
    token_count = row_count * ROW_LEN
    dp_count = lax.axis_size("dp")
    query_count = lax.axis_size("query")
    place = lax.axis_index("query")
    starts, segment = cell_layout(cell_lengths)
    gathered = (
        lax.all_gather(w_qkv, "query", axis=0, tiled=True),
        lax.all_gather(w_out, "query", axis=0, tiled=True),
        lax.all_gather(w_up, "query", axis=0, tiled=True),
        lax.all_gather(w_down, "query", axis=0, tiled=True),
        lax.all_gather(dec_cell, "query", axis=0, tiled=True),
        lax.all_gather(dec_gene, "query", axis=0, tiled=True),
        lax.all_gather(gene_table, "query", axis=0, tiled=True),
    )
    full_qkv, full_out, full_up, full_down, full_cell, full_gene, full_table = gathered
    flat_tokens = tokens.astype(jnp.float32).reshape(token_count, D)
    normed, first_pull = jax.vjp(layer_norm, flat_tokens, ln_gains[0], ln_biases[0])
    normed_low = normed.astype(jnp.bfloat16)
    zeroes = jnp.zeros((D,), jnp.float32)
    qkv_bias = jnp.concatenate([proj_biases[0], zeroes, proj_biases[1]])
    qkv_low = (jnp.dot(normed_low, full_qkv, preferred_element_type=jnp.float32) + qkv_bias).astype(
        jnp.bfloat16
    )
    qkv_rows = qkv_low.reshape(row_count, ROW_LEN, 3 * D)
    mixed_rows, log_totals = lax.map(attend_any, (qkv_rows, segment))
    mixed_low = mixed_rows.reshape(token_count, D)
    middle = (
        flat_tokens
        + jnp.dot(mixed_low, full_out, preferred_element_type=jnp.float32)
        + proj_biases[2]
    )
    second, second_pull = jax.vjp(layer_norm, middle, ln_gains[1], ln_biases[1])
    second_low = second.astype(jnp.bfloat16)
    hidden = jnp.dot(second_low, full_up, preferred_element_type=jnp.float32) + ff_biases[0]
    active, active_pull = jax.vjp(smooth_gate, hidden)
    active_low = active.astype(jnp.bfloat16)
    encoded = (
        middle + jnp.dot(active_low, full_down, preferred_element_type=jnp.float32) + proj_biases[3]
    )
    places = jnp.arange(ROW_LEN, dtype=jnp.int32)
    picker = (places[None, None, :] == starts[:, :, None]).astype(jnp.float32)
    local_cells = row_count * CELLS_ROW
    heads_low = (
        jnp.einsum(
            "rcl,rld->rcd", picker, encoded.reshape(row_count, ROW_LEN, D), precision=HIGHEST
        )
        .reshape(local_cells, D)
        .astype(jnp.bfloat16)
    )
    cell_heads = lax.all_gather(heads_low, "query", axis=0, tiled=True)
    cell_part = jnp.dot(cell_heads, full_cell, preferred_element_type=jnp.float32)
    gene_rows = jnp.take(full_table, query_ids, axis=0)
    before = (
        cell_part[:, None, :]
        + jnp.einsum("cqd,df->cqf", gene_rows, full_gene, preferred_element_type=jnp.float32)
        + ff_biases[1]
    )
    gated_dec, gated_pull = jax.vjp(smooth_gate, before)
    logit_weight = dec_out.astype(jnp.float32)
    logits = jnp.einsum("cqf,f->cq", gated_dec, logit_weight, precision=HIGHEST)
    logit_slope = jax.nn.sigmoid(logits) - labels.astype(jnp.float32)
    (grad_before,) = gated_pull(logit_slope[:, :, None] * logit_weight)
    before_low = grad_before.astype(jnp.bfloat16)
    grad_dec_bias = jnp.sum(before_low, axis=(0, 1), dtype=jnp.float32)
    grad_logit = jnp.einsum("cqf,cq->f", gated_dec, logit_slope, precision=HIGHEST)
    gene_terms = jnp.einsum(
        "cqd,cqf->df", gene_rows, before_low, preferred_element_type=jnp.float32
    )
    genes_back = jnp.einsum(
        "cqf,df->cqd", before_low, full_gene, preferred_element_type=jnp.float32
    ).astype(jnp.bfloat16)
    choose = (query_ids.reshape(-1)[:, None] == jnp.arange(GENES, dtype=jnp.int32)[None, :]).astype(
        jnp.bfloat16
    )
    table_terms = jnp.einsum(
        "ng,nd->gd", choose, genes_back.reshape(-1, D), preferred_element_type=jnp.float32
    )
    gene_parts, table_parts = (
        lax.all_to_all(
            owner_blocks(gene_terms, dp_count, query_count).astype(jnp.bfloat16),
            "query",
            split_axis=1,
            concat_axis=1,
            tiled=True,
        ).astype(jnp.float32),
        lax.all_to_all(
            owner_blocks(table_terms, dp_count, query_count).astype(jnp.bfloat16),
            "query",
            split_axis=1,
            concat_axis=1,
            tiled=True,
        ).astype(jnp.float32),
    )
    grad_gene = jnp.sum(gene_parts, axis=1)
    grad_table = jnp.sum(table_parts, axis=1)
    cell_total = lax.psum(
        jnp.sum(before_low, axis=1, dtype=jnp.float32).astype(jnp.bfloat16), "query"
    )
    grad_cell = owned_term(cell_heads, cell_total, dp_count, query_count, place)
    heads_all = jnp.einsum("cf,df->cd", cell_total, full_cell, preferred_element_type=jnp.float32)
    heads_back = (
        lax.dynamic_slice_in_dim(heads_all, place * local_cells, local_cells, 0)
        .astype(jnp.bfloat16)
        .astype(jnp.float32)
    )
    grad_encoded = out_cotangent.astype(jnp.float32) + jnp.einsum(
        "rcl,rcd->rld", picker, heads_back.reshape(row_count, CELLS_ROW, D), precision=HIGHEST
    )
    grad_flat = grad_encoded.reshape(token_count, D)

    def empty_term(left_width, right_width):
        return jnp.zeros(
            (dp_count, left_width // (dp_count * query_count), right_width), jnp.float32
        )

    branch_low = grad_flat.astype(jnp.bfloat16)
    grad_out_bias = jnp.sum(branch_low, axis=0, dtype=jnp.float32)
    grad_active = jnp.einsum("nd,fd->nf", branch_low, full_down, preferred_element_type=jnp.float32)
    (grad_hidden,) = active_pull(grad_active)
    hidden_low = grad_hidden.astype(jnp.bfloat16)
    grad_up_bias = jnp.sum(hidden_low, axis=0, dtype=jnp.float32)
    grad_second = jnp.einsum("nf,df->nd", hidden_low, full_up, preferred_element_type=jnp.float32)
    middle_part, grad_gain_two, grad_shift_two = second_pull(grad_second)
    grad_middle = grad_flat + middle_part
    ff_terms = jnp.stack([grad_up_bias, grad_dec_bias], axis=1)
    attn_low = grad_middle.astype(jnp.bfloat16)
    grad_attn_bias = jnp.sum(attn_low, axis=0, dtype=jnp.float32)
    mixed_back = jnp.einsum(
        "ne,de->nd", attn_low, full_out, preferred_element_type=jnp.float32
    ).astype(jnp.bfloat16)
    qkv_back = lax.map(
        attend_back_any, (qkv_rows, segment, log_totals, mixed_back.reshape(row_count, ROW_LEN, D))
    )
    qkv_back_low = qkv_back.reshape(token_count, 3 * D).astype(jnp.bfloat16)
    bias_sums = jnp.sum(qkv_back_low, axis=0, dtype=jnp.float32)
    grad_normed = jnp.einsum(
        "ne,de->nd", qkv_back_low, full_qkv, preferred_element_type=jnp.float32
    )
    token_part, grad_gain_one, grad_shift_one = first_pull(grad_normed)
    grad_tokens = (grad_middle + token_part).reshape(row_count, ROW_LEN, D)
    gain_terms = jnp.stack([grad_gain_one, grad_gain_two], axis=1)
    shift_terms = jnp.stack([grad_shift_one, grad_shift_two], axis=1)
    proj_terms = jnp.stack(
        [bias_sums[:D], bias_sums[2 * D :], grad_attn_bias, grad_out_bias], axis=1
    )
    totals = (empty_term(D, 3 * D), empty_term(D, D), empty_term(D, FF), empty_term(FF, D))
    pieces = (
        lax.all_gather(normed_low, "query", axis=0, tiled=True),
        lax.all_gather(qkv_back_low, "query", axis=0, tiled=True),
        lax.all_gather(mixed_low, "query", axis=0, tiled=True),
        lax.all_gather(attn_low, "query", axis=0, tiled=True),
        lax.all_gather(second_low, "query", axis=0, tiled=True),
        lax.all_gather(hidden_low, "query", axis=0, tiled=True),
        lax.all_gather(active_low, "query", axis=0, tiled=True),
        lax.all_gather(branch_low, "query", axis=0, tiled=True),
    )
    every_fold = tuple(
        (
            owned_term(pieces[2 * i], pieces[2 * i + 1], dp_count, query_count, place)
            for i in range(len(totals))
        )
    )
    every_sum = (
        lax.psum_scatter(
            every_fold[2].astype(jnp.bfloat16), "dp", scatter_dimension=0, tiled=True
        ).astype(jnp.float32),
        lax.psum_scatter(
            every_fold[3].astype(jnp.bfloat16), "dp", scatter_dimension=0, tiled=True
        ).astype(jnp.float32),
        lax.psum_scatter(
            grad_cell.astype(jnp.bfloat16), "dp", scatter_dimension=0, tiled=True
        ).astype(jnp.float32),
        lax.psum_scatter(
            grad_gene.astype(jnp.bfloat16), "dp", scatter_dimension=0, tiled=True
        ).astype(jnp.float32),
        lax.psum_scatter(
            grad_table.astype(jnp.bfloat16), "dp", scatter_dimension=0, tiled=True
        ).astype(jnp.float32),
        lax.psum_scatter(
            every_fold[0].astype(jnp.bfloat16), "dp", scatter_dimension=0, tiled=True
        ).astype(jnp.float32),
        lax.psum_scatter(
            every_fold[1].astype(jnp.bfloat16), "dp", scatter_dimension=0, tiled=True
        ).astype(jnp.float32),
    )
    ffn_sums = every_sum[:5]
    attn_sums = every_sum[5:]
    small_sums = (
        lax.psum_scatter(gain_terms, ("dp", "query"), scatter_dimension=0, tiled=True),
        lax.psum_scatter(shift_terms, ("dp", "query"), scatter_dimension=0, tiled=True),
        lax.psum_scatter(proj_terms, ("dp", "query"), scatter_dimension=0, tiled=True),
        lax.psum_scatter(ff_terms, ("dp", "query"), scatter_dimension=0, tiled=True),
        lax.psum_scatter(grad_logit, ("dp", "query"), scatter_dimension=0, tiled=True),
    )

    def flat_rows(values_in):
        return values_in.reshape(-1, values_in.shape[-1])

    return (
        encoded.reshape(row_count, ROW_LEN, D),
        grad_tokens,
        small_sums[0].T,
        small_sums[1].T,
        small_sums[2].T,
        small_sums[3].T,
        flat_rows(attn_sums[0]),
        flat_rows(attn_sums[1]),
        flat_rows(ffn_sums[0]),
        flat_rows(ffn_sums[1]),
        flat_rows(ffn_sums[2]),
        flat_rows(ffn_sums[3]),
        small_sums[4],
        flat_rows(ffn_sums[4]),
    )


def solution(mesh):
    placed = (
        P(("dp", "query"), None, None),
        P(("dp", "query"), None),
        P(("dp", "query"), None, None),
        P(),
        P(),
        P(),
        P(),
        P("query", None),
        P("query", None),
        P("query", None),
        P("query", None),
        P("query", None),
        P("query", None),
        P(),
        P("query", None),
        P("dp", "query"),
        P("dp", "query"),
    )
    rows = P(("dp", "query"), None)
    grid = Grid(mesh)
    return jax.shard_map(
        make_shards(grid) if grid.paired() else shards_any,
        mesh=mesh,
        in_specs=placed,
        out_specs=(
            P(("dp", "query"), None, None),
            P(("dp", "query"), None, None),
            P(None, ("dp", "query")),
            P(None, ("dp", "query")),
            P(None, ("dp", "query")),
            P(None, ("dp", "query")),
            rows,
            rows,
            rows,
            rows,
            rows,
            rows,
            P(("dp", "query")),
            rows,
        ),
        check_vma=False,
    )
```

```python
import math

import jax
import jax.numpy as jnp
from jax import lax
from jax.experimental import pallas as pl
from jax.experimental.pallas import tpu as pltpu
from jax.sharding import PartitionSpec as P

D = 1280
HEADS = 20
HEAD_DIM = 64
FF = 5120
ROW_LEN = 512
CELLS_ROW = 4
GENES = 1024
EPSILON = 1e-05
HIGHEST = lax.Precision.HIGHEST
F32 = jnp.float32
BF16 = jnp.bfloat16
VMEM_ASKED = 56 << 20


def layer_norm(values_in, scale_row, offset_row):
    center = values_in - jnp.mean(values_in, axis=-1, keepdims=True)
    spread = jnp.mean(center * center, axis=-1, keepdims=True)
    return center * lax.rsqrt(spread + EPSILON) * scale_row + offset_row


def smooth_gate(values_in):
    return jax.nn.gelu(values_in, approximate=False)


def dot(left, right):
    return jnp.dot(left, right, preferred_element_type=F32)


def dot_rt(left, right):
    return lax.dot_general(left, right, (((1,), (1,)), ((), ())), preferred_element_type=F32)


def dot_lt(left, right):
    return lax.dot_general(left, right, (((0,), (0,)), ((), ())), preferred_element_type=F32)


def cell_layout(lengths):
    cell_ends = jnp.cumsum(lengths, axis=-1, dtype=jnp.int32)
    starts = cell_ends - lengths
    places = jnp.arange(ROW_LEN, dtype=jnp.int32)
    segment = jnp.sum(
        (places[None, :, None] >= cell_ends[:, None, :]).astype(jnp.int32), axis=-1, dtype=jnp.int32
    )
    return (starts, segment)


def cell_mask(segment_row, segment_column, mask):
    same = segment_column[...] == segment_row[...]
    mask[...] = jnp.where(same, 0.0, -1e30)


PAIRS = 2
WIDE = PAIRS * 2 * HEAD_DIM


def attend_kernel(segment_row, segment_column, query, key, value, mixed, totals, mask):
    @pl.when(pl.program_id(1) == 0)
    def _():
        cell_mask(segment_row.at[0], segment_column.at[0], mask)

    ones = jnp.ones((8, ROW_LEN), BF16)
    value_t = value[0].T
    parts = []
    for head in range(2 * PAIRS):
        columns = slice(head * HEAD_DIM, (head + 1) * HEAD_DIM)
        scaled = query[0, :, columns] * jnp.asarray(1.0 / math.sqrt(HEAD_DIM), BF16)
        scores = dot_rt(key[0, :, columns], scaled) + mask[...]
        top = jnp.max(scores, axis=0, keepdims=True)
        weights = jnp.exp(scores - top).astype(BF16)
        left = jnp.concatenate([value_t[columns], ones], axis=0)
        product = dot(left, weights)
        total = product[HEAD_DIM : HEAD_DIM + 1]
        parts.append(product[:HEAD_DIM] / total)
        totals[0, 0, head : head + 1] = top + jnp.log(total)
    mixed[0] = jnp.concatenate(parts, axis=0).T.astype(BF16)


def attend(qkv, segment):
    rows = qkv.shape[0]
    pairs = HEADS // 2 // PAIRS
    wide = WIDE

    def part(offset):
        return pl.BlockSpec((1, ROW_LEN, wide), lambda r, i: (r, 0, offset + i))

    return pl.pallas_call(
        attend_kernel,
        grid=(rows, pairs),
        in_specs=[
            pl.BlockSpec((1, 1, ROW_LEN), lambda r, i: (r, 0, 0)),
            pl.BlockSpec((1, ROW_LEN, 1), lambda r, i: (r, 0, 0)),
            part(0),
            part(pairs),
            part(2 * pairs),
        ],
        out_specs=[
            pl.BlockSpec((1, ROW_LEN, wide), lambda r, i: (r, 0, i)),
            pl.BlockSpec((1, 1, 2 * PAIRS, ROW_LEN), lambda r, i: (r, i, 0, 0)),
        ],
        out_shape=[
            jax.ShapeDtypeStruct((rows, ROW_LEN, pairs * wide), BF16),
            jax.ShapeDtypeStruct((rows, pairs, 2 * PAIRS, ROW_LEN), F32),
        ],
        scratch_shapes=[pltpu.VMEM((ROW_LEN, ROW_LEN), F32)],
        compiler_params=pltpu.CompilerParams(vmem_limit_bytes=VMEM_ASKED),
        cost_estimate=pl.CostEstimate(flops=1, bytes_accessed=1, transcendentals=0),
    )(segment[:, None, :], segment[:, :, None], qkv, qkv, qkv)


def attend_back_kernel(
    segment_row, segment_column, query, key, value, mixed, back, totals, d_qkv, mask
):
    @pl.when(pl.program_id(1) == 0)
    def _():
        cell_mask(segment_row.at[0], segment_column.at[0], mask)

    scale = jnp.asarray(1.0 / math.sqrt(HEAD_DIM), BF16)
    key_t = key[0].T
    product_t = (back[0].astype(F32) * mixed[0].astype(F32)).T
    queries, keys, values = [], [], []
    for head in range(2 * PAIRS):
        columns = slice(head * HEAD_DIM, (head + 1) * HEAD_DIM)
        scaled = query[0, :, columns] * scale
        grad = back[0, :, columns]
        scores = dot_rt(key[0, :, columns], scaled) + mask[...]
        weights = jnp.exp(scores - totals[0, 0, head : head + 1])
        d_weights = dot_rt(value[0, :, columns], grad)
        shift = jnp.sum(product_t[columns], axis=0, keepdims=True)
        d_scores = (weights * (d_weights - shift)).astype(BF16)
        values.append(dot(weights.astype(BF16), grad))
        keys.append(dot(d_scores, scaled))
        queries.append(dot(key_t[columns], d_scores))
    pair = pl.program_id(1)
    parts = [
        jnp.concatenate(queries, axis=0).T * (1.0 / math.sqrt(HEAD_DIM)),
        jnp.concatenate(keys, axis=1),
        jnp.concatenate(values, axis=1),
    ]
    for i, part in enumerate(parts):
        columns = pl.ds(pl.multiple_of(i * D + pair * WIDE, 128), WIDE)
        d_qkv[0, :, columns] = part.astype(BF16)


def attend_back(qkv, segment, mixed, back, totals):
    rows = qkv.shape[0]
    pairs = HEADS // 2 // PAIRS
    wide = WIDE

    def part(offset):
        return pl.BlockSpec((1, ROW_LEN, wide), lambda r, i: (r, 0, offset + i))

    return pl.pallas_call(
        attend_back_kernel,
        grid=(rows, pairs),
        in_specs=[
            pl.BlockSpec((1, 1, ROW_LEN), lambda r, i: (r, 0, 0)),
            pl.BlockSpec((1, ROW_LEN, 1), lambda r, i: (r, 0, 0)),
            part(0),
            part(pairs),
            part(2 * pairs),
            part(0),
            part(0),
            pl.BlockSpec((1, 1, 2 * PAIRS, ROW_LEN), lambda r, i: (r, i, 0, 0)),
        ],
        out_specs=pl.BlockSpec((1, ROW_LEN, 3 * D), lambda r, i: (r, 0, 0)),
        out_shape=jax.ShapeDtypeStruct((rows, ROW_LEN, 3 * D), BF16),
        scratch_shapes=[pltpu.VMEM((ROW_LEN, ROW_LEN), F32)],
        compiler_params=pltpu.CompilerParams(vmem_limit_bytes=VMEM_ASKED),
        cost_estimate=pl.CostEstimate(flops=1, bytes_accessed=1, transcendentals=0),
    )(segment[:, None, :], segment[:, :, None], qkv, qkv, qkv, mixed, back, totals)


CHUNK = 1280
HALF_CHUNK = 640


def unit_places(outer, inner, core):
    mine = (outer ^ core, inner ^ (1 - core))
    theirs = (outer ^ (1 - core), inner ^ core)
    corner = (outer ^ 1, inner ^ 1)
    return [
        (outer, inner, core),
        (outer, inner, 1 - core),
        (*mine, core),
        (*mine, 1 - core),
        (*corner, core),
        (*theirs, 1 - core),
        (*theirs, core),
        (*corner, 1 - core),
    ]


def part_copies(sources, columns, place, buffer, sems, half_rows, act):
    shard, *units = sources
    query, outer, inner, core = (place[i] for i in range(4))
    size = units[0].shape[0]
    act(
        pltpu.make_async_copy(
            shard.at[:, columns],
            buffer.at[pl.ds(pl.multiple_of(query * half_rows, 16), half_rows), :],
            sems.at[0],
        )
    )
    for i, (unit, (zb, y, c)) in enumerate(zip(units, unit_places(outer, inner, core))):
        row = (1 - query) * half_rows + ((zb * 2 + y) * 2 + c) * size
        act(
            pltpu.make_async_copy(
                unit.at[:, columns],
                buffer.at[pl.ds(pl.multiple_of(row, 16), size), :],
                sems.at[1 + i],
            )
        )


def chunk_place(step, place, half):
    steps = half // CHUNK
    own = step < steps
    return jnp.where(own, place[0] * steps + step, (1 - place[0]) * steps + step - steps)


def up_copies(sources, place, step, buffer, sems, act):
    half = FF // 2
    start = pl.multiple_of(chunk_place(step, place, half) * CHUNK, 128)
    columns = pl.ds(start, CHUNK)
    part_copies(sources, columns, place, buffer, sems, sources[0].shape[0], act)


def down_copies(sources, place, step, buffer, sems, act):
    shard, *units = sources
    query, outer, inner, core = (place[i] for i in range(4))
    size = units[0].shape[0]
    steps = shard.shape[0] // CHUNK
    own = step < steps
    local = jnp.where(own, step, step - steps)

    @pl.when(own)
    def _():
        act(
            pltpu.make_async_copy(
                shard.at[pl.ds(pl.multiple_of(local * CHUNK, 16), CHUNK), :], buffer, sems.at[0]
            )
        )

    for piece in range(CHUNK // (2 * size)):
        at = local * (CHUNK // (2 * size)) + piece
        for i, (unit, (zb, y, c)) in enumerate(zip(units, unit_places(outer, inner, core))):

            @pl.when(jnp.logical_and(jnp.logical_not(own), at == zb * 2 + y))
            def _():
                row = pl.multiple_of((piece * 2 + c) * size, 16)
                act(
                    pltpu.make_async_copy(unit, buffer.at[pl.ds(row, size), :], sems.at[1 + i])
                )


def stream(copies, buffer, sems):
    step, steps = pl.program_id(0), pl.num_programs(0)
    slot = lax.rem(step, 2)

    @pl.when(step == 0)
    def _():
        copies(step, buffer.at[slot], sems.at[slot], lambda copy: copy.start())

    @pl.when(step + 1 < steps)
    def _():
        copies(step + 1, buffer.at[1 - slot], sems.at[1 - slot], lambda copy: copy.start())

    copies(step, buffer.at[slot], sems.at[slot], lambda copy: copy.wait())
    return buffer.at[slot]


def gate(values):
    inner = 0.5 * lax.erf(values * math.sqrt(0.5)) + 0.5
    bell = jnp.exp(values * values * -0.5) * (1.0 / math.sqrt(2.0 * math.pi))
    return values * inner, inner + values * bell


def up_kernel(place, second, bias, *refs):
    sources, (active, slope, buffer, sems) = refs[:9], refs[9:]
    weights = stream(lambda *at: up_copies(sources, place, *at), buffer, sems)
    value, rise = gate(dot(second[...], weights[...]) + bias[...])
    active[...] = value.astype(BF16)
    slope[...] = rise.astype(BF16)


def down_kernel(place, active, middle, bias, picker, *refs):
    sources, (out, heads, buffer, sems) = refs[:9], refs[9:]
    weights = stream(lambda *at: down_copies(sources, place, *at), buffer, sems)

    @pl.when(pl.program_id(0) == 0)
    def _():
        out[...] = middle[...] + bias[...]

    out[...] += dot(active[...], weights[...])

    @pl.when(pl.program_id(0) == pl.num_programs(0) - 1)
    def _():
        heads[...] = dot(picker[...], out[...].astype(BF16)).astype(BF16)


def back_kernel(place, branch, slope, *refs):
    up, down = refs[:9], refs[9:18]
    d_hidden, sums, out, buffer, sems, buffer_two, sems_two = refs[18:]
    up_part = stream(lambda *at: up_copies(up, place, *at), buffer, sems)
    down_part = stream(lambda *at: down_copies(down, place, *at), buffer_two, sems_two)

    @pl.when(pl.program_id(0) == 0)
    def _():
        out[...] = jnp.zeros_like(out)

    d_active = dot_rt(branch[...], down_part[...])
    low = (d_active * slope[...].astype(F32)).astype(BF16)
    d_hidden[...] = low
    sums[...] = jnp.sum(low.astype(F32), axis=0, keepdims=True)
    out[...] += dot_rt(low, up_part[...])


def qkv_kernel(place, normed, bias, *refs):
    sources, (out, buffer, sems) = refs[:9], refs[9:]

    def copies(step, *at):
        columns = pl.ds(pl.multiple_of(step * CHUNK, 128), CHUNK)
        part_copies(sources, columns, place, *at[:2], sources[0].shape[0], at[2])

    weights = stream(copies, buffer, sems)
    out[...] = (dot(normed[...], weights[...]) + bias[...]).astype(BF16)


def qkv_back_kernel(place, back, *refs):
    sources, (out, buffer, sems) = refs[:9], refs[9:]

    def copies(step, *at):
        columns = pl.ds(pl.multiple_of(step * CHUNK, 128), CHUNK)
        part_copies(sources, columns, place, *at[:2], sources[0].shape[0], at[2])

    weights = stream(copies, buffer, sems)
    terms = dot_rt(back[...], weights[...])

    @pl.when(pl.program_id(0) == 0)
    def _():
        out[...] = terms

    @pl.when(pl.program_id(0) > 0)
    def _():
        out[...] += terms


def qkv_call(kernel, place, inputs, specs, out_shape, out_spec, columns, weights):
    return pl.pallas_call(
        kernel,
        grid_spec=pltpu.PrefetchScalarGridSpec(
            num_scalar_prefetch=1,
            grid=(columns // CHUNK,),
            in_specs=specs + [pl.BlockSpec(memory_space=pl.ANY)] * 9,
            out_specs=out_spec,
            scratch_shapes=[pltpu.VMEM((2, D, CHUNK), BF16), pltpu.SemaphoreType.DMA((2, 9))],
        ),
        out_shape=out_shape,
        compiler_params=pltpu.CompilerParams(vmem_limit_bytes=VMEM_ASKED),
        cost_estimate=pl.CostEstimate(flops=1, bytes_accessed=1, transcendentals=0),
    )(place, *inputs, *weights)


def project(place, normed, bias, weights):
    count, columns = normed.shape[0], weights[0].shape[1]
    whole = pl.BlockSpec((count, D), lambda j, place: (0, 0))
    row = pl.BlockSpec((1, CHUNK), lambda j, place: (0, j))
    out = pl.BlockSpec((count, CHUNK), lambda j, place: (0, j))
    shape = jax.ShapeDtypeStruct((count, columns), BF16)
    return qkv_call(
        qkv_kernel, place, [normed, bias], [whole, row], shape, out, columns, weights
    )


def project_back(place, back, weights):
    count, columns = back.shape
    whole = pl.BlockSpec((count, D), lambda j, place: (0, 0))
    chunk = pl.BlockSpec((count, CHUNK), lambda j, place: (0, j))
    shape = jax.ShapeDtypeStruct((count, D), F32)
    return qkv_call(qkv_back_kernel, place, [back], [chunk], shape, whole, columns, weights)


def feed_call(kernel, count, inputs, outputs, slots, place, *values, keep=()):
    def at(j, place):
        return chunk_place(j, place, FF // 2)

    specs = {
        "hidden": pl.BlockSpec((count, CHUNK), lambda j, place: (0, at(j, place))),
        "row": pl.BlockSpec((1, CHUNK), lambda j, place: (0, at(j, place))),
        "whole": pl.BlockSpec((count, D), lambda j, place: (0, 0)),
        "any": pl.BlockSpec(memory_space=pl.ANY),
        "vector": pl.BlockSpec((1, D), lambda j, place: (0, 0)),
    }
    shapes = {
        "hidden": jax.ShapeDtypeStruct((count, FF), BF16),
        "row": jax.ShapeDtypeStruct((1, FF), F32),
        "whole": jax.ShapeDtypeStruct((count, D), F32),
    }
    for name, array in keep:
        block = array.shape
        specs[name] = pl.BlockSpec(block, lambda j, place: (0, 0))
        shapes[name] = jax.ShapeDtypeStruct(block, BF16)
    scratch = []
    for slot in slots:
        scratch += [pltpu.VMEM((2, *slot), BF16), pltpu.SemaphoreType.DMA((2, 9))]
    return pl.pallas_call(
        kernel,
        grid_spec=pltpu.PrefetchScalarGridSpec(
            num_scalar_prefetch=1,
            grid=(FF // CHUNK,),
            in_specs=[specs[name] for name in inputs],
            out_specs=[specs[name] for name in outputs],
            scratch_shapes=scratch,
        ),
        out_shape=[shapes[name] for name in outputs],
        compiler_params=pltpu.CompilerParams(vmem_limit_bytes=VMEM_ASKED),
        cost_estimate=pl.CostEstimate(flops=1, bytes_accessed=1, transcendentals=0),
    )(place, *values)


UP_SLOT, DOWN_SLOT = (D, CHUNK), (CHUNK, D)


def feed_up(place, second, bias, up):
    names = ["whole", "row"] + ["any"] * 9
    return feed_call(
        up_kernel, second.shape[0], names, ["hidden", "hidden"], [UP_SLOT], place, second, bias, *up
    )


def feed_down(place, active, middle, bias, picker, down):
    names = ["hidden", "whole", "vector", "picker"] + ["any"] * 9
    heads = jax.ShapeDtypeStruct((picker.shape[0], D), BF16)
    return feed_call(
        down_kernel, active.shape[0], names, ["whole", "heads"], [DOWN_SLOT],
        place, active, middle, bias, picker, *down, keep=(("picker", picker), ("heads", heads)),
    )


def feed_back(place, branch, slope, up, down):
    names = ["whole", "hidden"] + ["any"] * 18
    return feed_call(
        back_kernel, branch.shape[0], names, ["hidden", "row", "whole"], [UP_SLOT, DOWN_SLOT],
        place, branch, slope, *up, *down,
    )


def decode_kernel(mine, other, gene, got, bias, weight, labels, low, sums, by_weight):
    cells = mine.shape[0]
    shape = (cells, gene.shape[0] // cells, gene.shape[1])
    parts = (gene[...].astype(F32) + got[...].astype(F32) + bias[...]).reshape(shape)
    before = (mine[...].astype(F32) + other[...].astype(F32))[:, None, :] + parts
    value, rise = gate(before)
    row = weight[...].astype(F32)[None]
    logits = jnp.sum(value * row, axis=2, keepdims=True)
    slope = jax.nn.sigmoid(logits) - labels[...].astype(F32)
    grad = (rise * (slope * row)).astype(BF16)
    low[...] = grad.reshape(low.shape)
    sums[...] = jnp.sum(grad.astype(F32), axis=1).astype(BF16)
    by_weight[...] = jnp.sum(jnp.sum(value * slope, axis=0), axis=0, keepdims=True)


def decode(mine, other, gene, got, bias, weight, labels):
    cells, queries = labels.shape
    return pl.pallas_call(
        decode_kernel,
        out_shape=[
            jax.ShapeDtypeStruct((cells * queries, FF), BF16),
            jax.ShapeDtypeStruct((cells, FF), BF16),
            jax.ShapeDtypeStruct((1, FF), F32),
        ],
        compiler_params=pltpu.CompilerParams(vmem_limit_bytes=VMEM_ASKED),
        cost_estimate=pl.CostEstimate(flops=1, bytes_accessed=1, transcendentals=0),
    )(mine, other, gene, got, bias, weight, labels[:, :, None])


def term_kernel(count, mine, units, place, *refs):
    query, _, inner, core = (place[i] for i in range(4))
    inputs = 1 + max(source for unit in units for _, source in unit)
    lefts, rights, (out, blocks), turned = (
        refs[:count],
        refs[count : count + inputs],
        refs[count + inputs : count + inputs + 2],
        refs[count + inputs + 2 :],
    )
    step = pl.program_id(0)
    half = core if mine else 1 - core

    @pl.when(step == 0)
    def _():
        outer = blocks.shape[0] // 8
        size = 2 * outer * blocks.shape[1]
        for left, into in zip(lefts, turned):
            blocks[...] = left[...].astype(F32).T.reshape(blocks.shape)
            for to in range(4):
                first, second = to // 2, to % 2
                x = query ^ jnp.where(half == 0, first, second)
                y = inner ^ jnp.where(half == 0, second, first)
                rows = [
                    blocks[((z * 2 + y) * 2 + c) * 2 + x] for z in range(outer) for c in range(2)
                ]
                into[pl.ds(to * size, size), :] = jnp.concatenate(rows, axis=0).astype(BF16)

    for at, unit in enumerate(units):

        @pl.when(step == at)
        def _():
            for side, (pair, source) in enumerate(unit):
                terms = dot(turned[pair][...], rights[source][...]).astype(BF16)
                columns = slice(side * HALF_CHUNK, (side + 1) * HALF_CHUNK)
                out[:, :, :, columns] = terms.reshape(*out.shape[:3], HALF_CHUNK)


def weight_terms(place, mine, *pairs):
    count, rows = pairs[0][0].shape
    sizes = [right.shape[1] // 2 // HALF_CHUNK for _, right in pairs]
    blocks = [(i, block) for i, size in enumerate(sizes) for block in range(size)]
    plan = [blocks[i : i + 2] for i in range(0, len(blocks), 2)]
    steps = len(plan)
    sources = sorted({(side, unit[side][0]) for unit in plan for side in range(2)})

    def right_spec(side, pair):
        wanted = [unit[side][1] if unit[side][0] == pair else None for unit in plan]
        known = [block for block in wanted if block is not None]

        def at(j, place):
            half = place[3] if mine else 1 - place[3]
            index = known[0]
            for step, block in enumerate(wanted):
                if block is not None:
                    index = jnp.where(j >= step, block, index)
            return (0, half * sizes[pair] + index)

        return pl.BlockSpec((count, HALF_CHUNK), at)

    units = [
        [(pair, sources.index((side, pair))) for side, (pair, _) in enumerate(unit)] for unit in plan
    ]
    left_spec = pl.BlockSpec((count, rows), lambda j, place: (0, 0))
    return pl.pallas_call(
        lambda *refs: term_kernel(len(pairs), mine, units, *refs),
        grid_spec=pltpu.PrefetchScalarGridSpec(
            num_scalar_prefetch=1,
            grid=(steps,),
            in_specs=[left_spec] * len(pairs) + [right_spec(*source) for source in sources],
            out_specs=pl.BlockSpec((2, 2, rows // 4, CHUNK), lambda j, place: (0, 0, 0, j)),
            scratch_shapes=[pltpu.VMEM((32, rows // 32, count), F32)]
            + [pltpu.VMEM((rows, count), BF16)] * len(pairs),
        ),
        out_shape=jax.ShapeDtypeStruct((2, 2, rows // 4, steps * CHUNK), BF16),
        compiler_params=pltpu.CompilerParams(vmem_limit_bytes=VMEM_ASKED),
        cost_estimate=pl.CostEstimate(flops=1, bytes_accessed=1, transcendentals=0),
    )(place, *[left for left, _ in pairs], *[pairs[pair][1] for _, pair in sources])


def tall_kernel(place, left, right, own, sent, blocks, turned):
    query, _, inner, core = (place[i] for i in range(4))
    width = blocks.shape[1]
    blocks[...] = left[...].astype(F32).T.reshape(blocks.shape)
    for to in range(4):
        source = (to % 2) * 2 + to // 2
        turned[pl.ds(to * width, width), :] = blocks[source].astype(BF16)
    terms = dot(turned[...], right[...]).astype(BF16)
    size = terms.shape[1] // 2
    y_place = (pl.program_id(0) % 2) ^ inner
    for half in range(2):
        for x in range(2):
            x_place = x ^ query
            at = (x_place, y_place) if half == 0 else (y_place, x_place)
            value = terms[2 * x * width : 2 * (x + 1) * width, half * size : (half + 1) * size]

            @pl.when(core == half)
            def _():
                own[at[0], at[1], 0] = value

            @pl.when(core != half)
            def _():
                sent[at[0], at[1], 0] = value


def tall_terms(place, left, right, outer):
    count, rows = left.shape
    columns = right.shape[1]
    wide = rows // (2 * outer)
    shape = (2, 2, outer, wide // 2, columns // 2)
    out = pl.BlockSpec(
        (2, 2, 1, wide // 2, columns // 2), lambda j, place: (0, 0, j // 2, 0, 0)
    )
    own, sent = pl.pallas_call(
        tall_kernel,
        grid_spec=pltpu.PrefetchScalarGridSpec(
            num_scalar_prefetch=1,
            grid=(2 * outer,),
            in_specs=[
                pl.BlockSpec((count, wide), lambda j, place: (0, j)),
                pl.BlockSpec((count, columns), lambda j, place: (0, 0)),
            ],
            out_specs=[out, out],
            scratch_shapes=[
                pltpu.VMEM((4, wide // 4, count), F32),
                pltpu.VMEM((wide, count), BF16),
            ],
        ),
        out_shape=[jax.ShapeDtypeStruct(shape, BF16)] * 2,
        compiler_params=pltpu.CompilerParams(vmem_limit_bytes=VMEM_ASKED),
        cost_estimate=pl.CostEstimate(flops=1, bytes_accessed=1, transcendentals=0),
    )(place, left, right)
    flat = (2, 2, outer * wide // 2, columns // 2)
    return own.reshape(flat), sent.reshape(flat)


def small_cost():
    return pl.CostEstimate(flops=1, bytes_accessed=1, transcendentals=0)


def add_kernel(count, *refs):
    ins, outs = refs[: len(refs) - count], refs[len(refs) - count :]
    each = len(ins) // count
    for i, out in enumerate(outs):
        total = ins[i * each][...].astype(F32)
        for other in ins[i * each + 1 : (i + 1) * each]:
            total = total + other[...].astype(F32)
        out[...] = total.astype(BF16)


def add_call(*groups):
    first, _ = groups[0][0]
    rows, columns = first.shape[-2:]
    steps = 2
    size = rows // steps
    specs, arrays = [], []
    for group in groups:
        for array, at in group:
            lead = (None,) * len(at)
            specs.append(
                pl.BlockSpec((*lead, size, columns), lambda r, at=at: (*at, r, 0))
            )
            arrays.append(array)
    out = pl.BlockSpec((size, columns), lambda r: (r, 0))
    shape = jax.ShapeDtypeStruct((rows, columns), BF16)
    return pl.pallas_call(
        lambda *refs: add_kernel(len(groups), *refs),
        grid=(steps,),
        in_specs=specs,
        out_specs=[out] * len(groups),
        out_shape=[shape] * len(groups),
        compiler_params=pltpu.CompilerParams(vmem_limit_bytes=VMEM_ASKED),
        cost_estimate=small_cost(),
    )(*arrays)


def first_kernel(own, got, out):
    out[...] = (own[...].astype(F32) + got[...].astype(F32)).astype(BF16)


def add_first_call(own, got):
    rows, columns = own.shape[-2:]
    steps = 2
    size = rows // steps
    half = pl.BlockSpec((None, 2, size, columns), lambda r: (1, 0, r, 0))
    return pl.pallas_call(
        first_kernel,
        grid=(steps,),
        in_specs=[half, half],
        out_specs=pl.BlockSpec((2, size, columns), lambda r: (0, r, 0)),
        out_shape=jax.ShapeDtypeStruct((2, rows, columns), BF16),
        compiler_params=pltpu.CompilerParams(vmem_limit_bytes=VMEM_ASKED),
        cost_estimate=small_cost(),
    )(own, got)


def out_kernel(mixed, weight, tokens, bias, gain, shift, middle, second):
    values = tokens[...].astype(F32) + dot(mixed[...], weight[...]) + bias[...]
    middle[...] = values
    second[...] = layer_norm(values, gain[...], shift[...]).astype(BF16)


def attend_out(mixed, weight, tokens, bias, gain, shift):
    count = tokens.shape[0]
    size = 256
    row = pl.BlockSpec((size, D), lambda r: (r, 0))
    vector = pl.BlockSpec((1, D), lambda r: (0, 0))
    whole = pl.BlockSpec((D, D), lambda r: (0, 0))
    return pl.pallas_call(
        out_kernel,
        grid=(count // size,),
        in_specs=[row, whole, row, vector, vector, vector],
        out_specs=[row, row],
        out_shape=[
            jax.ShapeDtypeStruct((count, D), F32),
            jax.ShapeDtypeStruct((count, D), BF16),
        ],
        compiler_params=pltpu.CompilerParams(vmem_limit_bytes=VMEM_ASKED),
        cost_estimate=small_cost(),
    )(mixed, weight, tokens, bias[None, :], gain[None, :], shift[None, :])


def spread_kernel(left, right, out):
    out[...] = dot(left[...], right[...]).astype(BF16)


def spread(left, right):
    count, depth = left.shape
    columns = right.shape[1]
    return pl.pallas_call(
        spread_kernel,
        grid=(columns // CHUNK,),
        in_specs=[
            pl.BlockSpec((count, depth), lambda j: (0, 0)),
            pl.BlockSpec((depth, CHUNK), lambda j: (0, j)),
        ],
        out_specs=pl.BlockSpec((count, CHUNK), lambda j: (0, j)),
        out_shape=jax.ShapeDtypeStruct((count, columns), BF16),
        compiler_params=pltpu.CompilerParams(vmem_limit_bytes=VMEM_ASKED),
        cost_estimate=small_cost(),
    )(left, right)


def gather_kernel(left, right, out, total):
    terms = dot_rt(left[...], right[...])
    step = pl.program_id(0)

    @pl.when(step == 0)
    def _():
        total[...] = terms

    @pl.when(step > 0)
    def _():
        total[...] += terms

    @pl.when(step == pl.num_programs(0) - 1)
    def _():
        out[...] = total[...].astype(BF16)


def gather(left, right):
    count, columns = left.shape
    rows = right.shape[0]
    return pl.pallas_call(
        gather_kernel,
        grid=(columns // CHUNK,),
        in_specs=[
            pl.BlockSpec((count, CHUNK), lambda j: (0, j)),
            pl.BlockSpec((rows, CHUNK), lambda j: (0, j)),
        ],
        out_specs=pl.BlockSpec((count, rows), lambda j: (0, 0)),
        out_shape=jax.ShapeDtypeStruct((count, rows), BF16),
        scratch_shapes=[pltpu.VMEM((count, rows), F32)],
        compiler_params=pltpu.CompilerParams(vmem_limit_bytes=VMEM_ASKED),
        cost_estimate=small_cost(),
    )(left, right)


def norm_terms(values, grad, gain):
    center = values - jnp.mean(values, axis=-1, keepdims=True)
    spread = jnp.mean(center * center, axis=-1, keepdims=True)
    rise = lax.rsqrt(spread + EPSILON)
    unit = center * rise
    scaled = grad * gain
    first = jnp.mean(scaled, axis=-1, keepdims=True)
    second = jnp.mean(scaled * unit, axis=-1, keepdims=True)
    return (
        (scaled - first - unit * second) * rise,
        jnp.sum(grad * unit, axis=0, keepdims=True),
        jnp.sum(grad, axis=0, keepdims=True),
    )


def out_back_kernel(
    grad, middle, gain, flat, weight, grad_middle, low, back, gain_sum, shift_sum
):
    part, by_gain, by_shift = norm_terms(middle[...], grad[...], gain[...])
    total = flat[...] + part
    grad_middle[...] = total
    low[...] = total.astype(BF16)
    back[...] = dot_rt(total.astype(BF16), weight[...]).astype(BF16)

    @pl.when(pl.program_id(0) == 0)
    def _():
        gain_sum[...] = jnp.zeros_like(gain_sum)
        shift_sum[...] = jnp.zeros_like(shift_sum)

    gain_sum[...] += by_gain
    shift_sum[...] += by_shift


def attend_out_back(grad, middle, gain, flat, weight):
    count = grad.shape[0]
    size = 256
    row = pl.BlockSpec((size, D), lambda r: (r, 0))
    vector = pl.BlockSpec((1, D), lambda r: (0, 0))
    whole = pl.BlockSpec((D, D), lambda r: (0, 0))
    wide = jax.ShapeDtypeStruct((count, D), F32)
    low = jax.ShapeDtypeStruct((count, D), BF16)
    return pl.pallas_call(
        out_back_kernel,
        grid=(count // size,),
        in_specs=[row, row, vector, row, whole],
        out_specs=[row, row, row, vector, vector],
        out_shape=[wide, low, low] + [jax.ShapeDtypeStruct((1, D), F32)] * 2,
        compiler_params=pltpu.CompilerParams(vmem_limit_bytes=VMEM_ASKED),
        cost_estimate=small_cost(),
    )(grad, middle, gain[None, :], flat, weight)


def tokens_back_kernel(grad, tokens, gain, flat, out, gain_sum, shift_sum):
    part, by_gain, by_shift = norm_terms(tokens[...].astype(F32), grad[...], gain[...])
    out[...] = flat[...] + part

    @pl.when(pl.program_id(0) == 0)
    def _():
        gain_sum[...] = jnp.zeros_like(gain_sum)
        shift_sum[...] = jnp.zeros_like(shift_sum)

    gain_sum[...] += by_gain
    shift_sum[...] += by_shift


def tokens_back(grad, tokens, gain, flat):
    count = grad.shape[0]
    size = 256
    row = pl.BlockSpec((size, D), lambda r: (r, 0))
    vector = pl.BlockSpec((1, D), lambda r: (0, 0))
    return pl.pallas_call(
        tokens_back_kernel,
        grid=(count // size,),
        in_specs=[row, row, vector, row],
        out_specs=[row, vector, vector],
        out_shape=[jax.ShapeDtypeStruct((count, D), F32)]
        + [jax.ShapeDtypeStruct((1, D), F32)] * 2,
        compiler_params=pltpu.CompilerParams(vmem_limit_bytes=VMEM_ASKED),
        cost_estimate=small_cost(),
    )(grad, tokens, gain[None, :], flat)


def assemble_kernel(pieces, width, count, place_ref, *refs):
    sources, full, sems = refs[:count], refs[count], refs[count + 1]
    step = pl.program_id(0)
    copies = []
    for i, (source, row, rows, column) in enumerate(pieces):
        start = pl.multiple_of(place_ref[i], 16)
        columns = pl.ds(pl.multiple_of(column + step * width, 128), width)
        copies.append(
            pltpu.make_async_copy(
                sources[source].at[pl.ds(row, rows), columns],
                full.at[pl.ds(start, rows), :],
                sems.at[i],
            )
        )
    for copy in copies:
        copy.start()
    for copy in copies:
        copy.wait()


def assemble(sources, pieces, places, shape, width):
    count = len(sources)
    rows, columns = shape
    return pl.pallas_call(
        lambda *refs: assemble_kernel(pieces, width, count, *refs),
        grid=(columns // width,),
        out_shape=jax.ShapeDtypeStruct(shape, BF16),
        in_specs=[pl.BlockSpec(memory_space=pltpu.SMEM)]
        + [pl.BlockSpec(memory_space=pl.ANY)] * count,
        out_specs=pl.BlockSpec((rows, width), lambda j: (0, j)),
        scratch_shapes=[pltpu.SemaphoreType.DMA((len(pieces),))],
        compiler_params=pltpu.CompilerParams(vmem_limit_bytes=32 << 20),
        cost_estimate=pl.CostEstimate(flops=1, bytes_accessed=1, transcendentals=0),
    )(jnp.stack(places).astype(jnp.int32), *sources)


def sync(*values):
    return lax.optimization_barrier(values)


def tie(value, *others):
    return lax.optimization_barrier((value, others))[0] if others else value


class Grid:
    def __init__(self, mesh):
        dp, query = mesh.shape["dp"], mesh.shape["query"]
        core = 2 if dp % 2 == 0 else 1
        rest = dp // core
        outer = 4 if rest % 4 == 0 else rest
        inner = rest // outer
        self.dp, self.query = dp, query
        self.size = {"z": outer, "y": inner, "c": core, "x": query}
        self.stride = {"z": inner * core, "y": core, "c": 1}
        self.order = ["z", "y", "c", "x"]

    def paired(self):
        size = self.size
        pairs = size["x"] == 2 and size["y"] == 2 and size["c"] == 2
        return pairs and size["z"] == 4 and D % (self.dp * self.query * 8) == 0

    def place(self, axis):
        if axis == "zb":
            return self.place("z") % 2
        if axis == "zh":
            return self.place("z") // 2
        if axis == "x":
            return lax.axis_index("query")
        return (lax.axis_index("dp") // self.stride[axis]) % self.size[axis]

    def partner(self, axis, at, step):
        size = self.size[axis]
        return at ^ step if size & (size - 1) == 0 else (at + step) % size

    def sender(self, axis, at, step):
        size = self.size[axis]
        return at ^ step if size & (size - 1) == 0 else (at + size - step) % size

    def hop(self, value, axis, step=1):
        if axis == "x":
            pairs = [(i, self.partner("x", i, step)) for i in range(self.query)]
            return lax.ppermute(value, "query", pairs)
        stride, size = self.stride[axis], self.size[axis]
        pairs = []
        for i in range(self.dp):
            at = (i // stride) % size
            pairs.append((i, i + (self.partner(axis, at, step) - at) * stride))
        return lax.ppermute(value, "dp", pairs)

    def turn_hop(self, value, turn):
        pairs = []
        for i in range(self.dp):
            core = i % 2
            y = (i // self.stride["y"]) % 2
            for x in range(2):
                if core == turn:
                    to = i * 2 + 1 - x
                else:
                    to = (i + (1 - 2 * y) * self.stride["y"]) * 2 + x
                pairs.append((i * 2 + x, to))
        return lax.ppermute(value, ("dp", "query"), pairs)

    def share(self, value, axis=0, after=()):
        if self.query == 1:
            return value
        if self.query != 2:
            return lax.all_gather(value, "query", axis=axis, tiled=True)
        other = tie(self.hop(value, "x"), *after)
        first = lax.axis_index("query") == 0
        return jnp.concatenate(
            [jnp.where(first, value, other), jnp.where(first, other, value)], axis=axis
        )

    def joined_along(self, mine, other, axis):
        first = self.place(axis) == 0
        return jnp.concatenate(
            [jnp.where(first, mine, other), jnp.where(first, other, mine)], axis=0
        )

    def cut_half(self, value, axis):
        half = value.shape[1] // 2
        first = self.place(axis) == 0
        left, right = value[:, :half], value[:, half:]
        return jnp.where(first, left, right), jnp.where(first, right, left)

    def cut_fold(self, value, step):
        bits = value.reshape(value.shape[0] // 2, 2, *value.shape[1:])
        me = self.place("z") // step % 2
        return (
            lax.dynamic_index_in_dim(bits, me, axis=1, keepdims=False),
            lax.dynamic_index_in_dim(bits, 1 - me, axis=1, keepdims=False),
        )

    def joined(self, mine, other, axis=0):
        first = lax.axis_index("query") == 0
        return jnp.concatenate(
            [jnp.where(first, mine, other), jnp.where(first, other, mine)], axis=axis
        )

    def total(self, value):
        if self.query == 1:
            return value
        if self.query != 2:
            return lax.psum(value, "query")
        return value + self.hop(value, "x")

    def cut_step(self, value, axis, dim):
        me = self.place(axis)
        return (
            lax.dynamic_index_in_dim(value, me, axis=dim, keepdims=False),
            lax.dynamic_index_in_dim(value, 1 - me, axis=dim, keepdims=False),
        )

    def cut_columns(self, terms):
        half = terms.shape[1] // 2
        first = self.place("c") == 0
        left, right = terms[:, :half], terms[:, half:]
        return jnp.where(first, left, right), jnp.where(first, right, left)

    def trade(self, value, axis, dim, column):
        mine, other = self.cut_step(value, axis, dim)
        got = self.hop(other, axis) if axis != "zh" else self.hop(other, "z", 2)
        first = self.place(axis) == 0
        return jnp.concatenate(
            [jnp.where(first, mine, got), jnp.where(first, got, mine)], axis=column
        )

    def join_columns(self, value):
        value = value.reshape(2, -1, value.shape[-1])
        mine, other = self.cut_step(value, "c", 0)
        got = self.hop(other, "c")
        first = self.place("c") == 0
        return jnp.concatenate(
            [jnp.where(first, mine, got), jnp.where(first, got, mine)], axis=1
        )

    def scatter_step(self, value, axis, dim, kind):
        size = self.size[axis]
        me = self.place(axis)

        def part(index):
            return lax.dynamic_index_in_dim(value, index, axis=dim, keepdims=False)

        if size == 1:
            return part(0)
        sent = [
            self.hop(part(self.partner(axis, me, step)), axis, step) for step in range(1, size)
        ]
        total = part(me).astype(F32)
        for received in sent:
            total = total + received.astype(F32)
        return total.astype(kind)

    def scatter(self, value, order, kind=BF16):
        dims = [axis for axis in self.order if axis in order]
        for axis in order:
            dim = dims.index(axis)
            value = self.scatter_step(value, axis, dim, kind)
            dims.pop(dim)
        return value

    def scatter_z(self, value):
        stride, size = self.stride["z"], self.size["z"]
        groups = [[k * stride + i for k in range(size)] for i in range(stride)]
        return lax.psum_scatter(
            value, "dp", scatter_dimension=0, axis_index_groups=groups, tiled=True
        )

    def scatter_low(self, value):
        stride, size = self.stride["z"], self.size["z"]
        groups = [
            [(high * 2 + low) * stride + i for low in range(2)]
            for high in range(size // 2)
            for i in range(stride)
        ]
        return lax.psum_scatter(
            value, "dp", scatter_dimension=0, axis_index_groups=groups, tiled=True
        )

    def blocks(self, value):
        shape = [self.size[axis] for axis in self.order]
        rows = value.shape[0] // math.prod(shape)
        return value.reshape(*shape, rows, *value.shape[1:])

    def own_columns(self, value):
        width = value.shape[1] // (self.dp * self.query)
        shaped = value.reshape(value.shape[0], self.dp, self.query, width)
        mine = lax.dynamic_index_in_dim(shaped, self.place("x"), axis=2, keepdims=False)
        return mine.reshape(value.shape[0], self.dp * width)

    def part_of(self, shards):
        zb, y, c = self.place("z") % 2, self.place("y"), self.place("c")
        unit = min(shard.shape[0] for shard in shards) // 8
        mine = (zb * 2 + y) * 2 + c
        columns = []
        for shard in shards:
            fold = shard.shape[0] // (8 * unit)
            for k in range(fold):
                columns.append(
                    lax.dynamic_slice_in_dim(shard, (mine * fold + k) * unit, unit, 0)
                )
        return jnp.concatenate(columns, axis=1) if len(columns) > 1 else columns[0]

    def side_hop(self, value, turn):
        pairs = []
        for i in range(self.dp):
            axis = "y" if i % 2 == turn else "z"
            stride = self.stride[axis]
            at = (i // stride) % self.size[axis]
            pairs.append((i, i + ((at ^ 1) - at) * stride))
        return lax.ppermute(value, "dp", pairs)

    def join(self, shard, units, column):
        zb, y, c, x = self.place("z") % 2, self.place("y"), self.place("c"), self.place("x")
        rows, width = shard.shape
        size = rows // 8
        pieces, places = [(0, 0, rows, 0)], [x * rows]
        for i, (zb_, y_, c_) in enumerate(unit_places(zb, y, c)):
            pieces.append((1 + i, 0, size, column))
            places.append((1 - x) * rows + ((zb_ * 2 + y_) * 2 + c_) * size)
        return assemble([shard, *units], pieces, places, (2 * rows, width), 640)

    def places(self):
        return jnp.stack(
            [self.place("x"), self.place("z") % 2, self.place("y"), self.place("c")]
        ).astype(jnp.int32)


def added(*values):
    total = values[0].astype(F32)
    for value in values[1:]:
        total = total + value.astype(F32)
    return total.astype(BF16)


def added_wide(*values):
    total = values[0].astype(F32)
    for value in values[1:]:
        total = total + value.astype(F32)
    return total


class Sums:
    def __init__(self, grid):
        self.grid = grid

    def core(self, *after):
        self.got = self.grid.hop(tie(self.sent, *after), "c")

    def add_first(self, *after):
        own, got = tie((self.own, self.got), *after)
        self.one_in = add_first_call(own, got)

    def add_parts(self, *after):
        own, got = tie((self.own, self.got), *after)
        self.parts = add_call(*[[(own, (1, k)), (got, (1, k))] for k in (1, 0)])

    def go_part(self, part):
        return self.grid.turn_hop(self.parts[part], 0)

    def go_first(self):
        return self.grid.turn_hop(self.one_in, 0)

    def add_second(self, one):
        (self.two_in,) = add_call([(self.own, (0, 1)), (self.got, (0, 1)), one])

    def go_second(self):
        return self.grid.turn_hop(self.two_in, 1)

    def add_last(self, one, two):
        (whole,) = add_call([(self.own, (0, 0)), (self.got, (0, 0)), one, (two, ())])
        size = self.grid.size["z"]
        self.last_in = whole.reshape(size, whole.shape[0] // size, whole.shape[1])

    def last(self):
        self.sum = self.grid.scatter_z(self.last_in)

    def result(self, *after):
        value = tie(self.sum, *after)[0]
        value = value.reshape(2, value.shape[0] // 2, value.shape[1])
        mine, other = self.grid.cut_step(value, "c", 0)
        got = self.grid.hop(other, "c")
        first = self.grid.place("c") == 0
        return [
            jnp.where(first, mine, got).astype(F32),
            jnp.where(first, got, mine).astype(F32),
        ]


def make_shards(grid):
    def shards(
        tokens,
        cell_lengths,
        out_cotangent,
        ln_gains,
        ln_biases,
        proj_biases,
        ff_biases,
        w_qkv,
        w_out,
        w_up,
        w_down,
        dec_cell,
        dec_gene,
        dec_out,
        gene_table,
        query_ids,
        labels,
    ):
        row_count = tokens.shape[0]
        token_count = row_count * ROW_LEN
        dp_count, query_count = grid.dp, grid.query
        place = lax.axis_index("query")
        starts, segment = cell_layout(cell_lengths)
        local_cells = row_count * CELLS_ROW
        pair_cells, local_queries = query_ids.shape
        pairs = pair_cells * local_queries
        half_width = D // query_count

        row_tokens = tokens.reshape(token_count, D)
        where = grid.places()
        ids = grid.share(query_ids.reshape(1, pairs)).reshape(query_count * pairs)
        qkv_first = grid.hop(grid.part_of([w_qkv]), "x")
        normed_low = layer_norm(row_tokens.astype(F32), ln_gains[0], ln_biases[0]).astype(BF16)
        table_rows = gene_table.shape[0]
        local_ids = ids - place * table_rows
        held = (local_ids[:, None] == jnp.arange(table_rows, dtype=jnp.int32)[None, :]).astype(BF16)
        gene_found = dot(held, gene_table).astype(BF16)
        up_part = grid.part_of([w_up, w_out])
        down_part = grid.part_of([w_down])
        qkv_first, normed_low, gene_found, up_part, down_part = sync(
            qkv_first, normed_low, gene_found, up_part, down_part
        )
        up_first = grid.hop(up_part, "x")
        qkv_near = grid.hop(qkv_first, "c")
        qkv_side = grid.side_hop(qkv_first, 0)
        qkv_near, qkv_side = sync(qkv_near, qkv_side)
        qkv_side_two, qkv_corner = grid.side_hop(qkv_near, 0), grid.side_hop(qkv_side, 1)
        qkv_far = grid.hop(qkv_side, "c")
        qkv_side_two, qkv_corner, up_first = sync(qkv_side_two, qkv_corner, up_first)
        up_near = grid.hop(up_first, "c")
        up_side = grid.side_hop(up_first, 0)
        qkv_far_two, qkv_far_corner = grid.hop(qkv_side_two, "c"), grid.hop(qkv_corner, "c")
        qkv_far, qkv_far_two, qkv_far_corner = sync(qkv_far, qkv_far_two, qkv_far_corner)
        gene_hop = grid.hop(gene_found, "x")
        down_first = grid.hop(tie(down_part, up_first), "x")
        qkv_weights = (
            w_qkv, qkv_first, qkv_near, qkv_side, qkv_side_two, qkv_corner,
            qkv_far, qkv_far_two, qkv_far_corner,
        )
        zeroes = jnp.zeros((D,), F32)
        qkv_bias = jnp.concatenate([proj_biases[0], zeroes, proj_biases[1]])
        qkv_low = project(where, normed_low, qkv_bias[None, :], qkv_weights)
        qkv_low, up_near, up_side, gene_hop = sync(qkv_low, up_near, up_side, gene_hop)
        up_side_two, up_corner = grid.side_hop(up_near, 0), grid.side_hop(up_side, 1)
        up_far = grid.hop(up_side, "c")
        qkv_rows = qkv_low.reshape(row_count, ROW_LEN, 3 * D)
        mixed_rows, log_totals = attend(qkv_rows, segment)
        mixed_low = mixed_rows.reshape(token_count, D)
        gene_rows = added(gene_found, tie(gene_hop, mixed_low)) if query_count == 2 else gene_found
        gene_half = lax.dynamic_slice_in_dim(gene_rows, place * half_width, half_width, 1)
        gene_partial = spread(gene_half, dec_gene).reshape(query_count, pairs, FF)
        mixed_low, gene_partial, up_side_two, up_corner, up_far, down_first = sync(
            mixed_low, gene_partial, up_side_two, up_corner, up_far, down_first
        )
        gene_mine, gene_sent = grid.cut_step(gene_partial, "x", 0)
        down_near = grid.hop(down_first, "c")
        down_side = grid.side_hop(down_first, 0)
        up_far_two, up_far_corner = grid.hop(up_side_two, "c"), grid.hop(up_corner, "c")
        up_units = (
            up_first, up_near, up_side, up_side_two, up_corner, up_far, up_far_two, up_far_corner
        )
        up_weights = (w_up, *up_units)
        full_out = grid.join(w_out, up_units, FF)
        middle, second_low = attend_out(
            mixed_low, full_out, row_tokens, proj_biases[2], ln_gains[1], ln_biases[1]
        )
        second_low, down_near, down_side, gene_sent = sync(second_low, down_near, down_side, gene_sent)
        down_side_two, down_corner = grid.side_hop(down_near, 0), grid.side_hop(down_side, 1)
        down_far = grid.hop(down_side, "c")
        gene_got = grid.hop(gene_sent, "x")
        gene_pair = grid.hop(gene_rows, "z", 2)
        active_low, slope = feed_up(where, second_low, ff_biases[0][None, :], up_weights)
        active_low, slope, down_side_two, down_corner, down_far, gene_got, gene_pair = sync(
            active_low, slope, down_side_two, down_corner, down_far, gene_got, gene_pair
        )
        down_far_two, down_far_corner = grid.hop(down_side_two, "c"), grid.hop(down_corner, "c")
        down_weights = (
            w_down, down_first, down_near, down_side, down_side_two, down_corner,
            down_far, down_far_two, down_far_corner,
        )
        places = jnp.arange(ROW_LEN, dtype=jnp.int32)
        picker = (places[None, :, None] == starts[:, None, :]).astype(F32)
        rows_apart = jnp.arange(row_count)
        choice = jnp.where(
            rows_apart[:, None, None, None] == rows_apart[None, None, :, None],
            picker.transpose(0, 2, 1)[:, :, None, :],
            0,
        ).reshape(local_cells, token_count).astype(BF16)
        encoded, heads_low = feed_down(
            where, active_low, middle, proj_biases[3:], choice, down_weights
        )
        encoded_rows = encoded.reshape(row_count, ROW_LEN, D)
        cell_heads = grid.share(heads_low)
        heads_half = lax.dynamic_slice_in_dim(cell_heads, place * half_width, half_width, 1)
        cell_half = dot(heads_half, dec_cell).astype(BF16)
        cell_hop = grid.hop(cell_half, "x") if query_count == 2 else cell_half
        before_low, before_sums, grad_logit = decode(
            cell_half, cell_hop, gene_mine, gene_got, ff_biases[1][None, :], dec_out[None, :], labels
        )
        before_low = before_low.reshape(pair_cells, local_queries, FF)
        cell_total = grid.total(before_sums)
        heads_part = dot_rt(cell_total, dec_cell).astype(BF16)
        heads_all = grid.share(heads_part, axis=1)
        heads_back = lax.dynamic_slice_in_dim(
            heads_all, place * local_cells, local_cells, 0
        ).astype(F32)
        grad_encoded = out_cotangent.astype(F32) + jnp.sum(
            picker[:, :, :, None] * heads_back.reshape(row_count, 1, CELLS_ROW, D), axis=2
        )
        grad_flat = grad_encoded.reshape(token_count, D)
        branch_low = grad_flat.astype(BF16)
        branch_low, before_low = sync(branch_low, before_low)
        before_hop = grid.hop(before_low, "x") if query_count == 2 else before_low
        gathered = lax.all_gather(
            jnp.concatenate([cell_heads, cell_total], axis=1), "dp", axis=0, tiled=True
        )
        down_sums = Sums(grid)
        down_sums.own, down_sums.sent = tall_terms(where, active_low, branch_low, grid.size["z"])
        down_sums.own, down_sums.sent, before_hop = sync(down_sums.own, down_sums.sent, before_hop)
        down_sums.core()
        before_all = grid.joined(before_low, before_hop).reshape(query_count * pairs, FF)
        before_mine, before_sent = grid.cut_half(before_all, "zh")
        before_got = grid.hop(before_sent, "z", 2)
        hidden_low, up_bias_sums, grad_second = feed_back(
            where, tie(branch_low, down_sums.sent, before_sent), slope, up_weights, down_weights
        )
        hidden_low, grad_second, down_sums.got = sync(hidden_low, grad_second, down_sums.got)
        down_sums.add_parts()
        down_sums.parts = sync(*down_sums.parts)
        one, one_more = down_sums.go_part(0), down_sums.go_part(1)
        grad_middle, attn_low, mixed_back, grad_gain_two, grad_shift_two = attend_out_back(
            tie(grad_second, down_sums.parts), middle, ln_gains[1], grad_flat, full_out
        )
        gene_wide = grid.joined_along(gene_rows, gene_pair, "zh")
        before_wide = grid.joined_along(before_mine, tie(before_got, mixed_back), "zh")
        gene_left = grid.own_columns(gene_wide).reshape(gene_wide.shape[0], 2, 2, -1)
        gene_left = gene_left.transpose(0, 2, 1, 3).reshape(gene_wide.shape[0], -1)
        gene_half = before_wide.shape[1] // 2
        core = grid.place("c")
        gene_mine, gene_sent = [
            dot_lt(
                gene_left,
                lax.dynamic_slice_in_dim(before_wide, at * gene_half, gene_half, 1),
            ).astype(BF16)
            for at in (core, 1 - core)
        ]
        gene_got = grid.hop(gene_sent, "c")
        up_sums = Sums(grid)
        up_sums.sent = weight_terms(where, False, (second_low, tie(hidden_low, mixed_back, gene_sent)))
        up_sums.own = weight_terms(where, True, (second_low, tie(hidden_low, up_sums.sent)))
        up_sums.sent, up_sums.own, one, one_more, gene_got, gathered = sync(
            up_sums.sent, up_sums.own, one, one_more, gene_got, gathered
        )
        up_sums.core()
        down_sums.add_second((one, ()))
        two = down_sums.go_second()
        (gene_sum,) = add_call([(gene_mine, ()), (tie(gene_got, down_sums.two_in), ())])
        genes_part = gather(tie(before_all, gene_sum), dec_gene)
        choose = (
            tie(ids, genes_part)[:, None] == jnp.arange(GENES, dtype=jnp.int32)[None, :]
        ).astype(BF16)
        table_terms = dot_lt(choose, genes_part).astype(BF16)
        shape = [grid.size[axis] for axis in "zycx"]
        table_terms = table_terms.reshape(*shape, -1, half_width)
        table_mine, table_sent = grid.cut_step(table_terms, "c", 2)
        mixed_back, up_sums.got, gene_sum, table_mine, table_sent = sync(
            mixed_back, up_sums.got, gene_sum, table_mine, table_sent
        )
        gene_sum = grid.scatter_low(gene_sum)
        table_got = grid.hop(table_sent, "c")
        up_sums.add_parts()
        *up_sums.parts, mixed_back, two = sync(*up_sums.parts, mixed_back, two)
        up_one, up_more = up_sums.go_part(0), up_sums.go_part(1)
        qkv_back = attend_back(
            qkv_rows,
            segment,
            mixed_rows,
            mixed_back.reshape(row_count, ROW_LEN, D),
            log_totals,
        )
        qkv_back, table_got = sync(qkv_back, table_got)
        down_sums.add_last((one_more, ()), two)
        down_sums.last()
        qkv_back, up_one = sync(tie(qkv_back, down_sums.last_in), up_one)
        up_sums.add_second((up_one, ()))
        qkv_back_low = tie(qkv_back, up_sums.two_in).reshape(token_count, 3 * D)
        attn_sums = Sums(grid)
        attn_sums.sent = weight_terms(
            where,
            False,
            (normed_low, tie(qkv_back_low, down_sums.last_in)),
            (mixed_low, attn_low),
        )
        attn_sums.sent, qkv_back_low, up_more, gene_sum = sync(
            attn_sums.sent, qkv_back_low, up_more, gene_sum
        )
        up_two = up_sums.go_second()
        attn_sums.core()
        attn_sums.own = weight_terms(
            where, True, (normed_low, tie(qkv_back_low, up_sums.two_in)), (mixed_low, attn_low)
        )
        attn_sums.own, attn_sums.got = sync(attn_sums.own, attn_sums.got)
        attn_sums.add_first()
        attn_sums.one_in, qkv_back_low, up_two = sync(attn_sums.one_in, qkv_back_low, up_two)
        one = attn_sums.go_first()
        table_mine, table_sent = grid.cut_fold(added(tie(table_mine, attn_sums.one_in), table_got), 1)
        table_got = grid.hop(table_sent, "z", 1)
        grad_normed = project_back(where, qkv_back_low, qkv_weights)
        grad_normed, down_sums.sum = sync(grad_normed, down_sums.sum)
        up_sums.add_last((up_more, ()), up_two)
        up_sums.last()
        grad_tokens, grad_gain_one, grad_shift_one = tokens_back(
            tie(grad_normed, up_sums.last_in), row_tokens, ln_gains[0], grad_middle
        )
        one, grad_tokens, table_got = sync(one, grad_tokens, table_got)
        attn_sums.add_second((one, (1,)))
        two = attn_sums.go_second()

        table_mine, table_sent = grid.cut_fold(added(tie(table_mine, attn_sums.two_in), table_got), 2)
        table_got = grid.hop(table_sent, "z", 2)
        grad_tokens = grad_tokens.reshape(row_count, ROW_LEN, D)
        late_ties = (qkv_back_low, attn_low, branch_low, up_bias_sums, before_sums)
        qkv_late, attn_late, branch_late, up_bias_sums, sums_late = tie(late_ties, attn_sums.two_in)
        grad_up_bias = up_bias_sums[0]
        bias_sums = jnp.sum(qkv_late, axis=0, dtype=F32)
        grad_attn_bias = jnp.sum(attn_late, axis=0, dtype=F32)
        grad_out_bias = jnp.sum(branch_late, axis=0, dtype=F32)
        grad_dec_bias = jnp.sum(sums_late, axis=0, dtype=F32)
        owners = dp_count * query_count

        def owned_cols(values):
            return values.reshape(-1, owners, values.shape[-1] // owners).transpose(1, 0, 2).reshape(owners, -1)

        small = [
            jnp.concatenate([grad_gain_one, grad_gain_two]),
            jnp.concatenate([grad_shift_one, grad_shift_two]),
            jnp.stack([bias_sums[:D], bias_sums[2 * D :], grad_attn_bias, grad_out_bias]),
            jnp.stack([grad_up_bias, grad_dec_bias]),
            grad_logit,
        ]
        flat = [owned_cols(value) for value in small]
        sums = grid.scatter_step(grid.blocks(jnp.concatenate(flat, axis=1)), "c", 2, F32)
        sums, table_got, two, up_sums.sum = sync(sums, table_got, two, up_sums.sum)
        attn_sums.add_last((one, (0,)), two)
        attn_sums.last()

        sums, table_got, gene_sum = tie((sums, table_got, gene_sum), attn_sums.last_in)
        sums = grid.scatter_step(sums, "x", 2, F32)
        table_sum = grid.scatter_step(added(table_mine, table_got)[0], "y", 0, BF16)
        gene_sum = grid.scatter_step(
            gene_sum.reshape(2, grid.size["y"], -1, gene_sum.shape[-1]), "y", 1, BF16
        )
        up_result, down_result = up_sums.result(attn_sums.last_in), down_sums.result(attn_sums.last_in)
        sums, table_sum, gene_sum, up_result, down_result = sync(
            sums, table_sum, gene_sum, up_result, down_result
        )
        sums = grid.scatter_step(sums, "y", 1, F32)
        gene_sum = grid.trade(gene_sum.reshape(2, 2, -1, gene_sum.shape[-1]), "c", 1, 2)
        grad_table = grid.trade(table_sum, "x", 0, 1).astype(F32)
        sums, grad_table, gene_sum = sync(sums, grad_table, gene_sum)
        summed = grid.scatter_step(sums, "z", 0, F32).reshape(-1)
        grad_gene = grid.trade(gene_sum, "zh", 0, 1).astype(F32)
        all_heads, all_cells = jnp.split(tie(gathered, attn_sums.last_in), [D], axis=1)
        owned = D // (dp_count * query_count)
        mine = lax.axis_index("dp") * query_count + place
        grad_cell = dot_lt(
            lax.dynamic_slice_in_dim(all_heads, mine * owned, owned, 1), all_cells
        )
        outs = []
        start = 0
        for value, piece in zip(small, flat):
            size = piece.shape[1]
            outs.append(summed[start : start + size].reshape(value.shape[0], -1))
            start += size

        attn_sum = attn_sums.result()
        qkv_cut = 3 * D // 2

        return (
            encoded_rows,
            grad_tokens,
            outs[0],
            outs[1],
            outs[2],
            outs[3],
            jnp.concatenate([half[:, :qkv_cut] for half in attn_sum], axis=1),
            jnp.concatenate([half[:, qkv_cut:] for half in attn_sum], axis=1),
            jnp.concatenate(up_result, axis=1),
            jnp.concatenate(down_result, axis=1),
            grad_cell,
            grad_gene,
            outs[4][0],
            grad_table,
        )

    return shards


def split_heads(qkv_row):
    queries = qkv_row[:, :D].reshape(ROW_LEN, HEADS, HEAD_DIM)
    keys_in = qkv_row[:, D : 2 * D].reshape(ROW_LEN, HEADS, HEAD_DIM)
    values_in = qkv_row[:, 2 * D :].reshape(ROW_LEN, HEADS, HEAD_DIM)
    return (queries, keys_in, values_in)


def row_scores(queries, keys_in, segment_row):
    scores = jnp.einsum("qhd,khd->hqk", queries, keys_in, preferred_element_type=jnp.float32) * (
        1.0 / math.sqrt(HEAD_DIM)
    )
    same_cell = segment_row[:, None] == segment_row[None, :]
    return jnp.where(same_cell[None], scores, -1e30)


def attend_any(member):
    qkv_row, segment_row = member
    queries, keys_in, values_in = split_heads(qkv_row)
    scores = row_scores(queries, keys_in, segment_row)
    highest_score = jnp.max(scores, axis=-1, keepdims=True)
    weights = jnp.exp(scores - highest_score)
    weight_sum = jnp.sum(weights, axis=-1, keepdims=True)
    attention = (weights / weight_sum).astype(jnp.bfloat16)
    mixed = jnp.einsum(
        "hqk,khd->qhd", attention, values_in, preferred_element_type=jnp.float32
    ).astype(jnp.bfloat16)
    return (mixed.reshape(ROW_LEN, D), (highest_score + jnp.log(weight_sum))[:, :, 0])


def attend_back_any(member):
    qkv_row, segment_row, log_total, grad_mixed = member
    queries, keys_in, values_in = split_heads(qkv_row)
    scores = row_scores(queries, keys_in, segment_row)
    attention = jnp.exp(scores - log_total[:, :, None])
    grad_heads = grad_mixed.reshape(ROW_LEN, HEADS, HEAD_DIM)
    grad_probs = jnp.einsum(
        "qhd,khd->hqk", grad_heads, values_in, preferred_element_type=jnp.float32
    )
    grad_scores = (
        attention * (grad_probs - jnp.sum(attention * grad_probs, axis=-1, keepdims=True))
    ).astype(jnp.bfloat16)
    scale_factor = 1.0 / math.sqrt(HEAD_DIM)
    grad_query = (
        jnp.einsum("hqk,khd->qhd", grad_scores, keys_in, preferred_element_type=jnp.float32)
        * scale_factor
    )
    grad_keys = (
        jnp.einsum("hqk,qhd->khd", grad_scores, queries, preferred_element_type=jnp.float32)
        * scale_factor
    )
    grad_values = jnp.einsum(
        "hqk,qhd->khd",
        attention.astype(jnp.bfloat16),
        grad_heads,
        preferred_element_type=jnp.float32,
    )
    return jnp.concatenate(
        [
            grad_query.reshape(ROW_LEN, D),
            grad_keys.reshape(ROW_LEN, D),
            grad_values.reshape(ROW_LEN, D),
        ],
        axis=1,
    )


def owned_cols(values_in, dp_count, query_count, place):
    width = values_in.shape[1] // (dp_count * query_count)
    shaped = values_in.reshape(values_in.shape[0], dp_count, query_count, width)
    return lax.dynamic_index_in_dim(shaped, place, axis=2, keepdims=False)


def owned_term(left, right, dp_count, query_count, place):
    return jnp.einsum(
        "ndr,ne->dre",
        owned_cols(left, dp_count, query_count, place),
        right,
        preferred_element_type=jnp.float32,
    )


def owner_blocks(values_in, dp_count, query_count):
    width = values_in.shape[0] // (dp_count * query_count)
    return values_in.reshape(dp_count, query_count, width, values_in.shape[1])


def shards_any(
    tokens,
    cell_lengths,
    out_cotangent,
    ln_gains,
    ln_biases,
    proj_biases,
    ff_biases,
    w_qkv,
    w_out,
    w_up,
    w_down,
    dec_cell,
    dec_gene,
    dec_out,
    gene_table,
    query_ids,
    labels,
):
    row_count = tokens.shape[0]
    token_count = row_count * ROW_LEN
    dp_count = lax.axis_size("dp")
    query_count = lax.axis_size("query")
    place = lax.axis_index("query")
    starts, segment = cell_layout(cell_lengths)
    gathered = (
        lax.all_gather(w_qkv, "query", axis=0, tiled=True),
        lax.all_gather(w_out, "query", axis=0, tiled=True),
        lax.all_gather(w_up, "query", axis=0, tiled=True),
        lax.all_gather(w_down, "query", axis=0, tiled=True),
        lax.all_gather(dec_cell, "query", axis=0, tiled=True),
        lax.all_gather(dec_gene, "query", axis=0, tiled=True),
        lax.all_gather(gene_table, "query", axis=0, tiled=True),
    )
    full_qkv, full_out, full_up, full_down, full_cell, full_gene, full_table = gathered
    flat_tokens = tokens.astype(jnp.float32).reshape(token_count, D)
    normed, first_pull = jax.vjp(layer_norm, flat_tokens, ln_gains[0], ln_biases[0])
    normed_low = normed.astype(jnp.bfloat16)
    zeroes = jnp.zeros((D,), jnp.float32)
    qkv_bias = jnp.concatenate([proj_biases[0], zeroes, proj_biases[1]])
    qkv_low = (jnp.dot(normed_low, full_qkv, preferred_element_type=jnp.float32) + qkv_bias).astype(
        jnp.bfloat16
    )
    qkv_rows = qkv_low.reshape(row_count, ROW_LEN, 3 * D)
    mixed_rows, log_totals = lax.map(attend_any, (qkv_rows, segment))
    mixed_low = mixed_rows.reshape(token_count, D)
    middle = (
        flat_tokens
        + jnp.dot(mixed_low, full_out, preferred_element_type=jnp.float32)
        + proj_biases[2]
    )
    second, second_pull = jax.vjp(layer_norm, middle, ln_gains[1], ln_biases[1])
    second_low = second.astype(jnp.bfloat16)
    hidden = jnp.dot(second_low, full_up, preferred_element_type=jnp.float32) + ff_biases[0]
    active, active_pull = jax.vjp(smooth_gate, hidden)
    active_low = active.astype(jnp.bfloat16)
    encoded = (
        middle + jnp.dot(active_low, full_down, preferred_element_type=jnp.float32) + proj_biases[3]
    )
    places = jnp.arange(ROW_LEN, dtype=jnp.int32)
    picker = (places[None, None, :] == starts[:, :, None]).astype(jnp.float32)
    local_cells = row_count * CELLS_ROW
    heads_low = (
        jnp.einsum(
            "rcl,rld->rcd", picker, encoded.reshape(row_count, ROW_LEN, D), precision=HIGHEST
        )
        .reshape(local_cells, D)
        .astype(jnp.bfloat16)
    )
    cell_heads = lax.all_gather(heads_low, "query", axis=0, tiled=True)
    cell_part = jnp.dot(cell_heads, full_cell, preferred_element_type=jnp.float32)
    gene_rows = jnp.take(full_table, query_ids, axis=0)
    before = (
        cell_part[:, None, :]
        + jnp.einsum("cqd,df->cqf", gene_rows, full_gene, preferred_element_type=jnp.float32)
        + ff_biases[1]
    )
    gated_dec, gated_pull = jax.vjp(smooth_gate, before)
    logit_weight = dec_out.astype(jnp.float32)
    logits = jnp.einsum("cqf,f->cq", gated_dec, logit_weight, precision=HIGHEST)
    logit_slope = jax.nn.sigmoid(logits) - labels.astype(jnp.float32)
    (grad_before,) = gated_pull(logit_slope[:, :, None] * logit_weight)
    before_low = grad_before.astype(jnp.bfloat16)
    grad_dec_bias = jnp.sum(before_low, axis=(0, 1), dtype=jnp.float32)
    grad_logit = jnp.einsum("cqf,cq->f", gated_dec, logit_slope, precision=HIGHEST)
    gene_terms = jnp.einsum(
        "cqd,cqf->df", gene_rows, before_low, preferred_element_type=jnp.float32
    )
    genes_back = jnp.einsum(
        "cqf,df->cqd", before_low, full_gene, preferred_element_type=jnp.float32
    ).astype(jnp.bfloat16)
    choose = (query_ids.reshape(-1)[:, None] == jnp.arange(GENES, dtype=jnp.int32)[None, :]).astype(
        jnp.bfloat16
    )
    table_terms = jnp.einsum(
        "ng,nd->gd", choose, genes_back.reshape(-1, D), preferred_element_type=jnp.float32
    )
    gene_parts, table_parts = (
        lax.all_to_all(
            owner_blocks(gene_terms, dp_count, query_count).astype(jnp.bfloat16),
            "query",
            split_axis=1,
            concat_axis=1,
            tiled=True,
        ).astype(jnp.float32),
        lax.all_to_all(
            owner_blocks(table_terms, dp_count, query_count).astype(jnp.bfloat16),
            "query",
            split_axis=1,
            concat_axis=1,
            tiled=True,
        ).astype(jnp.float32),
    )
    grad_gene = jnp.sum(gene_parts, axis=1)
    grad_table = jnp.sum(table_parts, axis=1)
    cell_total = lax.psum(
        jnp.sum(before_low, axis=1, dtype=jnp.float32).astype(jnp.bfloat16), "query"
    )
    grad_cell = owned_term(cell_heads, cell_total, dp_count, query_count, place)
    heads_all = jnp.einsum("cf,df->cd", cell_total, full_cell, preferred_element_type=jnp.float32)
    heads_back = (
        lax.dynamic_slice_in_dim(heads_all, place * local_cells, local_cells, 0)
        .astype(jnp.bfloat16)
        .astype(jnp.float32)
    )
    grad_encoded = out_cotangent.astype(jnp.float32) + jnp.einsum(
        "rcl,rcd->rld", picker, heads_back.reshape(row_count, CELLS_ROW, D), precision=HIGHEST
    )
    grad_flat = grad_encoded.reshape(token_count, D)

    def empty_term(left_width, right_width):
        return jnp.zeros(
            (dp_count, left_width // (dp_count * query_count), right_width), jnp.float32
        )

    branch_low = grad_flat.astype(jnp.bfloat16)
    grad_out_bias = jnp.sum(branch_low, axis=0, dtype=jnp.float32)
    grad_active = jnp.einsum("nd,fd->nf", branch_low, full_down, preferred_element_type=jnp.float32)
    (grad_hidden,) = active_pull(grad_active)
    hidden_low = grad_hidden.astype(jnp.bfloat16)
    grad_up_bias = jnp.sum(hidden_low, axis=0, dtype=jnp.float32)
    grad_second = jnp.einsum("nf,df->nd", hidden_low, full_up, preferred_element_type=jnp.float32)
    middle_part, grad_gain_two, grad_shift_two = second_pull(grad_second)
    grad_middle = grad_flat + middle_part
    ff_terms = jnp.stack([grad_up_bias, grad_dec_bias], axis=1)
    attn_low = grad_middle.astype(jnp.bfloat16)
    grad_attn_bias = jnp.sum(attn_low, axis=0, dtype=jnp.float32)
    mixed_back = jnp.einsum(
        "ne,de->nd", attn_low, full_out, preferred_element_type=jnp.float32
    ).astype(jnp.bfloat16)
    qkv_back = lax.map(
        attend_back_any, (qkv_rows, segment, log_totals, mixed_back.reshape(row_count, ROW_LEN, D))
    )
    qkv_back_low = qkv_back.reshape(token_count, 3 * D).astype(jnp.bfloat16)
    bias_sums = jnp.sum(qkv_back_low, axis=0, dtype=jnp.float32)
    grad_normed = jnp.einsum(
        "ne,de->nd", qkv_back_low, full_qkv, preferred_element_type=jnp.float32
    )
    token_part, grad_gain_one, grad_shift_one = first_pull(grad_normed)
    grad_tokens = (grad_middle + token_part).reshape(row_count, ROW_LEN, D)
    gain_terms = jnp.stack([grad_gain_one, grad_gain_two], axis=1)
    shift_terms = jnp.stack([grad_shift_one, grad_shift_two], axis=1)
    proj_terms = jnp.stack(
        [bias_sums[:D], bias_sums[2 * D :], grad_attn_bias, grad_out_bias], axis=1
    )
    totals = (empty_term(D, 3 * D), empty_term(D, D), empty_term(D, FF), empty_term(FF, D))
    pieces = (
        lax.all_gather(normed_low, "query", axis=0, tiled=True),
        lax.all_gather(qkv_back_low, "query", axis=0, tiled=True),
        lax.all_gather(mixed_low, "query", axis=0, tiled=True),
        lax.all_gather(attn_low, "query", axis=0, tiled=True),
        lax.all_gather(second_low, "query", axis=0, tiled=True),
        lax.all_gather(hidden_low, "query", axis=0, tiled=True),
        lax.all_gather(active_low, "query", axis=0, tiled=True),
        lax.all_gather(branch_low, "query", axis=0, tiled=True),
    )
    every_fold = tuple(
        (
            owned_term(pieces[2 * i], pieces[2 * i + 1], dp_count, query_count, place)
            for i in range(len(totals))
        )
    )
    every_sum = (
        lax.psum_scatter(
            every_fold[2].astype(jnp.bfloat16), "dp", scatter_dimension=0, tiled=True
        ).astype(jnp.float32),
        lax.psum_scatter(
            every_fold[3].astype(jnp.bfloat16), "dp", scatter_dimension=0, tiled=True
        ).astype(jnp.float32),
        lax.psum_scatter(
            grad_cell.astype(jnp.bfloat16), "dp", scatter_dimension=0, tiled=True
        ).astype(jnp.float32),
        lax.psum_scatter(
            grad_gene.astype(jnp.bfloat16), "dp", scatter_dimension=0, tiled=True
        ).astype(jnp.float32),
        lax.psum_scatter(
            grad_table.astype(jnp.bfloat16), "dp", scatter_dimension=0, tiled=True
        ).astype(jnp.float32),
        lax.psum_scatter(
            every_fold[0].astype(jnp.bfloat16), "dp", scatter_dimension=0, tiled=True
        ).astype(jnp.float32),
        lax.psum_scatter(
            every_fold[1].astype(jnp.bfloat16), "dp", scatter_dimension=0, tiled=True
        ).astype(jnp.float32),
    )
    ffn_sums = every_sum[:5]
    attn_sums = every_sum[5:]
    small_sums = (
        lax.psum_scatter(gain_terms, ("dp", "query"), scatter_dimension=0, tiled=True),
        lax.psum_scatter(shift_terms, ("dp", "query"), scatter_dimension=0, tiled=True),
        lax.psum_scatter(proj_terms, ("dp", "query"), scatter_dimension=0, tiled=True),
        lax.psum_scatter(ff_terms, ("dp", "query"), scatter_dimension=0, tiled=True),
        lax.psum_scatter(grad_logit, ("dp", "query"), scatter_dimension=0, tiled=True),
    )

    def flat_rows(values_in):
        return values_in.reshape(-1, values_in.shape[-1])

    return (
        encoded.reshape(row_count, ROW_LEN, D),
        grad_tokens,
        small_sums[0].T,
        small_sums[1].T,
        small_sums[2].T,
        small_sums[3].T,
        flat_rows(attn_sums[0]),
        flat_rows(attn_sums[1]),
        flat_rows(ffn_sums[0]),
        flat_rows(ffn_sums[1]),
        flat_rows(ffn_sums[2]),
        flat_rows(ffn_sums[3]),
        small_sums[4],
        flat_rows(ffn_sums[4]),
    )


def solution(mesh):
    placed = (
        P(("dp", "query"), None, None),
        P(("dp", "query"), None),
        P(("dp", "query"), None, None),
        P(),
        P(),
        P(),
        P(),
        P("query", None),
        P("query", None),
        P("query", None),
        P("query", None),
        P("query", None),
        P("query", None),
        P(),
        P("query", None),
        P("dp", "query"),
        P("dp", "query"),
    )
    rows = P(("dp", "query"), None)
    grid = Grid(mesh)
    return jax.shard_map(
        make_shards(grid) if grid.paired() else shards_any,
        mesh=mesh,
        in_specs=placed,
        out_specs=(
            P(("dp", "query"), None, None),
            P(("dp", "query"), None, None),
            P(None, ("dp", "query")),
            P(None, ("dp", "query")),
            P(None, ("dp", "query")),
            P(None, ("dp", "query")),
            rows,
            rows,
            rows,
            rows,
            rows,
            rows,
            P(("dp", "query")),
            rows,
        ),
        check_vma=False,
    )
```
